128 devices in a mesh: row: 32 (over x, z_lo, y), col: 4 (over z_hi, core).
Axes of the slice: x: 4, y: 4, z: 4 (z_hi: 2, z_lo: 2; z = z_hi * 2 + z_lo), core: 2. Of those that a mesh axis runs over, the one named last changes fastest.
Arguments:
- query_near: bfloat16 [128, 512, 256], P('row', 'col'), may hold values from -9 to 9
- key_near: bfloat16 [128, 512, 256], P('row', 'col'), may hold values from -9 to 9
- value_near: bfloat16 [128, 512, 256], P('row', 'col'), may hold values from -6 to 6
- dilated_queries: bfloat16 [128, 512, 256], P('row', 'col'), may hold values from -9 to 9
- dilated_keys: bfloat16 [128, 512, 256], P('row', 'col'), may hold values from -9 to 9
- dilated_values: bfloat16 [128, 512, 256], P('row', 'col'), may hold values from -6 to 6
Outputs:
- attended_near: bfloat16 [128, 512, 256], P('row', 'col')
- dilated_attention_output: bfloat16 [128, 512, 256], P('row', 'col')
The draws below stay inside these ranges and needn't reach their ends.
All inputs are finite; a program needn't handle non-finite values.
Results may differ from the reference program's by a relative error of at most 0.0049.
Values may be sent and summed in bfloat16 or wider, within the bound.
A program may use at most 192 MiB of HBM per device.

```python
import math
import jax
import jax.numpy as jnp
from jax import lax

HEADS = 4
DILATION_STEP = 16
CH = 256
HEIGHT = 128
WIDTH = 512


def draw_query_near(key, part):
    own_key = jax.random.fold_in(key, 1)
    base = jnp.clip(jax.random.normal(own_key, (HEIGHT, WIDTH, CH), jnp.float32), -6.0, 6.0)
    return base.astype(jnp.bfloat16)


def draw_key_near(key, part):
    own_key = jax.random.fold_in(key, 2)
    base = jnp.clip(jax.random.normal(own_key, (HEIGHT, WIDTH, CH), jnp.float32), -6.0, 6.0)
    return base.astype(jnp.bfloat16)


def draw_dilated_queries(key, part):
    own_key = jax.random.fold_in(key, 3)
    base = jnp.clip(jax.random.normal(own_key, (HEIGHT, WIDTH, CH), jnp.float32), -6.0, 6.0)
    return base.astype(jnp.bfloat16)


def draw_dilated_keys(key, part):
    own_key = jax.random.fold_in(key, 4)
    base = jnp.clip(jax.random.normal(own_key, (HEIGHT, WIDTH, CH), jnp.float32), -6.0, 6.0)
    return base.astype(jnp.bfloat16)


def levels(key, dims, cuts, least, largest):
    def one(position, shards_of):
        draws = jax.random.uniform(jax.random.fold_in(jax.random.fold_in(key, 6), position), (shards_of,), jnp.float32, least / len(cuts), largest / len(cuts))
        return jnp.repeat(jnp.exp(draws), dims[position] // shards_of).reshape((-1,) + (1,) * (len(dims) - position - 1))

    level = one(*cuts[0])
    for cut in cuts[1:]:
        level = level * one(*cut)
    return level


def gaussian(rng, dims, scale, reach, shards=(), kind=jnp.bfloat16):
    drawn = jax.random.normal(rng, dims, jnp.float32) * scale
    if len(shards) > 0:
        drawn = levels(rng, dims, shards, -0.22, 0.18) * drawn
    return jnp.clip(drawn, min=-reach, max=reach).astype(kind)


def setup_inputs(seed: int = 0) -> dict:
    streams_of = jax.random.split(jax.random.key(seed), 7)
    query_near = draw_query_near(jax.random.fold_in(streams_of[6], 71), 0)
    key_near = draw_key_near(jax.random.fold_in(streams_of[6], 71), 0)
    value_near = gaussian(streams_of[2], (HEIGHT, WIDTH, CH), 1.0, 6.0, ((0, 32), (1, 4)))
    dilated_queries = draw_dilated_queries(jax.random.fold_in(streams_of[6], 71), 0)
    dilated_keys = draw_dilated_keys(jax.random.fold_in(streams_of[6], 71), 0)
    dilated_values = gaussian(streams_of[5], (HEIGHT, WIDTH, CH), 1.0, 6.0, ((0, 32), (1, 4)))
    return {"query_near": query_near, "key_near": key_near, "value_near": value_near, "dilated_queries": dilated_queries, "dilated_keys": dilated_keys, "dilated_values": dilated_values}


def neighbour_window_attention(query, key_rows, value_rows, spacing):
    image_height, complete_width, channels = query.shape
    head_size = channels // HEADS
    margin = 3 * spacing
    key_pad = jnp.pad(key_rows, ((margin, margin), (margin, margin), (0, 0)))
    value_pad = jnp.pad(value_rows, ((margin, margin), (margin, margin), (0, 0)))
    row_ids = jnp.arange(image_height, dtype=jnp.int32)
    col_ids = jnp.arange(complete_width, dtype=jnp.int32)
    query_heads = query.astype(jnp.float32).reshape(image_height, complete_width, HEADS, head_size)
    scaling = 1.0 / math.sqrt(head_size)
    zero_index = jnp.zeros((), jnp.int32)

    def starts(tap):
        tap_row = tap // 7 - 3
        tap_col = tap % 7 - 3
        first = (margin + tap_row * spacing).astype(jnp.int32)
        second = (margin + tap_col * spacing).astype(jnp.int32)
        return (tap_row, tap_col, first, second)

    def tap_scores(tap):
        tap_row, tap_col, first, second = starts(tap)
        shifted = lax.dynamic_slice(key_pad, (first, second, zero_index), (image_height, complete_width, channels))
        shifted = shifted.astype(jnp.float32).reshape(image_height, complete_width, HEADS, head_size)
        scores = jnp.einsum('xyhd,xyhd->xyh', query_heads, shifted) * scaling
        moved_row = row_ids + tap_row * spacing
        moved_col = col_ids + tap_col * spacing
        inside_row = (moved_row >= 0) & (moved_row < image_height)
        inside_col = (moved_col >= 0) & (moved_col < complete_width)
        inside = inside_row[:, None, None] & inside_col[None, :, None]
        return jnp.where(inside, scores, -jnp.inf)
    taps = jnp.arange(49, dtype=jnp.int32)
    scores = lax.map(tap_scores, taps)
    peak = lax.optimization_barrier(jnp.max(scores, axis=0))
    weights = jnp.exp(scores - peak[None])
    total = lax.optimization_barrier(jnp.sum(weights, axis=0))
    probs = (weights / total[None]).astype(jnp.bfloat16)

    def add_tap(tap, accum):
        tap_row, tap_col, first, second = starts(tap)
        shifted = lax.dynamic_slice(value_pad, (first, second, zero_index), (image_height, complete_width, channels))
        shifted = shifted.astype(jnp.float32).reshape(image_height, complete_width, HEADS, head_size)
        return accum + probs[tap].astype(jnp.float32)[..., None] * shifted
    accum = jnp.zeros((image_height, complete_width, HEADS, head_size), jnp.float32)
    accum = lax.fori_loop(0, 49, add_tap, accum)
    return accum.reshape(image_height, complete_width, channels).astype(jnp.bfloat16)

def reference(query_near, key_near, value_near, dilated_queries, dilated_keys, dilated_values):
    attended_near = neighbour_window_attention(query_near, key_near, value_near, 1)
    dilated_attention_output = neighbour_window_attention(dilated_queries, dilated_keys, dilated_values, DILATION_STEP)
    return (attended_near, dilated_attention_output)
```

```python
import functools
import math

import jax
import jax.numpy as jnp
from jax import lax
from jax.experimental import pallas as pl
from jax.experimental.pallas import tpu as pltpu
from jax.sharding import PartitionSpec as P

MESH = pl.DeviceIdType.MESH
HEADS = 4
HEAD = 64
CH = 256
ROWS = 4
COLS = 128
STRIP = 48
WIDE = COLS + 2 * STRIP
STEP = 16
SLOTS = 7
OWN = 3
EDGE = 16
NEAR_WIDE = COLS + 2 * EDGE
NEAR_ROWS = ROWS + 6
TILE = 32
TILES = COLS // TILE
KEYS = TILE + 2 * STRIP
NEAR_KEYS = TILE + 2 * EDGE
SCALE = math.log2(math.e) / math.sqrt(HEAD)
NONE = 99

SECOND = (
    (1, -1, -1, NONE, 1, -2, NONE, NONE),
    (NONE, NONE, 2, -1, NONE, 1, 1, -1),
    (4, 2, 2, 2, -2, -2, -2, -4),
)
FROM_STREAM = ((2, 2, 0, 0, 2, 0, 0, 0), (0, 0, 1, 2, 0, 1, 2, 2), (1, 1, 1, 1, 0, 0, 0, 0))
FROM_SECOND = ((0, 0, 1, 0, 0, 0, 0, 0), (0, 0, 0, 0, 0, 1, 0, 0), (1, 0, 0, 0, 0, 0, 0, 1))
VALUES_LAST = ((0, 5), (2, 7), ())


def pick(table, place):
    out = jnp.int32(table[0])
    for k in range(1, len(table)):
        out = jnp.where(place == k, jnp.int32(table[k]), out)
    return out


def one_of(place, places):
    out = jnp.bool_(False)
    for k in places:
        out = out | (place == k)
    return out


def kernel(
    qn_ref, kn_ref, vn_ref, qf_ref, kf_ref, vf_ref, on_ref, of_ref,
    far, near, qn, qf, qb, scores, peak, probs, total, acc, bias_far, bias_near, out_near, out_far,
    load_sem, far_send, far_recv, strip_send, strip_recv, side_send, side_recv, near_send, near_recv, out_sem,
):
    row = lax.axis_index("row")
    col = lax.axis_index("col")
    n_rows = lax.axis_size("row")
    n_cols = lax.axis_size("col")
    x = row // 8
    z = (row // 4) % 2
    core = col % 2
    place = 2 * x + z
    inner = (col == 1) | (col == 2)
    true = jnp.bool_(True)

    loads = [
        pltpu.make_async_copy(kf_ref, far.at[0, OWN, :, pl.ds(STRIP, COLS)], load_sem.at[0]),
        pltpu.make_async_copy(vf_ref, far.at[1, OWN, :, pl.ds(STRIP, COLS)], load_sem.at[1]),
        pltpu.make_async_copy(kn_ref, near.at[0, pl.ds(3, ROWS), pl.ds(EDGE, COLS)], load_sem.at[2]),
        pltpu.make_async_copy(vn_ref, near.at[1, pl.ds(3, ROWS), pl.ds(EDGE, COLS)], load_sem.at[3]),
        pltpu.make_async_copy(qf_ref, qf, load_sem.at[4]),
        pltpu.make_async_copy(qn_ref, qn, load_sem.at[5]),
    ]
    for load in loads:
        load.start()

    to_row = (row + 8, row - 8, row + 4 - 8 * z)
    first_send = (x < 3, x > 0, true)
    first_recv = (x > 0, x < 3, true)
    first_to = (jnp.int32(1), jnp.int32(5), 2 + 2 * z)
    first_in = (jnp.int32(1), jnp.int32(5), 4 - 2 * z)
    shift = (-2, 2, 2 * z - 1)
    second_rel = [pick(SECOND[s], place) for s in range(3)]
    second_send = [second_rel[s] != NONE for s in range(3)]
    second_src = [(second_rel[s] + 10) % 7 for s in range(3)]
    second_to = [(second_rel[s] + 10 + shift[s]) % 7 for s in range(3)]
    sender_place = (place - 2, place + 2, place + 1 - 2 * z)
    sender_rel = [pick(SECOND[s], sender_place[s]) for s in range(3)]
    second_recv = [first_recv[s] & (sender_rel[s] != NONE) for s in range(3)]
    second_in = [
        (sender_rel[s] + 10 + (-2, 2, 1 - 2 * z)[s]) % 7 for s in range(3)
    ]
    send_ok = (first_send, second_send)
    recv_ok = (first_recv, second_recv)
    src_slot = ((jnp.int32(OWN),) * 3, second_src)
    dst_slot = (first_to, second_to)
    in_slot = (first_in, second_in)
    values_last = [one_of(place, VALUES_LAST[s]) for s in range(3)]
    late_in = [first_recv[s] & one_of(sender_place[s], VALUES_LAST[s]) for s in range(3)]
    outer_col = jnp.where(col == 1, STRIP + COLS, 0)

    def part_cols(part):
        if part == 0:
            return pl.ds(STRIP, COLS)
        return pl.ds(pl.multiple_of(outer_col, 16), STRIP)

    def far_copy(s, o, kv, part):
        where = part_cols(part)
        return pltpu.make_async_remote_copy(
            far.at[kv, src_slot[o][s], :, where],
            far.at[kv, dst_slot[o][s], :, where],
            far_send.at[s, o, kv, part],
            far_recv.at[s, o, kv, part],
            device_id=(to_row[s], col),
            device_id_type=MESH,
        )

    def far_arrival(s, o, kv, part):
        where = part_cols(part)
        block = far.at[kv, in_slot[o][s], :, where]
        return pltpu.make_async_remote_copy(
            block, block, far_send.at[s, o, kv, part], far_recv.at[s, o, kv, part],
            device_id=(to_row[s], col), device_id_type=MESH,
        )

    def send_far(s, o, kv, ok=true, parts=(0, 1)):
        for part in parts:
            good = send_ok[o][s] & ok
            if part == 1:
                good = good & inner

            @pl.when(good)
            def _():
                far_copy(s, o, kv, part).start()

    def wait_far(s, o, kv, ok=true):
        for part in (0, 1):
            good = recv_ok[o][s] & ok
            if part == 1:
                good = good & inner

            @pl.when(good)
            def _():
                far_arrival(s, o, kv, part).wait_recv()

    mate = col + 1 - 2 * core
    strip_src = pl.multiple_of(jnp.where(core == 0, COLS, STRIP), 16)
    strip_dst = pl.multiple_of(jnp.where(core == 0, 0, STRIP + COLS), 16)
    strip_in = pl.multiple_of(jnp.where(core == 0, STRIP + COLS, 0), 16)

    def strip_copy(e, kv, slot):
        return pltpu.make_async_remote_copy(
            far.at[kv, slot, :, pl.ds(strip_src, STRIP)],
            far.at[kv, slot, :, pl.ds(strip_dst, STRIP)],
            strip_send.at[e, kv],
            strip_recv.at[e, kv],
            device_id=(row, mate),
            device_id_type=MESH,
        )

    def strip_arrival(e, kv, slot):
        block = far.at[kv, slot, :, pl.ds(strip_in, STRIP)]
        return pltpu.make_async_remote_copy(
            block, block, strip_send.at[e, kv], strip_recv.at[e, kv],
            device_id=(row, mate), device_id_type=MESH,
        )

    def send_strip(s, o, kv, ok=true):
        @pl.when(recv_ok[o][s] & ok)
        def _():
            strip_copy(1 + 3 * o + s, kv, in_slot[o][s]).start()

    def wait_strip(s, o, kv):
        @pl.when(recv_ok[o][s])
        def _():
            strip_arrival(1 + 3 * o + s, kv, in_slot[o][s]).wait_recv()

    side_src = pl.multiple_of(jnp.where(col == 1, COLS, STRIP), 16)
    side_dst = pl.multiple_of(jnp.where(col == 1, 0, STRIP + COLS), 16)

    def side_copy(kv):
        return pltpu.make_async_remote_copy(
            far.at[kv, OWN, :, pl.ds(side_src, STRIP)],
            far.at[kv, OWN, :, pl.ds(side_dst, STRIP)],
            side_send.at[kv],
            side_recv.at[kv],
            device_id=(row, 3 - col),
            device_id_type=MESH,
        )

    def side_arrival(kv):
        block = far.at[kv, OWN, :, part_cols(1)]
        return pltpu.make_async_remote_copy(
            block, block, side_send.at[kv], side_recv.at[kv], device_id=(row, 3 - col), device_id_type=MESH
        )

    sides = [(dr, dc) for dr in (-1, 0, 1) for dc in (-1, 0, 1) if (dr, dc) != (0, 0)]

    def there(dr, dc):
        good = true
        if dr:
            good = good & ((row + dr >= 0) & (row + dr < n_rows))
        if dc:
            good = good & ((col + dc >= 0) & (col + dc < n_cols))
        return good

    row_src = {1: (4, 3), -1: (3, 3), 0: (3, ROWS)}
    row_dst = {1: (0, 3), -1: (7, 3), 0: (3, ROWS)}
    col_src = {1: (COLS, EDGE), -1: (EDGE, EDGE), 0: (EDGE, COLS)}
    col_dst = {1: (0, EDGE), -1: (EDGE + COLS, EDGE), 0: (EDGE, COLS)}

    def near_copy(n, kv):
        dr, dc = sides[n]
        return pltpu.make_async_remote_copy(
            near.at[kv, pl.ds(*row_src[dr]), pl.ds(*col_src[dc])],
            near.at[kv, pl.ds(*row_dst[dr]), pl.ds(*col_dst[dc])],
            near_send.at[n, kv],
            near_recv.at[n, kv],
            device_id=(row + dr, col + dc),
            device_id_type=MESH,
        )

    def near_arrival(n, kv):
        dr, dc = sides[n]
        block = near.at[kv, pl.ds(*row_dst[dr]), pl.ds(*col_dst[dc])]
        return pltpu.make_async_remote_copy(
            block, block, near_send.at[n, kv], near_recv.at[n, kv],
            device_id=(row - dr, col - dc), device_id_type=MESH,
        )

    barrier = pltpu.get_barrier_semaphore()
    expected = jnp.int32(0)
    for s in range(3):
        @pl.when(first_send[s])
        def _():
            pl.semaphore_signal(barrier, inc=1, device_id=(to_row[s], col), device_id_type=MESH)

        expected = expected + first_recv[s].astype(jnp.int32)
    for dr, dc in sides:
        @pl.when(there(dr, dc))
        def _():
            pl.semaphore_signal(barrier, inc=1, device_id=(row + dr, col + dc), device_id_type=MESH)

        expected = expected + there(-dr, -dc).astype(jnp.int32)
    pl.semaphore_wait(barrier, expected)

    loads[0].wait()
    for s in range(3):
        send_far(s, 0, 0, parts=(0,))
    strip_copy(0, 0, OWN).start()

    @pl.when(inner)
    def _():
        side_copy(0).start()

    loads[1].wait()

    @pl.when(inner)
    def _():
        side_copy(1).start()

    for s in range(3):
        send_far(s, 0, 1, ok=~values_last[s], parts=(0,))
    strip_copy(0, 1, OWN).start()
    loads[2].wait()
    loads[3].wait()
    for n, (dr, dc) in enumerate(sides):
        @pl.when(there(dr, dc))
        def _():
            near_copy(n, 0).start()
            near_copy(n, 1).start()

    c0 = col * COLS
    width = n_cols * COLS
    for t in range(TILES):
        q_at = lax.broadcasted_iota(jnp.int32, (TILE, KEYS), 0)
        k_at = lax.broadcasted_iota(jnp.int32, (TILE, KEYS), 1)
        apart = k_at - q_at
        k_col = c0 + TILE * t - STRIP + k_at
        good = ((apart & (STEP - 1)) == 0) & (apart >= 0) & (apart <= 2 * STRIP) & (k_col >= 0) & (k_col < width)
        bias_far[t] = jnp.where(good, 0.0, -jnp.inf)
    for rp in range(2):
        for t in range(TILES):
            shape = (2, TILE, 8, NEAR_KEYS)
            shape = (2 * TILE, 8 * NEAR_KEYS)
            q_id = lax.broadcasted_iota(jnp.int32, shape, 0)
            k_id = lax.broadcasted_iota(jnp.int32, shape, 1)
            r_off = (k_id // NEAR_KEYS) - (q_id // TILE)
            c_off = (k_id % NEAR_KEYS) - (q_id % TILE) - EDGE
            k_row = row * ROWS + 2 * rp - 3 + (k_id // NEAR_KEYS)
            k_col = c0 + TILE * t - EDGE + (k_id % NEAR_KEYS)
            good = (r_off >= 0) & (r_off <= 6) & (c_off >= -3) & (c_off <= 3)
            good = good & (k_row >= 0) & (k_row < n_rows * ROWS) & (k_col >= 0) & (k_col < width)
            bias_near[rp * TILES + t] = jnp.where(good, 0.0, -jnp.inf)

    zero = lambda shape: jnp.zeros(shape, jnp.bfloat16)
    for a in range(SLOTS):
        relayed = (a == 0) & (place == 0) | (a == 6) & (place == 7)
        lost = ((place + a - OWN < 0) | (place + a - OWN > 7)) & ~relayed

        @pl.when(lost)
        def _():
            for kv in range(2):
                for r in range(ROWS):
                    far[kv, a, r] = zero((WIDE, CH))

        @pl.when(~lost & (col == 0))
        def _():
            for kv in range(2):
                for r in range(ROWS):
                    far[kv, a, r, 0:STRIP] = zero((STRIP, CH))

        @pl.when(~lost & (col == 3))
        def _():
            for kv in range(2):
                for r in range(ROWS):
                    far[kv, a, r, STRIP + COLS : WIDE] = zero((STRIP, CH))

    for kv in range(2):
        @pl.when(row == 0)
        def _():
            near[kv, 0:3] = zero((3, NEAR_WIDE, CH))

        @pl.when(row == n_rows - 1)
        def _():
            near[kv, 7:10] = zero((3, NEAR_WIDE, CH))

        @pl.when(col == 0)
        def _():
            near[kv, :, 0:EDGE] = zero((NEAR_ROWS, EDGE, CH))

        @pl.when(col == n_cols - 1)
        def _():
            near[kv, :, EDGE + COLS : NEAR_WIDE] = zero((NEAR_ROWS, EDGE, CH))

    lane_head = lax.broadcasted_iota(jnp.int32, (1, CH), 1) // HEAD
    head_mask = [(lane_head == h).astype(jnp.float32) for h in range(HEADS)]
    head_mask_narrow = [m.astype(jnp.bfloat16) for m in head_mask]
    dims_t = (((1,), (1,)), ((), ()))
    dims = (((1,), (0,)), ((), ()))

    loads[4].wait()
    loads[5].wait()

    def block_queries(q):
        return jnp.concatenate([q * head_mask_narrow[h] for h in range(HEADS)], axis=0)

    @pl.loop(0, ROWS)
    def _(r):
        for t in range(TILES):
            qb[r * TILES + t] = block_queries(qf[r, TILE * t : TILE * (t + 1), :])

    def score_block(slot, first=False):
        ok = (place + slot - OWN >= 0) & (place + slot - OWN <= 7)
        row_bias = jnp.where(ok, 0.0, -jnp.inf).astype(jnp.float32)

        @pl.loop(0, ROWS)
        def _(r):
            for t in range(TILES):
                idx = r * TILES + t
                k = far[0, slot, r, TILE * t : TILE * t + KEYS, :]
                s = lax.dot_general(qb[idx], k, dims_t, preferred_element_type=jnp.float32) * SCALE
                b = bias_far[t] + row_bias
                s = s.reshape(HEADS, TILE, KEYS) + b[None]
                s = s.reshape(HEADS * TILE, KEYS)
                scores[slot, idx] = s
                peak[idx] = s if first else jnp.maximum(peak[idx], s)

    def value_blocks(slots, first=False):
        @pl.loop(0, ROWS)
        def _(r):
            for t in range(TILES):
                idx = r * TILES + t
                o = None if first else acc[idx]
                for slot in slots:
                    v = far[1, slot, r, TILE * t : TILE * t + KEYS, :]
                    d = lax.dot_general(probs[slot, idx], v, dims, preferred_element_type=jnp.float32)
                    o = d if o is None else o + d
                acc[idx] = o

    strip_arrival(0, 0, OWN).wait_recv()

    @pl.when(inner)
    def _():
        side_arrival(0).wait_recv()

    for s in range(3):
        send_far(s, 0, 0, parts=(1,))

    @pl.when(inner)
    def _():
        side_arrival(1).wait_recv()

    for s in range(3):
        send_far(s, 0, 1, ok=~values_last[s], parts=(1,))
    score_block(OWN, first=True)

    from_stream = [pick(FROM_STREAM[s], place) for s in range(3)]
    after_first = [pick(FROM_SECOND[s], place) == 0 for s in range(3)]
    needs_second = [jnp.bool_(False)] * 3
    for s in range(3):
        for d in range(3):
            needs_second[d] = needs_second[d] | (second_send[s] & ~after_first[s] & (from_stream[s] == d))

    for s in range(3):
        wait_far(s, 0, 0)
    for s in range(3):
        send_far(s, 1, 0, ok=after_first[s])
    for s in range(3):
        send_strip(s, 0, 0)
    for s in range(3):
        wait_strip(s, 0, 0)
    for s in range(3):
        score_block(first_in[s])

    for s in range(3):
        wait_far(s, 0, 1, ok=~late_in[s])
    for s in range(3):
        send_far(s, 1, 1, ok=after_first[s])
    for s in range(3):
        send_far(s, 0, 1, ok=values_last[s])
    for s in range(3):
        wait_far(s, 1, 0, ok=needs_second[s])
    for s in range(3):
        send_far(s, 1, 0, ok=~after_first[s])
    for s in range(3):
        send_strip(s, 0, 1, ok=~late_in[s])

    for n, (dr, dc) in enumerate(sides):
        @pl.when(there(-dr, -dc))
        def _():
            near_arrival(n, 0).wait_recv()
            near_arrival(n, 1).wait_recv()

    @pl.loop(0, 2)
    def _(rp):
        for t in range(TILES):
            q = qn[pl.ds(2 * rp, 2), TILE * t : TILE * (t + 1), :].reshape(2 * TILE, CH)
            k = near[0, pl.ds(2 * rp, 8), TILE * t : TILE * t + NEAR_KEYS, :].reshape(8 * NEAR_KEYS, CH)
            v = near[1, pl.ds(2 * rp, 8), TILE * t : TILE * t + NEAR_KEYS, :].reshape(8 * NEAR_KEYS, CH)
            b = bias_near[rp * TILES + t]
            out = None
            for h in range(HEADS):
                s = lax.dot_general(q * head_mask_narrow[h], k, dims_t, preferred_element_type=jnp.float32)
                s = s * SCALE + b
                p = jnp.exp2(s - jnp.max(s, axis=1, keepdims=True))
                o = lax.dot_general(p.astype(jnp.bfloat16), v, dims, preferred_element_type=jnp.float32)
                o = o * (head_mask[h] / jnp.sum(p, axis=1, keepdims=True))
                out = o if out is None else out + o
            out_near[pl.ds(2 * rp, 2), TILE * t : TILE * (t + 1), :] = out.astype(jnp.bfloat16).reshape(2, TILE, CH)

    near_out = pltpu.make_async_copy(out_near, on_ref, out_sem.at[0])
    near_out.start()

    for s in range(3):
        wait_far(s, 1, 1, ok=needs_second[s])
    for s in range(3):
        send_far(s, 1, 1, ok=~after_first[s])
    for s in range(3):
        wait_far(s, 1, 0, ok=~needs_second[s])
    for s in range(3):
        send_strip(s, 1, 0)
    for s in range(3):
        wait_strip(s, 1, 0)
    second_slots = (jnp.int32(0), jnp.int32(6), 2 + 2 * z)
    for s in range(3):
        score_block(second_slots[s])

    @pl.loop(0, ROWS)
    def _(r):
        for t in range(TILES):
            idx = r * TILES + t
            m = jnp.max(peak[idx], axis=1, keepdims=True)
            summed = None
            for a in range(SLOTS):
                p = jnp.exp2(scores[a, idx] - m)
                probs[a, idx] = p.astype(jnp.bfloat16)
                summed = p if summed is None else summed + p
            total[idx] = jnp.broadcast_to(1.0 / jnp.sum(summed, axis=1, keepdims=True), (HEADS * TILE, 128))

    strip_arrival(0, 1, OWN).wait_recv()
    value_blocks((OWN,), first=True)
    for s in range(3):
        wait_far(s, 0, 1, ok=late_in[s])
        send_strip(s, 0, 1, ok=late_in[s])
    for s in range(3):
        wait_far(s, 1, 1, ok=~needs_second[s])
        send_strip(s, 1, 1)
    for s in range(3):
        wait_strip(s, 0, 1)
    value_blocks(first_in)
    for s in range(3):
        wait_strip(s, 1, 1)
    value_blocks(second_slots)

    @pl.loop(0, ROWS)
    def _(r):
        for t in range(TILES):
            idx = r * TILES + t
            out = None
            for h in range(HEADS):
                part = slice(h * TILE, (h + 1) * TILE)
                inverse = total[idx, part, :]
                o = acc[idx, part, :] * jnp.concatenate([inverse, inverse], axis=1) * head_mask[h]
                out = o if out is None else out + o
            out_far[r, TILE * t : TILE * (t + 1), :] = out.astype(jnp.bfloat16)

    far_out = pltpu.make_async_copy(out_far, of_ref, out_sem.at[1])
    far_out.start()

    for o in range(2):
        for s in range(3):
            for kv in range(2):
                for part in (0, 1):
                    @pl.when((send_ok[o][s] & inner) if part else send_ok[o][s])
                    def _():
                        far_copy(s, o, kv, part).wait_send()

                @pl.when(recv_ok[o][s])
                def _():
                    strip_copy(1 + 3 * o + s, kv, in_slot[o][s]).wait_send()

    for kv in range(2):
        strip_copy(0, kv, OWN).wait_send()

        @pl.when(inner)
        def _():
            side_copy(kv).wait_send()

    for n, (dr, dc) in enumerate(sides):
        @pl.when(there(dr, dc))
        def _():
            near_copy(n, 0).wait_send()
            near_copy(n, 1).wait_send()

    near_out.wait()
    far_out.wait()


def per_device(query_near, key_near, value_near, dilated_queries, dilated_keys, dilated_values):
    block = jax.ShapeDtypeStruct((ROWS, COLS, CH), jnp.bfloat16)
    tiles = ROWS * TILES
    dma = pltpu.SemaphoreType.DMA
    anywhere = pl.BlockSpec(memory_space=pl.ANY)
    return pl.pallas_call(
        kernel,
        out_shape=(block, block),
        in_specs=[anywhere] * 6,
        out_specs=(anywhere, anywhere),
        scratch_shapes=[
            pltpu.VMEM((2, SLOTS, ROWS, WIDE, CH), jnp.bfloat16),
            pltpu.VMEM((2, NEAR_ROWS, NEAR_WIDE, CH), jnp.bfloat16),
            pltpu.VMEM((ROWS, COLS, CH), jnp.bfloat16),
            pltpu.VMEM((ROWS, COLS, CH), jnp.bfloat16),
            pltpu.VMEM((tiles, HEADS * TILE, CH), jnp.bfloat16),
            pltpu.VMEM((SLOTS, tiles, HEADS * TILE, KEYS), jnp.float32),
            pltpu.VMEM((tiles, HEADS * TILE, KEYS), jnp.float32),
            pltpu.VMEM((SLOTS, tiles, HEADS * TILE, KEYS), jnp.bfloat16),
            pltpu.VMEM((tiles, HEADS * TILE, 128), jnp.float32),
            pltpu.VMEM((tiles, HEADS * TILE, CH), jnp.float32),
            pltpu.VMEM((TILES, TILE, KEYS), jnp.float32),
            pltpu.VMEM((2 * TILES, 2 * TILE, 8 * NEAR_KEYS), jnp.float32),
            pltpu.VMEM((ROWS, COLS, CH), jnp.bfloat16),
            pltpu.VMEM((ROWS, COLS, CH), jnp.bfloat16),
            dma((6,)),
            dma((3, 2, 2, 2)),
            dma((3, 2, 2, 2)),
            dma((7, 2)),
            dma((7, 2)),
            dma((2,)),
            dma((2,)),
            dma((8, 2)),
            dma((8, 2)),
            dma((2,)),
        ],
        compiler_params=pltpu.CompilerParams(
            collective_id=0, has_side_effects=True, vmem_limit_bytes=48 << 20
        ),
        name="two_layers",
    )(query_near, key_near, value_near, dilated_queries, dilated_keys, dilated_values)


def solution(mesh):
    placed = (P("row", "col", None),) * 6
    return jax.shard_map(
        per_device,
        mesh=mesh,
        in_specs=placed,
        out_specs=(P("row", "col", None), P("row", "col", None)),
        check_vma=False,
    )
```

```python
import functools
import math

import jax
import jax.numpy as jnp
from jax import lax
from jax.experimental import pallas as pl
from jax.experimental.pallas import tpu as pltpu
from jax.sharding import PartitionSpec as P

MESH = pl.DeviceIdType.MESH
HEADS = 4
HEAD = 64
CH = 256
ROWS = 4
COLS = 128
STRIP = 48
WIDE = COLS + 2 * STRIP
STEP = 16
HALF = ROWS // 2
SLOTS = 7
OWN = 3
EDGE = 16
NEAR_WIDE = COLS + 2 * EDGE
NEAR_ROWS = ROWS + 6
TILE = 32
TILES = COLS // TILE
KEYS = TILE + 2 * STRIP
NEAR_KEYS = TILE + 2 * EDGE
SCALE = math.log2(math.e) / math.sqrt(HEAD)
NONE = 99

SECOND = (
    (1, -1, -1, NONE, 1, -2, NONE, NONE),
    (NONE, NONE, 2, -1, NONE, 1, 1, -1),
    (4, 2, 2, 2, -2, -2, -2, -4),
)
FROM_STREAM = ((2, 2, 0, 0, 2, 0, 0, 0), (0, 0, 1, 2, 0, 1, 2, 2), (1, 1, 1, 1, 0, 0, 0, 0))
FROM_SECOND = ((0, 0, 1, 0, 0, 0, 0, 0), (0, 0, 0, 0, 0, 1, 0, 0), (1, 0, 0, 0, 0, 0, 0, 1))
VALUES_LAST = ((0, 5), (2, 7), ())


def pick(table, place):
    out = jnp.int32(table[0])
    for k in range(1, len(table)):
        out = jnp.where(place == k, jnp.int32(table[k]), out)
    return out


def one_of(place, places):
    out = jnp.bool_(False)
    for k in places:
        out = out | (place == k)
    return out


def kernel(
    qn_ref, kn_ref, vn_ref, qf_ref, kf_ref, vf_ref, on_ref, of_ref,
    far, near, qn, qf, qb, scores, peak, probs, total, acc, bias_far, bias_near, edge_out, edge_in, passing, out_near, out_far,
    load_sem, far_send, far_recv, strip_send, strip_recv, side_send, side_recv, extra_send, extra_recv, near_send, near_recv, pass_send, pass_recv, out_sem,
):
    row = lax.axis_index("row")
    col = lax.axis_index("col")
    n_rows = lax.axis_size("row")
    n_cols = lax.axis_size("col")
    x = row // 8
    z = (row // 4) % 2
    y = row % 4
    core = col % 2
    place = 2 * x + z
    inner = (col == 1) | (col == 2)
    true = jnp.bool_(True)

    loads = [
        pltpu.make_async_copy(kf_ref, far.at[0, OWN, :, pl.ds(STRIP, COLS)], load_sem.at[0]),
        pltpu.make_async_copy(vf_ref, far.at[1, OWN, :, pl.ds(STRIP, COLS)], load_sem.at[1]),
        pltpu.make_async_copy(kn_ref, near.at[0, pl.ds(3, ROWS), pl.ds(EDGE, COLS)], load_sem.at[2]),
        pltpu.make_async_copy(vn_ref, near.at[1, pl.ds(3, ROWS), pl.ds(EDGE, COLS)], load_sem.at[3]),
        pltpu.make_async_copy(qf_ref, qf, load_sem.at[4]),
        pltpu.make_async_copy(qn_ref, qn, load_sem.at[5]),
    ]
    for load in loads:
        load.start()

    to_row = (row + 8, row - 8, row + 4 - 8 * z)
    hop = 1 - 2 * z

    def arrivals(at, hop):
        first_ok = (at >= 2, at < 6, true)
        back = (-2, 2, hop)
        sent = [pick(SECOND[s], at + back[s]) for s in range(3)]
        second_ok = [first_ok[s] & (sent[s] != NONE) for s in range(3)]
        return (first_ok, second_ok), (back, [sent[s] + back[s] for s in range(3)])

    def slot_of(rel):
        return (rel + 10) % 7

    recv_ok, recv_rel = arrivals(place, hop)
    mate_ok, mate_rel = arrivals(place + hop, -hop)
    in_slot = [[slot_of(jnp.int32(rel)) for rel in rels] for rels in recv_rel]
    second_rel = [pick(SECOND[s], place) for s in range(3)]
    second_send = [second_rel[s] != NONE for s in range(3)]
    send_ok = ((x < 3, x > 0, true), second_send)
    shift = (-2, 2, -hop)
    src_slot = ([jnp.int32(OWN)] * 3, [slot_of(second_rel[s]) for s in range(3)])
    dst_slot = ([slot_of(jnp.int32(shift[s])) for s in range(3)], [slot_of(second_rel[s] + shift[s]) for s in range(3)])
    values_last = [one_of(place, VALUES_LAST[s]) for s in range(3)]
    late_in = [recv_ok[0][s] & one_of(place + (-2, 2, hop)[s], VALUES_LAST[s]) for s in range(3)]

    def piece(kv, hf):
        if kv == 0:
            return pl.ds(hf * HALF, HALF), pl.ds(STRIP, COLS)
        right = (col < 2) == (hf == 0)
        return pl.ds(0, ROWS), pl.ds(pl.multiple_of(jnp.where(right, STRIP + COLS // 2, STRIP), 16), COLS // 2)

    def strip_rows(kv, hf):
        return pl.ds(hf * HALF, HALF) if kv == 0 else pl.ds(0, ROWS)

    def far_copy(s, o, kv, hf):
        return pltpu.make_async_remote_copy(
            far.at[kv, src_slot[o][s], *piece(kv, hf)],
            far.at[kv, dst_slot[o][s], *piece(kv, hf)],
            far_send.at[s, o, kv, hf],
            far_recv.at[s, o, kv, hf],
            device_id=(to_row[s], col),
            device_id_type=MESH,
        )

    def send_far(s, o, kv, hf, ok=true):
        @pl.when(send_ok[o][s] & ok)
        def _():
            far_copy(s, o, kv, hf).start()

    def wait_far(s, o, kv, hf, ok=true):
        @pl.when(recv_ok[o][s] & ok)
        def _():
            block = far.at[kv, in_slot[o][s], *piece(kv, hf)]
            pltpu.make_async_remote_copy(
                block, block, far_send.at[s, o, kv, hf], far_recv.at[s, o, kv, hf],
                device_id=(to_row[s], col), device_id_type=MESH,
            ).wait_recv()

    mate = col + 1 - 2 * core
    strip_src = pl.multiple_of(jnp.where(core == 0, COLS, STRIP), 16)
    strip_dst = pl.multiple_of(jnp.where(core == 0, 0, STRIP + COLS), 16)
    strip_in = pl.multiple_of(jnp.where(core == 0, STRIP + COLS, 0), 16)

    def strip_copy(e, kv, hf, slot):
        return pltpu.make_async_remote_copy(
            far.at[kv, slot, strip_rows(kv, hf), pl.ds(strip_src, STRIP)],
            far.at[kv, slot, strip_rows(kv, hf), pl.ds(strip_dst, STRIP)],
            strip_send.at[e, kv, hf],
            strip_recv.at[e, kv, hf],
            device_id=(row, mate),
            device_id_type=MESH,
        )

    def wait_strip_at(e, kv, hf, slot):
        block = far.at[kv, slot, strip_rows(kv, hf), pl.ds(strip_in, STRIP)]
        pltpu.make_async_remote_copy(
            block, block, strip_send.at[e, kv, hf], strip_recv.at[e, kv, hf],
            device_id=(row, mate), device_id_type=MESH,
        ).wait_recv()

    def event(s, o):
        return 1 + 3 * o + s

    side_src = pl.multiple_of(jnp.where(col == 1, COLS, STRIP), 16)
    side_dst = pl.multiple_of(jnp.where(col == 1, 0, STRIP + COLS), 16)
    side_in = pl.multiple_of(jnp.where(col == 1, STRIP + COLS, 0), 16)

    def side_ok(ok, rel):
        return inner & ok & (rel >= -3) & (rel <= 3)

    def side_copy(e, kv, hf, rel):
        return pltpu.make_async_remote_copy(
            far.at[kv, slot_of(rel), strip_rows(kv, hf), pl.ds(side_src, STRIP)],
            far.at[kv, OWN + rel - hop, strip_rows(kv, hf), pl.ds(side_dst, STRIP)],
            side_send.at[e, kv, hf],
            side_recv.at[e, kv, hf],
            device_id=(to_row[2], 3 - col),
            device_id_type=MESH,
        )

    def wait_side(e, kv, hf, ok, rel):
        @pl.when(side_ok(ok, rel + hop))
        def _():
            block = far.at[kv, OWN + rel + hop, strip_rows(kv, hf), pl.ds(side_in, STRIP)]
            pltpu.make_async_remote_copy(
                block, block, side_send.at[e, kv, hf], side_recv.at[e, kv, hf],
                device_id=(to_row[2], 3 - col), device_id_type=MESH,
            ).wait_recv()

    own_rel = jnp.int32(0)
    extra_ok = (inner & (place == 4), inner & (place == 3))
    extra_slot = (0, 6)

    def extra_copy(s, kv, hf):
        return pltpu.make_async_remote_copy(
            far.at[kv, extra_slot[s], strip_rows(kv, hf), pl.ds(side_src, STRIP)],
            far.at[kv, extra_slot[s], strip_rows(kv, hf), pl.ds(side_dst, STRIP)],
            extra_send.at[kv, hf],
            extra_recv.at[kv, hf],
            device_id=(row, 3 - col),
            device_id_type=MESH,
        )

    def wait_extra(kv, hf):
        for s in range(2):
            @pl.when(extra_ok[s])
            def _():
                block = far.at[kv, extra_slot[s], strip_rows(kv, hf), pl.ds(side_in, STRIP)]
                pltpu.make_async_remote_copy(
                    block, block, extra_send.at[kv, hf], extra_recv.at[kv, hf],
                    device_id=(row, 3 - col), device_id_type=MESH,
                ).wait_recv()

    def send_strips(s, o, kv, hf, ok=true):
        ok = recv_ok[o][s] & ok
        rel = recv_rel[o][s]
        e = event(s, o)
        mine = true if kv == 0 else (inner if hf else ~inner)
        part = hf if kv == 0 else 0

        @pl.when(ok & mine)
        def _():
            strip_copy(e, kv, part, in_slot[o][s]).start()

        if kv == 0 or hf == 0:
            @pl.when(side_ok(ok, rel - hop))
            def _():
                side_copy(e, kv, part, rel).start()

            if o == 1 and s < 2:
                @pl.when(extra_ok[s] & ok)
                def _():
                    extra_copy(s, kv, part).start()

    def wait_strip(s, o, kv, hf):
        @pl.when(recv_ok[o][s])
        def _():
            wait_strip_at(event(s, o), kv, hf, in_slot[o][s])

    sides = [(dr, dc) for dr in (-1, 0, 1) for dc in (-1, 0, 1) if (dr, dc) != (0, 0)]

    def there(dr, dc):
        good = true
        if dr:
            good = good & ((row + dr >= 0) & (row + dr < n_rows))
        if dc:
            good = good & ((col + dc >= 0) & (col + dc < n_cols))
        return good

    row_src = {1: (4, 3), -1: (3, 3)}
    row_dst = {1: (0, 3), -1: (7, 3)}
    row_from = {1: 1, 0: 0, -1: 0}
    row_to = {1: 0, 0: 3, -1: 7}
    main = pl.ds(EDGE, COLS)

    def crossing(dr):
        return {0: jnp.bool_(False), 1: y == 3, -1: y == 0}[dr]

    def crossed(dr):
        return {0: jnp.bool_(False), 1: y == 0, -1: y == 3}[dr]

    def passed(dr):
        return {1: (y == 1) & (row - 2 >= 0) & (row - 2 < n_rows), -1: (y == 2) & (row + 2 >= 0) & (row + 2 < n_rows)}[dr]

    def pass_in(dr):
        return pltpu.make_async_remote_copy(
            near.at[0, pl.ds(*row_src[dr]), main],
            passing,
            pass_send.at[0],
            pass_recv.at[0],
            device_id=(row + 2 * dr, col),
            device_id_type=MESH,
        )

    def pass_on(dr):
        n = sides.index((dr, 0))
        return pltpu.make_async_remote_copy(
            passing,
            near.at[0, pl.ds(*row_dst[dr]), main],
            pass_send.at[0],
            near_recv.at[n, 0],
            device_id=(row + -1 * dr, col),
            device_id_type=MESH,
        )

    def near_copy(n, kv):
        dr, dc = sides[n]
        if dc:
            src, dst = edge_out.at[(dc + 1) // 2], edge_in.at[n]
        else:
            src, dst = near.at[kv, pl.ds(*row_src[dr]), main], near.at[kv, pl.ds(*row_dst[dr]), main]
        return pltpu.make_async_remote_copy(
            src, dst, near_send.at[n, kv], near_recv.at[n, kv], device_id=(row + dr, col + dc), device_id_type=MESH
        )

    def near_arrival(n, kv):
        dr, dc = sides[n]
        block = edge_in.at[n] if dc else near.at[kv, pl.ds(*row_dst[dr]), main]
        return pltpu.make_async_remote_copy(
            block, block, near_send.at[n, kv], near_recv.at[n, kv],
            device_id=(row - dr, col - dc), device_id_type=MESH,
        )

    barrier = pltpu.get_barrier_semaphore()
    expected = jnp.int32(0)
    for s in range(3):
        @pl.when(send_ok[0][s])
        def _():
            pl.semaphore_signal(barrier, inc=1, device_id=(to_row[s], col), device_id_type=MESH)

        expected = expected + recv_ok[0][s].astype(jnp.int32)

    @pl.when(inner)
    def _():
        pl.semaphore_signal(barrier, inc=1, device_id=(to_row[2], 3 - col), device_id_type=MESH)

    expected = expected + inner.astype(jnp.int32)
    for dr, dc in sides:
        @pl.when(there(dr, dc))
        def _():
            pl.semaphore_signal(barrier, inc=1, device_id=(row + dr, col + dc), device_id_type=MESH)

        expected = expected + there(-dr, -dc).astype(jnp.int32)
    for dr in (-1, 1):
        @pl.when(crossing(dr) & there(dr, 0))
        def _():
            pl.semaphore_signal(barrier, inc=1, device_id=(row + 2 * dr, col), device_id_type=MESH)

        @pl.when(passed(dr))
        def _():
            pl.semaphore_signal(barrier, inc=1, device_id=(row - 2 * dr, col), device_id_type=MESH)


        expected = expected + (crossing(dr) & there(dr, 0)).astype(jnp.int32) + passed(dr).astype(jnp.int32)
    pl.semaphore_wait(barrier, expected)

    for kv in range(2):
        loads[kv].wait()
        for hf in range(2):
            for s in range(3):
                send_far(s, 0, kv, hf, ok=~values_last[s] if kv else true)
            if kv == 0 or hf == 0:
                strip_copy(0, kv, hf, OWN).start()

                @pl.when(inner)
                def _():
                    side_copy(0, kv, hf, own_rel).start()

    loads[2].wait()
    loads[3].wait()
    for dc in (-1, 1):
        at = EDGE + (COLS - EDGE if dc == 1 else 0)
        inside = EDGE - 4 if dc == 1 else 0
        for kv in range(2):
            parts = [near[kv, 3 + r, at : at + EDGE, :].astype(jnp.float32)[inside : inside + 4] for r in range(ROWS)]
            edge_out[(dc + 1) // 2, kv] = jnp.concatenate(parts, axis=0).astype(jnp.bfloat16)

    def send_near(late):
        for n, (dr, dc) in enumerate(sides):
            good = there(dr, dc) & (crossing(dr) == late)
            for kv in range(1 if dc else 2):
                ok = good & ~crossing(dr) if (kv == 0 and not dc) else good

                @pl.when(ok)
                def _():
                    near_copy(n, kv).start()

        if late:
            for dr in (-1, 1):
                @pl.when(crossing(dr) & there(dr, 0))
                def _():
                    pass_in(dr).start()

    def pass_near():
        for dr in (-1, 1):
            @pl.when(passed(dr))
            def _():
                pltpu.make_async_remote_copy(
                    passing, passing, pass_send.at[0], pass_recv.at[0],
                    device_id=(row - 2 * dr, col), device_id_type=MESH,
                ).wait_recv()
                pass_on(dr).start()

    def wait_near(late):
        for n, (dr, dc) in enumerate(sides):
            @pl.when(there(-dr, -dc) & (crossing(-dr) == late))
            def _():
                near_arrival(n, 0).wait_recv()
                if dc == 0:
                    near_arrival(n, 1).wait_recv()
                else:
                    at = 0 if dc == 1 else EDGE + COLS
                    blank = jnp.zeros((EDGE - 4, CH), jnp.float32)
                    for kv in range(2):
                        packed = edge_in[n, kv].astype(jnp.float32)
                        for r in range(ROWS if dr == 0 else 3):
                            four = packed[4 * (row_from[dr] + r) : 4 * (row_from[dr] + r) + 4]
                            full = [blank, four] if dc == 1 else [four, blank]
                            near[kv, row_to[dr] + r, at : at + EDGE, :] = jnp.concatenate(full, axis=0).astype(
                                jnp.bfloat16
                            )

    send_near(False)
    send_near(True)

    c0 = col * COLS
    width = n_cols * COLS
    for t in range(TILES):
        q_at = lax.broadcasted_iota(jnp.int32, (TILE, KEYS), 0)
        k_at = lax.broadcasted_iota(jnp.int32, (TILE, KEYS), 1)
        apart = k_at - q_at
        k_col = c0 + TILE * t - STRIP + k_at
        good = ((apart & (STEP - 1)) == 0) & (apart >= 0) & (apart <= 2 * STRIP) & (k_col >= 0) & (k_col < width)
        bias_far[t] = jnp.where(good, 0.0, -jnp.inf)
    for rp in range(2):
        for t in range(TILES):
            shape = (2, TILE, 8, NEAR_KEYS)
            shape = (2 * TILE, 8 * NEAR_KEYS)
            q_id = lax.broadcasted_iota(jnp.int32, shape, 0)
            k_id = lax.broadcasted_iota(jnp.int32, shape, 1)
            r_off = (k_id // NEAR_KEYS) - (q_id // TILE)
            c_off = (k_id % NEAR_KEYS) - (q_id % TILE) - EDGE
            k_row = row * ROWS + 2 * rp - 3 + (k_id // NEAR_KEYS)
            k_col = c0 + TILE * t - EDGE + (k_id % NEAR_KEYS)
            good = (r_off >= 0) & (r_off <= 6) & (c_off >= -3) & (c_off <= 3)
            good = good & (k_row >= 0) & (k_row < n_rows * ROWS) & (k_col >= 0) & (k_col < width)
            bias_near[rp * TILES + t] = jnp.where(good, 0.0, -jnp.inf)

    zero = lambda shape: jnp.zeros(shape, jnp.bfloat16)
    for a in range(SLOTS):
        relayed = (a == 0) & (place == 0) | (a == 6) & (place == 7)
        lost = ((place + a - OWN < 0) | (place + a - OWN > 7)) & ~relayed

        @pl.when(lost)
        def _():
            for kv in range(2):
                for r in range(ROWS):
                    far[kv, a, r] = zero((WIDE, CH))

        @pl.when(~lost & (col == 0))
        def _():
            for kv in range(2):
                for r in range(ROWS):
                    far[kv, a, r, 0:STRIP] = zero((STRIP, CH))

        @pl.when(~lost & (col == 3))
        def _():
            for kv in range(2):
                for r in range(ROWS):
                    far[kv, a, r, STRIP + COLS : WIDE] = zero((STRIP, CH))

        if a in (0, 6):
            @pl.when(relayed & inner)
            def _():
                for kv in range(2):
                    for r in range(ROWS):
                        far[kv, a, r, pl.ds(side_in, STRIP)] = zero((STRIP, CH))

    for kv in range(2):
        @pl.when(row == 0)
        def _():
            near[kv, 0:3] = zero((3, NEAR_WIDE, CH))

        @pl.when(row == n_rows - 1)
        def _():
            near[kv, 7:10] = zero((3, NEAR_WIDE, CH))

        @pl.when(col == 0)
        def _():
            near[kv, :, 0:EDGE] = zero((NEAR_ROWS, EDGE, CH))

        @pl.when(col == n_cols - 1)
        def _():
            near[kv, :, EDGE + COLS : NEAR_WIDE] = zero((NEAR_ROWS, EDGE, CH))

    lane_head = lax.broadcasted_iota(jnp.int32, (1, CH), 1) // HEAD
    head_mask = [(lane_head == h).astype(jnp.float32) for h in range(HEADS)]
    head_mask_narrow = [m.astype(jnp.bfloat16) for m in head_mask]
    dims_t = (((1,), (1,)), ((), ()))
    dims = (((1,), (0,)), ((), ()))

    loads[4].wait()
    loads[5].wait()

    def block_queries(q):
        return jnp.concatenate([q * head_mask_narrow[h] for h in range(HEADS)], axis=0)

    @pl.loop(0, ROWS, unroll=2)
    def _(r):
        for t in range(TILES):
            qb[r * TILES + t] = block_queries(qf[r, TILE * t : TILE * (t + 1), :])

    half_tiles = (jnp.where(col < 2, 0, 2), jnp.where(col < 2, 2, 0))

    def score_blocks(hf, slots, part, first=False):
        row_bias = []
        for slot in slots:
            ok = (place + slot - OWN >= 0) & (place + slot - OWN <= 7)
            row_bias.append(jnp.where(ok, 0.0, -jnp.inf).astype(jnp.float32))

        @pl.loop(hf * HALF, hf * HALF + HALF, unroll=True)
        def _(r):
            for tt in range(2):
                t = half_tiles[part] + tt
                idx = r * TILES + t
                where = pl.ds(pl.multiple_of(TILE * t, TILE), KEYS)
                top = None if first else peak[idx]
                for n in range(0, len(slots), 2):
                    pair = slots[n : n + 2]
                    k = jnp.concatenate([far[0, slot, r, where, :] for slot in pair], axis=0)
                    both = lax.dot_general(qb[idx], k, dims_t, preferred_element_type=jnp.float32) * SCALE
                    for m, slot in enumerate(pair):
                        b = bias_far[t] + row_bias[n + m]
                        s = both[:, m * KEYS : (m + 1) * KEYS].reshape(HEADS, TILE, KEYS) + b[None]
                        s = s.reshape(HEADS * TILE, KEYS)
                        scores[slot, idx] = s
                        top = s if top is None else jnp.maximum(top, s)
                peak[idx] = top

    def value_sum(idx, r, t, slots, o):
        where = pl.ds(pl.multiple_of(TILE * t, TILE), KEYS)
        for n in range(0, len(slots), 2):
            pair = slots[n : n + 2]
            p = jnp.concatenate([probs[slot, idx] for slot in pair], axis=1)
            v = jnp.concatenate([far[1, slot, r, where, :] for slot in pair], axis=0)
            d = lax.dot_general(p, v, dims, preferred_element_type=jnp.float32)
            o = d if o is None else o + d
        return o

    from_stream = [pick(FROM_STREAM[s], place) for s in range(3)]
    after_first = [pick(FROM_SECOND[s], place) == 0 for s in range(3)]
    needs_second = [jnp.bool_(False)] * 3
    for s in range(3):
        for d in range(3):
            needs_second[d] = needs_second[d] | (second_send[s] & ~after_first[s] & (from_stream[s] == d))

    first_slots = (jnp.int32(1), jnp.int32(5), OWN + hop)
    second_slots = (jnp.int32(0), jnp.int32(6), OWN - hop)
    own = jnp.int32(OWN)

    def later_sides(kv, hf):
        for o in range(2):
            for s in range(3):
                if (s, o) != (2, 0):
                    wait_side(event(s, o), kv, hf, mate_ok[o][s], mate_rel[o][s])
        wait_extra(kv, hf)

    for hf in range(2):
        for s in range(3):
            wait_far(s, 0, 0, hf)
        for s in range(3):
            send_far(s, 1, 0, hf, ok=after_first[s])
        for s in range(3):
            send_strips(s, 0, 0, hf)
    for hf in range(2):
        wait_strip_at(0, 0, hf, OWN)
        for s in range(3):
            wait_strip(s, 0, 0, hf)
        score_blocks(hf, (own,) + first_slots, 0, first=True)
    for hf in range(2):
        wait_side(0, 0, hf, true, own_rel)
        wait_side(event(2, 0), 0, hf, mate_ok[0][2], mate_rel[0][2])
        score_blocks(hf, (own, first_slots[2]), 1, first=True)

    for hf in range(2):
        for s in range(3):
            wait_far(s, 0, 1, hf, ok=~late_in[s])
        for s in range(3):
            send_far(s, 1, 1, hf, ok=after_first[s])
        if hf == 1:
            for h in range(2):
                for s in range(3):
                    send_far(s, 0, 1, h, ok=values_last[s])
        for s in range(3):
            wait_far(s, 1, 0, hf, ok=needs_second[s])
        for s in range(3):
            send_far(s, 1, 0, hf, ok=~after_first[s])
        for s in range(3):
            send_strips(s, 0, 1, hf, ok=~late_in[s])

    def near_layer(rp):
        @pl.loop(0, TILES, unroll=True)
        def _(t):
            cols = pl.ds(pl.multiple_of(TILE * t, TILE), TILE)
            keys = pl.ds(pl.multiple_of(TILE * t, TILE), NEAR_KEYS)
            q = qn[pl.ds(2 * rp, 2), cols, :].reshape(2 * TILE, CH)
            k = near[0, pl.ds(2 * rp, 8), keys, :].reshape(8 * NEAR_KEYS, CH)
            v = near[1, pl.ds(2 * rp, 8), keys, :].reshape(8 * NEAR_KEYS, CH)
            s = lax.dot_general(block_queries(q), k, dims_t, preferred_element_type=jnp.float32) * SCALE
            s = s.reshape(HEADS, 2 * TILE, 8 * NEAR_KEYS) + bias_near[rp * TILES + t][None]
            s = s.reshape(HEADS * 2 * TILE, 8 * NEAR_KEYS)
            p = jnp.exp2(s - jnp.max(s, axis=1, keepdims=True))
            inverse = 1.0 / jnp.sum(p, axis=1, keepdims=True)
            o = lax.dot_general(p.astype(jnp.bfloat16), v, dims, preferred_element_type=jnp.float32) * inverse
            out = None
            for h in range(HEADS):
                part = o[h * 2 * TILE : (h + 1) * 2 * TILE] * head_mask[h]
                out = part if out is None else out + part
            out_near[pl.ds(2 * rp, 2), cols, :] = out.astype(jnp.bfloat16).reshape(2, TILE, CH)

    def relay_second_values(hf):
        for s in range(3):
            wait_far(s, 1, 1, hf, ok=needs_second[s])
        for s in range(3):
            send_far(s, 1, 1, hf, ok=~after_first[s])

    for hf in range(2):
        relay_second_values(hf)
        for s in range(3):
            wait_far(s, 1, 0, hf, ok=~needs_second[s])
        for s in range(3):
            send_strips(s, 1, 0, hf)
        if hf == 0:
            pass_near()
    for hf in range(2):
        for s in range(3):
            wait_strip(s, 1, 0, hf)
        score_blocks(hf, second_slots, 0)

    def last_values(hf):
        for s in range(2):
            wait_far(s, 0, 1, hf, ok=late_in[s])
        for s in range(2):
            send_strips(s, 0, 1, hf, ok=late_in[s])
        for s in range(3):
            wait_far(s, 1, 1, hf, ok=~needs_second[s])
        for s in range(3):
            send_strips(s, 1, 1, hf)

    later_sides(0, 0)
    later_sides(0, 1)
    last_values(0)
    for hf in range(2):
        score_blocks(hf, first_slots[:2] + second_slots, 1)

    @pl.loop(0, ROWS, unroll=2)
    def _(r):
        for t in range(TILES):
            idx = r * TILES + t
            m = jnp.max(peak[idx], axis=1, keepdims=True)
            summed = None
            for a in range(SLOTS):
                p = jnp.exp2(scores[a, idx] - m)
                probs[a, idx] = p.astype(jnp.bfloat16)
                summed = p if summed is None else summed + p
            total[idx] = jnp.broadcast_to(1.0 / jnp.sum(summed, axis=1, keepdims=True), (HEADS * TILE, 128))

    wait_strip_at(0, 1, 0, OWN)
    wait_strip(2, 0, 1, 0)
    wait_side(0, 1, 0, true, own_rel)
    wait_side(event(2, 0), 1, 0, mate_ok[0][2], mate_rel[0][2])

    @pl.loop(0, ROWS, unroll=2)
    def _(r):
        for t in range(TILES):
            idx = r * TILES + t
            acc[idx] = value_sum(idx, r, t, (own, first_slots[2]), None)

    last_values(1)
    wait_near(False)
    wait_near(True)
    near_layer(0)
    near_layer(1)
    near_out = pltpu.make_async_copy(out_near, on_ref, out_sem.at[0])
    near_out.start()
    for s in range(2):
        wait_strip(s, 0, 1, 0)
    for s in range(3):
        wait_strip(s, 1, 1, 0)
    later_sides(1, 0)

    @pl.loop(0, ROWS, unroll=2)
    def _(r):
        for t in range(TILES):
            idx = r * TILES + t
            o = value_sum(idx, r, t, first_slots[:2] + second_slots, acc[idx])
            out = None
            for h in range(HEADS):
                part = slice(h * TILE, (h + 1) * TILE)
                inverse = total[idx, part, :]
                one = o[part, :] * jnp.concatenate([inverse, inverse], axis=1) * head_mask[h]
                out = one if out is None else out + one
            out_far[r, TILE * t : TILE * (t + 1), :] = out.astype(jnp.bfloat16)

    far_out = pltpu.make_async_copy(out_far, of_ref, out_sem.at[1])
    far_out.start()

    for kv in range(2):
        for hf in range(2):
            if kv == 0 or hf == 0:
                strip_copy(0, kv, hf, OWN).wait_send()

                @pl.when(inner)
                def _():
                    side_copy(0, kv, hf, own_rel).wait_send()

                for s in range(2):
                    @pl.when(extra_ok[s])
                    def _():
                        extra_copy(s, kv, hf).wait_send()

            for o in range(2):
                for s in range(3):
                    @pl.when(send_ok[o][s])
                    def _():
                        far_copy(s, o, kv, hf).wait_send()

                    if kv == 0 or hf == 0:
                        @pl.when(recv_ok[o][s])
                        def _():
                            strip_copy(event(s, o), kv, hf, in_slot[o][s]).wait_send()

                        @pl.when(side_ok(recv_ok[o][s], recv_rel[o][s] - hop))
                        def _():
                            side_copy(event(s, o), kv, hf, recv_rel[o][s]).wait_send()

    for n, (dr, dc) in enumerate(sides):
        for kv in range(1 if dc else 2):
            good = there(dr, dc) & ~crossing(dr) if (kv == 0 and not dc) else there(dr, dc)

            @pl.when(good)
            def _():
                near_copy(n, kv).wait_send()

    for dr in (-1, 1):
        @pl.when(crossing(dr) & there(dr, 0))
        def _():
            pass_in(dr).wait_send()

        @pl.when(passed(dr))
        def _():
            pass_on(dr).wait_send()

    near_out.wait()
    far_out.wait()


def per_device(query_near, key_near, value_near, dilated_queries, dilated_keys, dilated_values):
    block = jax.ShapeDtypeStruct((ROWS, COLS, CH), jnp.bfloat16)
    tiles = ROWS * TILES
    dma = pltpu.SemaphoreType.DMA
    anywhere = pl.BlockSpec(memory_space=pl.ANY)
    return pl.pallas_call(
        kernel,
        out_shape=(block, block),
        in_specs=[pl.BlockSpec(memory_space=pltpu.HBM)] * 6,
        out_specs=(anywhere, anywhere),
        scratch_shapes=[
            pltpu.VMEM((2, SLOTS, ROWS, WIDE, CH), jnp.bfloat16),
            pltpu.VMEM((2, NEAR_ROWS, NEAR_WIDE, CH), jnp.bfloat16),
            pltpu.VMEM((ROWS, COLS, CH), jnp.bfloat16),
            pltpu.VMEM((ROWS, COLS, CH), jnp.bfloat16),
            pltpu.VMEM((tiles, HEADS * TILE, CH), jnp.bfloat16),
            pltpu.VMEM((SLOTS, tiles, HEADS * TILE, KEYS), jnp.float32),
            pltpu.VMEM((tiles, HEADS * TILE, KEYS), jnp.float32),
            pltpu.VMEM((SLOTS, tiles, HEADS * TILE, KEYS), jnp.bfloat16),
            pltpu.VMEM((tiles, HEADS * TILE, 128), jnp.float32),
            pltpu.VMEM((tiles, HEADS * TILE, CH), jnp.float32),
            pltpu.VMEM((TILES, TILE, KEYS), jnp.float32),
            pltpu.VMEM((2 * TILES, 2 * TILE, 8 * NEAR_KEYS), jnp.float32),
            pltpu.VMEM((2, 2, 4 * ROWS, CH), jnp.bfloat16),
            pltpu.VMEM((9, 2, 4 * ROWS, CH), jnp.bfloat16),
            pltpu.VMEM((3, COLS, CH), jnp.bfloat16),
            pltpu.VMEM((ROWS, COLS, CH), jnp.bfloat16),
            pltpu.VMEM((ROWS, COLS, CH), jnp.bfloat16),
            dma((6,)),
            dma((3, 2, 2, 2)),
            dma((3, 2, 2, 2)),
            dma((7, 2, 2)),
            dma((7, 2, 2)),
            dma((7, 2, 2)),
            dma((7, 2, 2)),
            dma((2, 2)),
            dma((2, 2)),
            dma((8, 2)),
            dma((8, 2)),
            dma((1,)),
            dma((1,)),
            dma((2,)),
        ],
        compiler_params=pltpu.CompilerParams(
            collective_id=0, has_side_effects=True, vmem_limit_bytes=56 << 20
        ),
        name="two_layers",
    )(query_near, key_near, value_near, dilated_queries, dilated_keys, dilated_values)


def solution(mesh):
    placed = (P("row", "col", None),) * 6
    return jax.shard_map(
        per_device,
        mesh=mesh,
        in_specs=placed,
        out_specs=(P("row", "col", None), P("row", "col", None)),
        check_vma=False,
    )
```

```python
import functools
import math

import jax
import jax.numpy as jnp
from jax import lax
from jax.experimental import pallas as pl
from jax.experimental.pallas import tpu as pltpu
from jax.sharding import PartitionSpec as P

MESH = pl.DeviceIdType.MESH
HEADS = 4
HEAD = 64
CH = 256
ROWS = 4
COLS = 128
STRIP = 48
WIDE = COLS + 2 * STRIP
STEP = 16
HALF = ROWS // 2
SLOTS = 7
OWN = 3
EDGE = 16
NEAR_WIDE = COLS + 2 * EDGE
NEAR_ROWS = ROWS + 6
TILE = 32
TILES = COLS // TILE
KEYS = TILE + 2 * STRIP
NEAR_KEYS = TILE + 2 * EDGE
SCALE = math.log2(math.e) / math.sqrt(HEAD)
NONE = 99

SECOND = (
    (1, -1, -1, NONE, 1, -2, NONE, NONE),
    (NONE, NONE, 2, -1, NONE, 1, 1, -1),
    (4, 2, 2, 2, -2, -2, -2, -4),
)
FROM_STREAM = ((2, 2, 0, 0, 2, 0, 0, 0), (0, 0, 1, 2, 0, 1, 2, 2), (1, 1, 1, 1, 0, 0, 0, 0))
FROM_SECOND = ((0, 0, 1, 0, 0, 0, 0, 0), (0, 0, 0, 0, 0, 1, 0, 0), (1, 0, 0, 0, 0, 0, 0, 1))
VALUES_LAST = ((0, 5), (2, 7), ())


def pick(table, place):
    out = jnp.int32(table[0])
    for k in range(1, len(table)):
        out = jnp.where(place == k, jnp.int32(table[k]), out)
    return out


def one_of(place, places):
    out = jnp.bool_(False)
    for k in places:
        out = out | (place == k)
    return out


def kernel(
    qn_ref, kn_ref, vn_ref, qf_ref, kf_ref, vf_ref, on_ref, of_ref,
    far, near, qn, qf, qb, scores, peak, probs, total, acc, bias_far, bias_near, edge_out, edge_in, passing, out_near, out_far,
    load_sem, far_send, far_recv, strip_send, strip_recv, side_send, side_recv, extra_send, extra_recv, near_send, near_recv, pass_send, pass_recv, out_sem,
):
    row = lax.axis_index("row")
    col = lax.axis_index("col")
    n_rows = lax.axis_size("row")
    n_cols = lax.axis_size("col")
    x = row // 8
    z = (row // 4) % 2
    y = row % 4
    core = col % 2
    place = 2 * x + z
    inner = (col == 1) | (col == 2)
    true = jnp.bool_(True)

    loads = [
        pltpu.make_async_copy(kf_ref, far.at[0, OWN, :, pl.ds(STRIP, COLS)], load_sem.at[0]),
        pltpu.make_async_copy(vf_ref, far.at[1, OWN, :, pl.ds(STRIP, COLS)], load_sem.at[1]),
        pltpu.make_async_copy(kn_ref, near.at[0, pl.ds(3, ROWS), pl.ds(EDGE, COLS)], load_sem.at[2]),
        pltpu.make_async_copy(vn_ref, near.at[1, pl.ds(3, ROWS), pl.ds(EDGE, COLS)], load_sem.at[3]),
        pltpu.make_async_copy(qf_ref, qf, load_sem.at[4]),
        pltpu.make_async_copy(qn_ref, qn, load_sem.at[5]),
    ]
    for load in loads:
        load.start()

    to_row = (row + 8, row - 8, row + 4 - 8 * z)
    hop = 1 - 2 * z

    def arrivals(at, hop):
        first_ok = (at >= 2, at < 6, true)
        back = (-2, 2, hop)
        sent = [pick(SECOND[s], at + back[s]) for s in range(3)]
        second_ok = [first_ok[s] & (sent[s] != NONE) for s in range(3)]
        return (first_ok, second_ok), (back, [sent[s] + back[s] for s in range(3)])

    def slot_of(rel):
        return (rel + 10) % 7

    recv_ok, recv_rel = arrivals(place, hop)
    mate_ok, mate_rel = arrivals(place + hop, -hop)
    in_slot = [[slot_of(jnp.int32(rel)) for rel in rels] for rels in recv_rel]
    second_rel = [pick(SECOND[s], place) for s in range(3)]
    second_send = [second_rel[s] != NONE for s in range(3)]
    send_ok = ((x < 3, x > 0, true), second_send)
    shift = (-2, 2, -hop)
    src_slot = ([jnp.int32(OWN)] * 3, [slot_of(second_rel[s]) for s in range(3)])
    dst_slot = ([slot_of(jnp.int32(shift[s])) for s in range(3)], [slot_of(second_rel[s] + shift[s]) for s in range(3)])
    values_last = [one_of(place, VALUES_LAST[s]) for s in range(3)]
    late_in = [recv_ok[0][s] & one_of(place + (-2, 2, hop)[s], VALUES_LAST[s]) for s in range(3)]

    def piece(kv, hf):
        if kv == 0:
            return pl.ds(hf * HALF, HALF), pl.ds(STRIP, COLS)
        right = (col < 2) == (hf == 0)
        return pl.ds(0, ROWS), pl.ds(pl.multiple_of(jnp.where(right, STRIP + COLS // 2, STRIP), 16), COLS // 2)

    def strip_rows(kv, hf):
        return pl.ds(hf * HALF, HALF) if kv == 0 else pl.ds(0, ROWS)

    def far_copy(s, o, kv, hf):
        return pltpu.make_async_remote_copy(
            far.at[kv, src_slot[o][s], *piece(kv, hf)],
            far.at[kv, dst_slot[o][s], *piece(kv, hf)],
            far_send.at[s, o, kv, hf],
            far_recv.at[s, o, kv, hf],
            device_id=(to_row[s], col),
            device_id_type=MESH,
        )

    def send_far(s, o, kv, hf, ok=true):
        @pl.when(send_ok[o][s] & ok)
        def _():
            far_copy(s, o, kv, hf).start()

    def wait_far(s, o, kv, hf, ok=true):
        @pl.when(recv_ok[o][s] & ok)
        def _():
            block = far.at[kv, in_slot[o][s], *piece(kv, hf)]
            pltpu.make_async_remote_copy(
                block, block, far_send.at[s, o, kv, hf], far_recv.at[s, o, kv, hf],
                device_id=(to_row[s], col), device_id_type=MESH,
            ).wait_recv()

    mate = col + 1 - 2 * core
    strip_src = pl.multiple_of(jnp.where(core == 0, COLS, STRIP), 16)
    strip_dst = pl.multiple_of(jnp.where(core == 0, 0, STRIP + COLS), 16)
    strip_in = pl.multiple_of(jnp.where(core == 0, STRIP + COLS, 0), 16)

    def strip_copy(e, kv, hf, slot):
        return pltpu.make_async_remote_copy(
            far.at[kv, slot, strip_rows(kv, hf), pl.ds(strip_src, STRIP)],
            far.at[kv, slot, strip_rows(kv, hf), pl.ds(strip_dst, STRIP)],
            strip_send.at[e, kv, hf],
            strip_recv.at[e, kv, hf],
            device_id=(row, mate),
            device_id_type=MESH,
        )

    def wait_strip_at(e, kv, hf, slot):
        block = far.at[kv, slot, strip_rows(kv, hf), pl.ds(strip_in, STRIP)]
        pltpu.make_async_remote_copy(
            block, block, strip_send.at[e, kv, hf], strip_recv.at[e, kv, hf],
            device_id=(row, mate), device_id_type=MESH,
        ).wait_recv()

    def event(s, o):
        return 1 + 3 * o + s

    side_src = pl.multiple_of(jnp.where(col == 1, COLS, STRIP), 16)
    side_dst = pl.multiple_of(jnp.where(col == 1, 0, STRIP + COLS), 16)
    side_in = pl.multiple_of(jnp.where(col == 1, STRIP + COLS, 0), 16)

    def side_ok(ok, rel):
        return inner & ok & (rel >= -3) & (rel <= 3)

    def side_copy(e, kv, hf, rel):
        return pltpu.make_async_remote_copy(
            far.at[kv, slot_of(rel), strip_rows(kv, hf), pl.ds(side_src, STRIP)],
            far.at[kv, OWN + rel - hop, strip_rows(kv, hf), pl.ds(side_dst, STRIP)],
            side_send.at[e, kv, hf],
            side_recv.at[e, kv, hf],
            device_id=(to_row[2], 3 - col),
            device_id_type=MESH,
        )

    def wait_side(e, kv, hf, ok, rel):
        @pl.when(side_ok(ok, rel + hop))
        def _():
            block = far.at[kv, OWN + rel + hop, strip_rows(kv, hf), pl.ds(side_in, STRIP)]
            pltpu.make_async_remote_copy(
                block, block, side_send.at[e, kv, hf], side_recv.at[e, kv, hf],
                device_id=(to_row[2], 3 - col), device_id_type=MESH,
            ).wait_recv()

    own_rel = jnp.int32(0)
    extra_ok = (inner & (place == 3), inner & (place == 4))
    extra_from = (1, 5)
    extra_to = (0, 6)
    extra_row = (row + 4, row - 4)

    def extra_copy(s, kv, hf):
        return pltpu.make_async_remote_copy(
            far.at[kv, extra_from[s], strip_rows(kv, hf), pl.ds(side_src, STRIP)],
            far.at[kv, extra_to[s], strip_rows(kv, hf), pl.ds(side_dst, STRIP)],
            extra_send.at[kv, hf],
            extra_recv.at[kv, hf],
            device_id=(extra_row[s], 3 - col),
            device_id_type=MESH,
        )

    def wait_extra(kv, hf):
        for s in range(2):
            @pl.when(extra_ok[s])
            def _():
                block = far.at[kv, extra_to[1 - s], strip_rows(kv, hf), pl.ds(side_in, STRIP)]
                pltpu.make_async_remote_copy(
                    block, block, extra_send.at[kv, hf], extra_recv.at[kv, hf],
                    device_id=(extra_row[s], 3 - col), device_id_type=MESH,
                ).wait_recv()

    def send_strips(s, o, kv, hf, ok=true):
        ok = recv_ok[o][s] & ok
        rel = recv_rel[o][s]
        e = event(s, o)
        mine = true if kv == 0 else (inner if hf else ~inner)
        part = hf if kv == 0 else 0

        @pl.when(ok & mine)
        def _():
            strip_copy(e, kv, part, in_slot[o][s]).start()

        if kv == 0 or hf == 0:
            @pl.when(side_ok(ok, rel - hop))
            def _():
                side_copy(e, kv, part, rel).start()

            if o == 0 and s < 2:
                @pl.when(extra_ok[s] & ok)
                def _():
                    extra_copy(s, kv, part).start()

    def wait_strip(s, o, kv, hf):
        @pl.when(recv_ok[o][s])
        def _():
            wait_strip_at(event(s, o), kv, hf, in_slot[o][s])

    sides = [(dr, dc) for dr in (-1, 0, 1) for dc in (-1, 0, 1) if (dr, dc) != (0, 0)]

    def there(dr, dc):
        good = true
        if dr:
            good = good & ((row + dr >= 0) & (row + dr < n_rows))
        if dc:
            good = good & ((col + dc >= 0) & (col + dc < n_cols))
        return good

    row_src = {1: (4, 3), -1: (3, 3)}
    row_dst = {1: (0, 3), -1: (7, 3)}
    row_from = {1: 1, 0: 0, -1: 0}
    row_to = {1: 0, 0: 3, -1: 7}
    main = pl.ds(EDGE, COLS)

    def crossing(dr):
        return {0: jnp.bool_(False), 1: y == 3, -1: y == 0}[dr]

    FIRST_LEG = (2, -1)
    LAST_LEG = (-1, 2)

    def sends_pass(dr):
        return crossing(dr) & there(dr, 0)

    def passes(kv, dr):
        at = {(0, 1): 1, (0, -1): 2, (1, 1): 2, (1, -1): 1}[kv, dr]
        back, on = row - FIRST_LEG[kv] * dr, row + LAST_LEG[kv] * dr
        return (y == at) & (back >= 0) & (back < n_rows) & (on >= 0) & (on < n_rows)

    def pass_in(kv, dr):
        return pltpu.make_async_remote_copy(
            near.at[kv, pl.ds(*row_src[dr]), main],
            passing.at[kv],
            pass_send.at[kv],
            pass_recv.at[kv],
            device_id=(row + FIRST_LEG[kv] * dr, col),
            device_id_type=MESH,
        )

    def pass_on(kv, dr):
        n = sides.index((dr, 0))
        return pltpu.make_async_remote_copy(
            passing.at[kv],
            near.at[kv, pl.ds(*row_dst[dr]), main],
            pass_send.at[kv],
            near_recv.at[n, kv],
            device_id=(row + LAST_LEG[kv] * dr, col),
            device_id_type=MESH,
        )

    def near_copy(n, kv):
        dr, dc = sides[n]
        if dc:
            src, dst = edge_out.at[(dc + 1) // 2], edge_in.at[n]
        else:
            src, dst = near.at[kv, pl.ds(*row_src[dr]), main], near.at[kv, pl.ds(*row_dst[dr]), main]
        return pltpu.make_async_remote_copy(
            src, dst, near_send.at[n, kv], near_recv.at[n, kv], device_id=(row + dr, col + dc), device_id_type=MESH
        )

    def near_arrival(n, kv):
        dr, dc = sides[n]
        block = edge_in.at[n] if dc else near.at[kv, pl.ds(*row_dst[dr]), main]
        return pltpu.make_async_remote_copy(
            block, block, near_send.at[n, kv], near_recv.at[n, kv],
            device_id=(row - dr, col - dc), device_id_type=MESH,
        )

    barrier = pltpu.get_barrier_semaphore()
    expected = jnp.int32(0)
    for s in range(3):
        @pl.when(send_ok[0][s])
        def _():
            pl.semaphore_signal(barrier, inc=1, device_id=(to_row[s], col), device_id_type=MESH)

        expected = expected + recv_ok[0][s].astype(jnp.int32)

    @pl.when(inner)
    def _():
        pl.semaphore_signal(barrier, inc=1, device_id=(to_row[2], 3 - col), device_id_type=MESH)

    expected = expected + inner.astype(jnp.int32)
    for s in range(2):
        @pl.when(extra_ok[s])
        def _():
            pl.semaphore_signal(barrier, inc=1, device_id=(extra_row[s], 3 - col), device_id_type=MESH)

        expected = expected + extra_ok[s].astype(jnp.int32)
    for dr, dc in sides:
        @pl.when(there(dr, dc))
        def _():
            pl.semaphore_signal(barrier, inc=1, device_id=(row + dr, col + dc), device_id_type=MESH)

        expected = expected + there(-dr, -dc).astype(jnp.int32)
    for dr in (-1, 1):
        @pl.when(sends_pass(dr))
        def _():
            pl.semaphore_signal(barrier, inc=1, device_id=(row + 2 * dr, col), device_id_type=MESH)

        @pl.when(passes(0, dr))
        def _():
            pl.semaphore_signal(barrier, inc=1, device_id=(row - 2 * dr, col), device_id_type=MESH)

        @pl.when(passes(1, dr))
        def _():
            pl.semaphore_signal(barrier, inc=1, device_id=(row + 2 * dr, col), device_id_type=MESH)

        @pl.when(sends_pass(-dr))
        def _():
            pl.semaphore_signal(barrier, inc=1, device_id=(row - 2 * dr, col), device_id_type=MESH)

        for good in (sends_pass(dr), passes(0, dr), passes(1, dr), sends_pass(-dr)):
            expected = expected + good.astype(jnp.int32)
    pl.semaphore_wait(barrier, expected)

    for kv in range(2):
        loads[kv].wait()
        for hf in range(2):
            for s in range(3):
                send_far(s, 0, kv, hf, ok=~values_last[s] if kv else true)
            if kv == 0 or hf == 0:
                strip_copy(0, kv, hf, OWN).start()

                @pl.when(inner)
                def _():
                    side_copy(0, kv, hf, own_rel).start()

    loads[2].wait()
    loads[3].wait()
    for dc in (-1, 1):
        at = EDGE + (COLS - EDGE if dc == 1 else 0)
        inside = EDGE - 4 if dc == 1 else 0
        for kv in range(2):
            parts = [near[kv, 3 + r, at : at + EDGE, :].astype(jnp.float32)[inside : inside + 4] for r in range(ROWS)]
            edge_out[(dc + 1) // 2, kv] = jnp.concatenate(parts, axis=0).astype(jnp.bfloat16)

    def send_near():
        for n, (dr, dc) in enumerate(sides):
            for kv in range(1 if dc else 2):
                @pl.when(there(dr, dc) if dc else there(dr, dc) & ~crossing(dr))
                def _():
                    near_copy(n, kv).start()

        for dr in (-1, 1):
            @pl.when(sends_pass(dr))
            def _():
                pass_in(0, dr).start()
                pass_in(1, dr).start()

    def pass_near():
        for kv in range(2):
            for dr in (-1, 1):
                @pl.when(passes(kv, dr))
                def _():
                    pltpu.make_async_remote_copy(
                        passing.at[kv], passing.at[kv], pass_send.at[kv], pass_recv.at[kv],
                        device_id=(row - FIRST_LEG[kv] * dr, col), device_id_type=MESH,
                    ).wait_recv()
                    pass_on(kv, dr).start()

    def wait_near():
        for n, (dr, dc) in enumerate(sides):
            @pl.when(there(-dr, -dc))
            def _():
                near_arrival(n, 0).wait_recv()
                if dc == 0:
                    near_arrival(n, 1).wait_recv()
                else:
                    at = 0 if dc == 1 else EDGE + COLS
                    blank = jnp.zeros((EDGE - 4, CH), jnp.float32)
                    for kv in range(2):
                        packed = edge_in[n, kv].astype(jnp.float32)
                        for r in range(ROWS if dr == 0 else 3):
                            four = packed[4 * (row_from[dr] + r) : 4 * (row_from[dr] + r) + 4]
                            full = [blank, four] if dc == 1 else [four, blank]
                            near[kv, row_to[dr] + r, at : at + EDGE, :] = jnp.concatenate(full, axis=0).astype(
                                jnp.bfloat16
                            )

    send_near()

    c0 = col * COLS
    width = n_cols * COLS
    for t in range(TILES):
        q_at = lax.broadcasted_iota(jnp.int32, (TILE, KEYS), 0)
        k_at = lax.broadcasted_iota(jnp.int32, (TILE, KEYS), 1)
        apart = k_at - q_at
        k_col = c0 + TILE * t - STRIP + k_at
        good = ((apart & (STEP - 1)) == 0) & (apart >= 0) & (apart <= 2 * STRIP) & (k_col >= 0) & (k_col < width)
        bias_far[t] = jnp.where(good, 0.0, -jnp.inf)
    for rp in range(2):
        for t in range(TILES):
            shape = (2, TILE, 8, NEAR_KEYS)
            shape = (2 * TILE, 8 * NEAR_KEYS)
            q_id = lax.broadcasted_iota(jnp.int32, shape, 0)
            k_id = lax.broadcasted_iota(jnp.int32, shape, 1)
            r_off = (k_id // NEAR_KEYS) - (q_id // TILE)
            c_off = (k_id % NEAR_KEYS) - (q_id % TILE) - EDGE
            k_row = row * ROWS + 2 * rp - 3 + (k_id // NEAR_KEYS)
            k_col = c0 + TILE * t - EDGE + (k_id % NEAR_KEYS)
            good = (r_off >= 0) & (r_off <= 6) & (c_off >= -3) & (c_off <= 3)
            good = good & (k_row >= 0) & (k_row < n_rows * ROWS) & (k_col >= 0) & (k_col < width)
            bias_near[rp * TILES + t] = jnp.where(good, 0.0, -jnp.inf)

    zero = lambda shape: jnp.zeros(shape, jnp.bfloat16)
    for a in range(SLOTS):
        relayed = (a == 0) & (place == 0) | (a == 6) & (place == 7)
        lost = ((place + a - OWN < 0) | (place + a - OWN > 7)) & ~relayed

        @pl.when(lost)
        def _():
            for kv in range(2):
                for r in range(ROWS):
                    far[kv, a, r] = zero((WIDE, CH))

        @pl.when(~lost & (col == 0))
        def _():
            for kv in range(2):
                for r in range(ROWS):
                    far[kv, a, r, 0:STRIP] = zero((STRIP, CH))

        @pl.when(~lost & (col == 3))
        def _():
            for kv in range(2):
                for r in range(ROWS):
                    far[kv, a, r, STRIP + COLS : WIDE] = zero((STRIP, CH))

        if a in (0, 6):
            @pl.when(relayed & inner)
            def _():
                for kv in range(2):
                    for r in range(ROWS):
                        far[kv, a, r, pl.ds(side_in, STRIP)] = zero((STRIP, CH))

    for kv in range(2):
        @pl.when(row == 0)
        def _():
            near[kv, 0:3] = zero((3, NEAR_WIDE, CH))

        @pl.when(row == n_rows - 1)
        def _():
            near[kv, 7:10] = zero((3, NEAR_WIDE, CH))

        @pl.when(col == 0)
        def _():
            near[kv, :, 0:EDGE] = zero((NEAR_ROWS, EDGE, CH))

        @pl.when(col == n_cols - 1)
        def _():
            near[kv, :, EDGE + COLS : NEAR_WIDE] = zero((NEAR_ROWS, EDGE, CH))

    lane_head = lax.broadcasted_iota(jnp.int32, (1, CH), 1) // HEAD
    head_mask = [(lane_head == h).astype(jnp.float32) for h in range(HEADS)]
    head_mask_narrow = [m.astype(jnp.bfloat16) for m in head_mask]
    dims_t = (((1,), (1,)), ((), ()))
    dims = (((1,), (0,)), ((), ()))

    loads[4].wait()
    loads[5].wait()

    def block_queries(q):
        return jnp.concatenate([q * head_mask_narrow[h] for h in range(HEADS)], axis=0)

    @pl.loop(0, ROWS, unroll=2)
    def _(r):
        for t in range(TILES):
            qb[r * TILES + t] = block_queries(qf[r, TILE * t : TILE * (t + 1), :])

    half_tiles = (jnp.where(col < 2, 0, 2), jnp.where(col < 2, 2, 0))

    def score_blocks(hf, slots, part, first=False):
        row_bias = []
        for slot in slots:
            ok = (place + slot - OWN >= 0) & (place + slot - OWN <= 7)
            row_bias.append(jnp.where(ok, 0.0, -jnp.inf).astype(jnp.float32))

        @pl.loop(hf * HALF, hf * HALF + HALF, unroll=True)
        def _(r):
            for tt in range(2):
                t = half_tiles[part] + tt
                idx = r * TILES + t
                where = pl.ds(pl.multiple_of(TILE * t, TILE), KEYS)
                top = None if first else peak[idx]
                for n in range(0, len(slots), 2):
                    pair = slots[n : n + 2]
                    k = jnp.concatenate([far[0, slot, r, where, :] for slot in pair], axis=0)
                    both = lax.dot_general(qb[idx], k, dims_t, preferred_element_type=jnp.float32) * SCALE
                    for m, slot in enumerate(pair):
                        b = bias_far[t] + row_bias[n + m]
                        s = both[:, m * KEYS : (m + 1) * KEYS].reshape(HEADS, TILE, KEYS) + b[None]
                        s = s.reshape(HEADS * TILE, KEYS)
                        scores[slot, idx] = s
                        top = s if top is None else jnp.maximum(top, s)
                peak[idx] = top

    def value_sum(idx, r, t, slots, o):
        where = pl.ds(pl.multiple_of(TILE * t, TILE), KEYS)
        for n in range(0, len(slots), 2):
            pair = slots[n : n + 2]
            p = jnp.concatenate([probs[slot, idx] for slot in pair], axis=1)
            v = jnp.concatenate([far[1, slot, r, where, :] for slot in pair], axis=0)
            d = lax.dot_general(p, v, dims, preferred_element_type=jnp.float32)
            o = d if o is None else o + d
        return o

    from_stream = [pick(FROM_STREAM[s], place) for s in range(3)]
    after_first = [pick(FROM_SECOND[s], place) == 0 for s in range(3)]
    needs_second = [jnp.bool_(False)] * 3
    for s in range(3):
        for d in range(3):
            needs_second[d] = needs_second[d] | (second_send[s] & ~after_first[s] & (from_stream[s] == d))

    first_slots = (jnp.int32(1), jnp.int32(5), OWN + hop)
    second_slots = (jnp.int32(0), jnp.int32(6), OWN - hop)
    own = jnp.int32(OWN)

    def later_sides(kv, hf):
        for o in range(2):
            for s in range(3):
                if (s, o) != (2, 0):
                    wait_side(event(s, o), kv, hf, mate_ok[o][s], mate_rel[o][s])
        wait_extra(kv, hf)

    for hf in range(2):
        for s in range(3):
            wait_far(s, 0, 0, hf)
        for s in range(3):
            send_far(s, 1, 0, hf, ok=after_first[s])
        for s in range(3):
            send_strips(s, 0, 0, hf)
    for hf in range(2):
        wait_strip_at(0, 0, hf, OWN)
        for s in range(3):
            wait_strip(s, 0, 0, hf)
        score_blocks(hf, (own,) + first_slots, 0, first=True)
    for hf in range(2):
        wait_side(0, 0, hf, true, own_rel)
        wait_side(event(2, 0), 0, hf, mate_ok[0][2], mate_rel[0][2])
        score_blocks(hf, (own, first_slots[2]), 1, first=True)

    for hf in range(2):
        for s in range(3):
            wait_far(s, 0, 1, hf, ok=~late_in[s])
        for s in range(3):
            send_far(s, 1, 1, hf, ok=after_first[s])
        if hf == 1:
            for h in range(2):
                for s in range(3):
                    send_far(s, 0, 1, h, ok=values_last[s])
        for s in range(3):
            wait_far(s, 1, 0, hf, ok=needs_second[s])
        for s in range(3):
            send_far(s, 1, 0, hf, ok=~after_first[s])
        for s in range(3):
            send_strips(s, 0, 1, hf, ok=~late_in[s])

    def near_layer(rp):
        @pl.loop(0, TILES, unroll=True)
        def _(t):
            cols = pl.ds(pl.multiple_of(TILE * t, TILE), TILE)
            keys = pl.ds(pl.multiple_of(TILE * t, TILE), NEAR_KEYS)
            q = qn[pl.ds(2 * rp, 2), cols, :].reshape(2 * TILE, CH)
            k = near[0, pl.ds(2 * rp, 8), keys, :].reshape(8 * NEAR_KEYS, CH)
            v = near[1, pl.ds(2 * rp, 8), keys, :].reshape(8 * NEAR_KEYS, CH)
            s = lax.dot_general(block_queries(q), k, dims_t, preferred_element_type=jnp.float32) * SCALE
            s = s.reshape(HEADS, 2 * TILE, 8 * NEAR_KEYS) + bias_near[rp * TILES + t][None]
            s = s.reshape(HEADS * 2 * TILE, 8 * NEAR_KEYS)
            p = jnp.exp2(s - jnp.max(s, axis=1, keepdims=True))
            inverse = 1.0 / jnp.sum(p, axis=1, keepdims=True)
            o = lax.dot_general(p.astype(jnp.bfloat16), v, dims, preferred_element_type=jnp.float32) * inverse
            out = None
            for h in range(HEADS):
                part = o[h * 2 * TILE : (h + 1) * 2 * TILE] * head_mask[h]
                out = part if out is None else out + part
            out_near[pl.ds(2 * rp, 2), cols, :] = out.astype(jnp.bfloat16).reshape(2, TILE, CH)

    def relay_second_values(hf):
        for s in range(3):
            wait_far(s, 1, 1, hf, ok=needs_second[s])
        for s in range(3):
            send_far(s, 1, 1, hf, ok=~after_first[s])

    for hf in range(2):
        relay_second_values(hf)
        for s in range(3):
            wait_far(s, 1, 0, hf, ok=~needs_second[s])
        for s in range(3):
            send_strips(s, 1, 0, hf)
        if hf == 0:
            pass_near()
    for hf in range(2):
        for s in range(3):
            wait_strip(s, 1, 0, hf)
        score_blocks(hf, second_slots, 0)

    def last_values(hf):
        for s in range(2):
            wait_far(s, 0, 1, hf, ok=late_in[s])
        for s in range(2):
            send_strips(s, 0, 1, hf, ok=late_in[s])
        for s in range(3):
            wait_far(s, 1, 1, hf, ok=~needs_second[s])
        for s in range(3):
            send_strips(s, 1, 1, hf)

    later_sides(0, 0)
    later_sides(0, 1)
    last_values(0)
    for hf in range(2):
        score_blocks(hf, first_slots[:2] + second_slots, 1)

    @pl.loop(0, ROWS, unroll=2)
    def _(r):
        for t in range(TILES):
            idx = r * TILES + t
            m = jnp.max(peak[idx], axis=1, keepdims=True)
            summed = None
            for a in range(SLOTS):
                p = jnp.exp2(scores[a, idx] - m)
                probs[a, idx] = p.astype(jnp.bfloat16)
                summed = p if summed is None else summed + p
            total[idx] = jnp.broadcast_to(1.0 / jnp.sum(summed, axis=1, keepdims=True), (HEADS * TILE, 128))

    wait_strip_at(0, 1, 0, OWN)
    wait_strip(2, 0, 1, 0)
    wait_side(0, 1, 0, true, own_rel)
    wait_side(event(2, 0), 1, 0, mate_ok[0][2], mate_rel[0][2])

    @pl.loop(0, ROWS, unroll=2)
    def _(r):
        for t in range(TILES):
            idx = r * TILES + t
            acc[idx] = value_sum(idx, r, t, (own, first_slots[2]), None)

    last_values(1)
    wait_near()
    near_layer(0)
    near_layer(1)
    near_out = pltpu.make_async_copy(out_near, on_ref, out_sem.at[0])
    near_out.start()
    for s in range(2):
        wait_strip(s, 0, 1, 0)
    for s in range(3):
        wait_strip(s, 1, 1, 0)
    later_sides(1, 0)

    @pl.loop(0, ROWS, unroll=2)
    def _(r):
        for t in range(TILES):
            idx = r * TILES + t
            o = value_sum(idx, r, t, first_slots[:2] + second_slots, acc[idx])
            out = None
            for h in range(HEADS):
                part = slice(h * TILE, (h + 1) * TILE)
                inverse = total[idx, part, :]
                one = o[part, :] * jnp.concatenate([inverse, inverse], axis=1) * head_mask[h]
                out = one if out is None else out + one
            out_far[r, TILE * t : TILE * (t + 1), :] = out.astype(jnp.bfloat16)

    far_out = pltpu.make_async_copy(out_far, of_ref, out_sem.at[1])
    far_out.start()

    for kv in range(2):
        for hf in range(2):
            if kv == 0 or hf == 0:
                strip_copy(0, kv, hf, OWN).wait_send()

                @pl.when(inner)
                def _():
                    side_copy(0, kv, hf, own_rel).wait_send()

                for s in range(2):
                    @pl.when(extra_ok[s])
                    def _():
                        extra_copy(s, kv, hf).wait_send()

            for o in range(2):
                for s in range(3):
                    @pl.when(send_ok[o][s])
                    def _():
                        far_copy(s, o, kv, hf).wait_send()

                    if kv == 0 or hf == 0:
                        @pl.when(recv_ok[o][s])
                        def _():
                            strip_copy(event(s, o), kv, hf, in_slot[o][s]).wait_send()

                        @pl.when(side_ok(recv_ok[o][s], recv_rel[o][s] - hop))
                        def _():
                            side_copy(event(s, o), kv, hf, recv_rel[o][s]).wait_send()

    for n, (dr, dc) in enumerate(sides):
        for kv in range(1 if dc else 2):
            @pl.when(there(dr, dc) if dc else there(dr, dc) & ~crossing(dr))
            def _():
                near_copy(n, kv).wait_send()

    for kv in range(2):
        for dr in (-1, 1):
            @pl.when(sends_pass(dr))
            def _():
                pass_in(kv, dr).wait_send()

            @pl.when(passes(kv, dr))
            def _():
                pass_on(kv, dr).wait_send()

    near_out.wait()
    far_out.wait()


def per_device(query_near, key_near, value_near, dilated_queries, dilated_keys, dilated_values):
    block = jax.ShapeDtypeStruct((ROWS, COLS, CH), jnp.bfloat16)
    tiles = ROWS * TILES
    dma = pltpu.SemaphoreType.DMA
    anywhere = pl.BlockSpec(memory_space=pl.ANY)
    return pl.pallas_call(
        kernel,
        out_shape=(block, block),
        in_specs=[pl.BlockSpec(memory_space=pltpu.HBM)] * 6,
        out_specs=(anywhere, anywhere),
        scratch_shapes=[
            pltpu.VMEM((2, SLOTS, ROWS, WIDE, CH), jnp.bfloat16),
            pltpu.VMEM((2, NEAR_ROWS, NEAR_WIDE, CH), jnp.bfloat16),
            pltpu.VMEM((ROWS, COLS, CH), jnp.bfloat16),
            pltpu.VMEM((ROWS, COLS, CH), jnp.bfloat16),
            pltpu.VMEM((tiles, HEADS * TILE, CH), jnp.bfloat16),
            pltpu.VMEM((SLOTS, tiles, HEADS * TILE, KEYS), jnp.float32),
            pltpu.VMEM((tiles, HEADS * TILE, KEYS), jnp.float32),
            pltpu.VMEM((SLOTS, tiles, HEADS * TILE, KEYS), jnp.bfloat16),
            pltpu.VMEM((tiles, HEADS * TILE, 128), jnp.float32),
            pltpu.VMEM((tiles, HEADS * TILE, CH), jnp.float32),
            pltpu.VMEM((TILES, TILE, KEYS), jnp.float32),
            pltpu.VMEM((2 * TILES, 2 * TILE, 8 * NEAR_KEYS), jnp.float32),
            pltpu.VMEM((2, 2, 4 * ROWS, CH), jnp.bfloat16),
            pltpu.VMEM((9, 2, 4 * ROWS, CH), jnp.bfloat16),
            pltpu.VMEM((2, 3, COLS, CH), jnp.bfloat16),
            pltpu.VMEM((ROWS, COLS, CH), jnp.bfloat16),
            pltpu.VMEM((ROWS, COLS, CH), jnp.bfloat16),
            dma((6,)),
            dma((3, 2, 2, 2)),
            dma((3, 2, 2, 2)),
            dma((7, 2, 2)),
            dma((7, 2, 2)),
            dma((7, 2, 2)),
            dma((7, 2, 2)),
            dma((2, 2)),
            dma((2, 2)),
            dma((8, 2)),
            dma((8, 2)),
            dma((2,)),
            dma((2,)),
            dma((2,)),
        ],
        compiler_params=pltpu.CompilerParams(
            collective_id=0, has_side_effects=True, vmem_limit_bytes=56 << 20
        ),
        name="two_layers",
    )(query_near, key_near, value_near, dilated_queries, dilated_keys, dilated_values)


def solution(mesh):
    placed = (P("row", "col", None),) * 6
    return jax.shard_map(
        per_device,
        mesh=mesh,
        in_specs=placed,
        out_specs=(P("row", "col", None), P("row", "col", None)),
        check_vma=False,
    )
```

```python
import functools
import math

import jax
import jax.numpy as jnp
from jax import lax
from jax.experimental import pallas as pl
from jax.experimental.pallas import tpu as pltpu
from jax.sharding import PartitionSpec as P

MESH = pl.DeviceIdType.MESH
HEADS = 4
HEAD = 64
CH = 256
ROWS = 4
COLS = 128
STRIP = 48
WIDE = COLS + 2 * STRIP
STEP = 16
SLOTS = 7
OWN = 3
EDGE = 16
NEAR_WIDE = COLS + 2 * EDGE
NEAR_ROWS = ROWS + 6
TILE = 32
TILES = COLS // TILE
KEYS = TILE + 2 * STRIP
NEAR_KEYS = TILE + 2 * EDGE
SCALE = math.log2(math.e) / math.sqrt(HEAD)
NONE = 99

SECOND = (
    (1, -1, -1, NONE, 1, NONE, -2, NONE),
    (NONE, 2, NONE, -1, NONE, 1, 1, -1),
    (4, 2, 2, 2, -2, -2, -2, -4),
)
FROM_STREAM = ((2, 2, 0, 0, 2, 0, 0, 0), (0, 1, 0, 2, 0, 1, 2, 2), (0, 1, 1, 1, 0, 0, 0, 1))
FROM_SECOND = ((0, 0, 1, 0, 0, 0, 0, 0), (0, 0, 0, 0, 0, 1, 0, 0), (1, 0, 0, 0, 0, 0, 0, 1))
VALUES_LAST = ((0,), (7,), ())


def pick(table, place):
    out = jnp.int32(table[0])
    for k in range(1, len(table)):
        out = jnp.where(place == k, jnp.int32(table[k]), out)
    return out


def one_of(place, places):
    out = jnp.bool_(False)
    for k in places:
        out = out | (place == k)
    return out


def kernel(
    qn_ref, kn_ref, vn_ref, qf_ref, kf_ref, vf_ref, on_ref, of_ref,
    far, near, qn, qf, qb, scores, peak, probs, total, acc, bias_far, bias_near, edge_out, edge_in, passing, out_near, out_far,
    load_sem, far_send, far_recv, strip_send, strip_recv, side_send, side_recv, extra_send, extra_recv, near_send, near_recv, pass_send, pass_recv, out_sem,
):
    row = lax.axis_index("row")
    col = lax.axis_index("col")
    n_rows = lax.axis_size("row")
    n_cols = lax.axis_size("col")
    x = row // 8
    z = (row // 4) % 2
    y = row % 4
    core = col % 2
    place = 2 * x + z
    inner = (col == 1) | (col == 2)
    true = jnp.bool_(True)

    loads = [
        pltpu.make_async_copy(kf_ref, far.at[0, OWN, :, pl.ds(STRIP, COLS)], load_sem.at[0]),
        pltpu.make_async_copy(vf_ref, far.at[1, OWN, :, pl.ds(STRIP, COLS)], load_sem.at[1]),
        pltpu.make_async_copy(kn_ref, near.at[0, pl.ds(3, ROWS), pl.ds(EDGE, COLS)], load_sem.at[2]),
        pltpu.make_async_copy(vn_ref, near.at[1, pl.ds(3, ROWS), pl.ds(EDGE, COLS)], load_sem.at[3]),
        pltpu.make_async_copy(qf_ref, qf, load_sem.at[4]),
        pltpu.make_async_copy(qn_ref, qn, load_sem.at[5]),
    ]
    for load in loads:
        load.start()

    to_row = ((row + 8) % n_rows, (row + n_rows - 8) % n_rows, row + 4 - 8 * z)
    hop = 1 - 2 * z

    def arrivals(at, hop):
        first_ok = (at >= 2, at < 6, true)
        back = (-2, 2, hop)
        sent = [pick(SECOND[s], (at + back[s] + 8) % 8) for s in range(3)]
        second_ok = [sent[s] != NONE for s in range(3)]
        ring = (jnp.where(at < 2, 8, 0), jnp.where(at >= 6, -8, 0), 0)
        return (first_ok, second_ok), (back, [sent[s] + back[s] + ring[s] for s in range(3)])

    def slot_of(rel):
        return (rel + 10) % 7

    recv_ok, recv_rel = arrivals(place, hop)
    mate_ok, mate_rel = arrivals(place + hop, -hop)
    in_slot = [[slot_of(jnp.int32(rel)) for rel in rels] for rels in recv_rel]
    second_rel = [pick(SECOND[s], place) for s in range(3)]
    second_send = [second_rel[s] != NONE for s in range(3)]
    send_ok = ((x < 3, x > 0, true), second_send)
    shift = (-2, 2, -hop)
    ring = (jnp.where(place >= 6, 8, 0), jnp.where(place < 2, -8, 0), 0)
    src_slot = ([jnp.int32(OWN)] * 3, [slot_of(second_rel[s]) for s in range(3)])
    dst_slot = ([slot_of(jnp.int32(shift[s])) for s in range(3)], [slot_of(second_rel[s] + shift[s] + ring[s]) for s in range(3)])
    values_last = [one_of(place, VALUES_LAST[s]) for s in range(3)]
    late_in = [recv_ok[0][s] & one_of(place + (-2, 2, hop)[s], VALUES_LAST[s]) for s in range(3)]

    def piece(hf):
        offset = jnp.where(col < 2, (COLS, STRIP)[hf], (STRIP, 2 * STRIP)[hf])
        return pl.ds(0, ROWS), pl.ds(pl.multiple_of(offset, 16), (STRIP, COLS - STRIP)[hf])

    def far_copy(s, o, kv, hf):
        return pltpu.make_async_remote_copy(
            far.at[kv, src_slot[o][s], *piece(hf)],
            far.at[kv, dst_slot[o][s], *piece(hf)],
            far_send.at[s, o, kv, hf],
            far_recv.at[s, o, kv, hf],
            device_id=(to_row[s], col),
            device_id_type=MESH,
        )

    def send_far(s, o, kv, hf, ok=true):
        @pl.when(send_ok[o][s] & ok)
        def _():
            far_copy(s, o, kv, hf).start()

    def wait_far(s, o, kv, hf, ok=true):
        @pl.when(recv_ok[o][s] & ok)
        def _():
            block = far.at[kv, in_slot[o][s], *piece(hf)]
            pltpu.make_async_remote_copy(
                block, block, far_send.at[s, o, kv, hf], far_recv.at[s, o, kv, hf],
                device_id=(to_row[s], col), device_id_type=MESH,
            ).wait_recv()

    mate = col + 1 - 2 * core
    strip_src = pl.multiple_of(jnp.where(core == 0, COLS, STRIP), 16)
    strip_dst = pl.multiple_of(jnp.where(core == 0, 0, STRIP + COLS), 16)
    strip_in = pl.multiple_of(jnp.where(core == 0, STRIP + COLS, 0), 16)

    def strip_copy(e, kv, slot):
        return pltpu.make_async_remote_copy(
            far.at[kv, slot, :, pl.ds(strip_src, STRIP)],
            far.at[kv, slot, :, pl.ds(strip_dst, STRIP)],
            strip_send.at[e, kv],
            strip_recv.at[e, kv],
            device_id=(row, mate),
            device_id_type=MESH,
        )

    def wait_strip_at(e, kv, slot):
        block = far.at[kv, slot, :, pl.ds(strip_in, STRIP)]
        pltpu.make_async_remote_copy(
            block, block, strip_send.at[e, kv], strip_recv.at[e, kv],
            device_id=(row, mate), device_id_type=MESH,
        ).wait_recv()

    def event(s, o):
        return 1 + 3 * o + s

    side_src = pl.multiple_of(jnp.where(col == 1, COLS, STRIP), 16)
    side_dst = pl.multiple_of(jnp.where(col == 1, 0, STRIP + COLS), 16)
    side_in = pl.multiple_of(jnp.where(col == 1, STRIP + COLS, 0), 16)

    def side_ok(ok, rel):
        return inner & ok & (rel >= -3) & (rel <= 3)

    def side_copy(e, kv, rel):
        return pltpu.make_async_remote_copy(
            far.at[kv, slot_of(rel), :, pl.ds(side_src, STRIP)],
            far.at[kv, OWN + rel - hop, :, pl.ds(side_dst, STRIP)],
            side_send.at[e, kv],
            side_recv.at[e, kv],
            device_id=(to_row[2], 3 - col),
            device_id_type=MESH,
        )

    def wait_side(e, kv, ok, rel):
        @pl.when(side_ok(ok, rel + hop))
        def _():
            block = far.at[kv, OWN + rel + hop, :, pl.ds(side_in, STRIP)]
            pltpu.make_async_remote_copy(
                block, block, side_send.at[e, kv], side_recv.at[e, kv],
                device_id=(to_row[2], 3 - col), device_id_type=MESH,
            ).wait_recv()

    own_rel = jnp.int32(0)
    extra_ok = (inner & (place == 3), inner & (place == 4))
    extra_from = (1, 5)
    extra_to = (0, 6)
    extra_row = (row + 4, row - 4)

    def extra_copy(s, kv):
        return pltpu.make_async_remote_copy(
            far.at[kv, extra_from[s], :, pl.ds(side_src, STRIP)],
            far.at[kv, extra_to[s], :, pl.ds(side_dst, STRIP)],
            extra_send.at[kv],
            extra_recv.at[kv],
            device_id=(extra_row[s], 3 - col),
            device_id_type=MESH,
        )

    def wait_extra(kv):
        for s in range(2):
            @pl.when(extra_ok[s])
            def _():
                block = far.at[kv, extra_to[1 - s], :, pl.ds(side_in, STRIP)]
                pltpu.make_async_remote_copy(
                    block, block, extra_send.at[kv], extra_recv.at[kv],
                    device_id=(extra_row[s], 3 - col), device_id_type=MESH,
                ).wait_recv()

    def send_strips(s, o, kv, hf, ok=true):
        ok = recv_ok[o][s] & ok
        rel = recv_rel[o][s]
        e = event(s, o)

        @pl.when(ok & (inner if hf else ~inner))
        def _():
            strip_copy(e, kv, in_slot[o][s]).start()

        if hf == 0:
            @pl.when(side_ok(ok, rel - hop))
            def _():
                side_copy(e, kv, rel).start()

            if o == 0 and s < 2:
                @pl.when(extra_ok[s] & ok)
                def _():
                    extra_copy(s, kv).start()

    def wait_strip(s, o, kv):
        @pl.when(recv_ok[o][s])
        def _():
            wait_strip_at(event(s, o), kv, in_slot[o][s])

    sides = [(dr, dc) for dr in (-1, 0, 1) for dc in (-1, 0, 1) if (dr, dc) != (0, 0)]

    def there(dr, dc):
        good = true
        if dr:
            good = good & ((row + dr >= 0) & (row + dr < n_rows))
        if dc:
            good = good & ((col + dc >= 0) & (col + dc < n_cols))
        return good

    row_src = {1: (4, 3), -1: (3, 3)}
    row_dst = {1: (0, 3), -1: (7, 3)}
    row_from = {1: 1, 0: 0, -1: 0}
    row_to = {1: 0, 0: 3, -1: 7}
    main = pl.ds(EDGE, COLS)

    def crossing(dr):
        return {0: jnp.bool_(False), 1: y == 3, -1: y == 0}[dr]

    FIRST_LEG = (2, -1)
    LAST_LEG = (-1, 2)

    def sends_pass(dr):
        return crossing(dr) & there(dr, 0)

    def passes(kv, dr):
        at = {(0, 1): 1, (0, -1): 2, (1, 1): 2, (1, -1): 1}[kv, dr]
        back, on = row - FIRST_LEG[kv] * dr, row + LAST_LEG[kv] * dr
        return (y == at) & (back >= 0) & (back < n_rows) & (on >= 0) & (on < n_rows)

    def pass_in(kv, dr):
        return pltpu.make_async_remote_copy(
            near.at[kv, pl.ds(*row_src[dr]), main],
            passing.at[kv],
            pass_send.at[kv],
            pass_recv.at[kv],
            device_id=(row + FIRST_LEG[kv] * dr, col),
            device_id_type=MESH,
        )

    def pass_on(kv, dr):
        n = sides.index((dr, 0))
        return pltpu.make_async_remote_copy(
            passing.at[kv],
            near.at[kv, pl.ds(*row_dst[dr]), main],
            pass_send.at[kv],
            near_recv.at[n, kv],
            device_id=(row + LAST_LEG[kv] * dr, col),
            device_id_type=MESH,
        )

    def near_copy(n, kv):
        dr, dc = sides[n]
        if dc:
            src, dst = edge_out.at[(dc + 1) // 2], edge_in.at[n]
        else:
            src, dst = near.at[kv, pl.ds(*row_src[dr]), main], near.at[kv, pl.ds(*row_dst[dr]), main]
        return pltpu.make_async_remote_copy(
            src, dst, near_send.at[n, kv], near_recv.at[n, kv], device_id=(row + dr, col + dc), device_id_type=MESH
        )

    def near_arrival(n, kv):
        dr, dc = sides[n]
        block = edge_in.at[n] if dc else near.at[kv, pl.ds(*row_dst[dr]), main]
        return pltpu.make_async_remote_copy(
            block, block, near_send.at[n, kv], near_recv.at[n, kv],
            device_id=(row - dr, col - dc), device_id_type=MESH,
        )

    barrier = pltpu.get_barrier_semaphore()
    expected = jnp.int32(0)
    for s in range(3):
        @pl.when(send_ok[0][s])
        def _():
            pl.semaphore_signal(barrier, inc=1, device_id=(to_row[s], col), device_id_type=MESH)

        expected = expected + recv_ok[0][s].astype(jnp.int32)

    for s, places in ((0, (6, 7)), (1, (0, 1))):
        @pl.when(one_of(place, places))
        def _():
            pl.semaphore_signal(barrier, inc=1, device_id=(to_row[s], col), device_id_type=MESH)

        expected = expected + one_of(place, places).astype(jnp.int32)

    @pl.when(inner)
    def _():
        pl.semaphore_signal(barrier, inc=1, device_id=(to_row[2], 3 - col), device_id_type=MESH)

    expected = expected + inner.astype(jnp.int32)
    for s in range(2):
        @pl.when(extra_ok[s])
        def _():
            pl.semaphore_signal(barrier, inc=1, device_id=(extra_row[s], 3 - col), device_id_type=MESH)

        expected = expected + extra_ok[s].astype(jnp.int32)
    for dr, dc in sides:
        @pl.when(there(dr, dc))
        def _():
            pl.semaphore_signal(barrier, inc=1, device_id=(row + dr, col + dc), device_id_type=MESH)

        expected = expected + there(-dr, -dc).astype(jnp.int32)
    for dr in (-1, 1):
        @pl.when(sends_pass(dr))
        def _():
            pl.semaphore_signal(barrier, inc=1, device_id=(row + 2 * dr, col), device_id_type=MESH)

        @pl.when(passes(0, dr))
        def _():
            pl.semaphore_signal(barrier, inc=1, device_id=(row - 2 * dr, col), device_id_type=MESH)

        @pl.when(passes(1, dr))
        def _():
            pl.semaphore_signal(barrier, inc=1, device_id=(row + 2 * dr, col), device_id_type=MESH)

        @pl.when(sends_pass(-dr))
        def _():
            pl.semaphore_signal(barrier, inc=1, device_id=(row - 2 * dr, col), device_id_type=MESH)

        for good in (sends_pass(dr), passes(0, dr), passes(1, dr), sends_pass(-dr)):
            expected = expected + good.astype(jnp.int32)
    pl.semaphore_wait(barrier, expected)

    for hf in range(2):
        for kv in range(2):
            if hf == 0:
                loads[kv].wait()
            for s in range(3):
                send_far(s, 0, kv, hf, ok=~values_last[s] if (kv and hf) else true)
            if hf == 0:
                strip_copy(0, kv, OWN).start()

                @pl.when(inner)
                def _():
                    side_copy(0, kv, own_rel).start()

    loads[2].wait()
    loads[3].wait()
    for dc in (-1, 1):
        at = EDGE + (COLS - EDGE if dc == 1 else 0)
        inside = EDGE - 4 if dc == 1 else 0
        for kv in range(2):
            parts = [near[kv, 3 + r, at : at + EDGE, :].astype(jnp.float32)[inside : inside + 4] for r in range(ROWS)]
            edge_out[(dc + 1) // 2, kv] = jnp.concatenate(parts, axis=0).astype(jnp.bfloat16)

    def send_near():
        for n, (dr, dc) in enumerate(sides):
            for kv in range(1 if dc else 2):
                @pl.when(there(dr, dc) if dc else there(dr, dc) & ~crossing(dr))
                def _():
                    near_copy(n, kv).start()

        for dr in (-1, 1):
            @pl.when(sends_pass(dr))
            def _():
                pass_in(0, dr).start()
                pass_in(1, dr).start()

    def pass_near():
        for kv in range(2):
            for dr in (-1, 1):
                @pl.when(passes(kv, dr))
                def _():
                    pltpu.make_async_remote_copy(
                        passing.at[kv], passing.at[kv], pass_send.at[kv], pass_recv.at[kv],
                        device_id=(row - FIRST_LEG[kv] * dr, col), device_id_type=MESH,
                    ).wait_recv()
                    pass_on(kv, dr).start()

    def wait_near():
        for n, (dr, dc) in enumerate(sides):
            @pl.when(there(-dr, -dc))
            def _():
                near_arrival(n, 0).wait_recv()
                if dc == 0:
                    near_arrival(n, 1).wait_recv()
                else:
                    at = 0 if dc == 1 else EDGE + COLS
                    blank = jnp.zeros((EDGE - 4, CH), jnp.float32)
                    for kv in range(2):
                        packed = edge_in[n, kv].astype(jnp.float32)
                        for r in range(ROWS if dr == 0 else 3):
                            four = packed[4 * (row_from[dr] + r) : 4 * (row_from[dr] + r) + 4]
                            full = [blank, four] if dc == 1 else [four, blank]
                            near[kv, row_to[dr] + r, at : at + EDGE, :] = jnp.concatenate(full, axis=0).astype(
                                jnp.bfloat16
                            )

    send_near()

    c0 = col * COLS
    width = n_cols * COLS
    for t in range(TILES):
        q_at = lax.broadcasted_iota(jnp.int32, (TILE, KEYS), 0)
        k_at = lax.broadcasted_iota(jnp.int32, (TILE, KEYS), 1)
        apart = k_at - q_at
        k_col = c0 + TILE * t - STRIP + k_at
        good = ((apart & (STEP - 1)) == 0) & (apart >= 0) & (apart <= 2 * STRIP) & (k_col >= 0) & (k_col < width)
        bias_far[t] = jnp.where(good, 0.0, -jnp.inf)
    for rp in range(2):
        for t in range(TILES):
            shape = (2, TILE, 8, NEAR_KEYS)
            shape = (2 * TILE, 8 * NEAR_KEYS)
            q_id = lax.broadcasted_iota(jnp.int32, shape, 0)
            k_id = lax.broadcasted_iota(jnp.int32, shape, 1)
            r_off = (k_id // NEAR_KEYS) - (q_id // TILE)
            c_off = (k_id % NEAR_KEYS) - (q_id % TILE) - EDGE
            k_row = row * ROWS + 2 * rp - 3 + (k_id // NEAR_KEYS)
            k_col = c0 + TILE * t - EDGE + (k_id % NEAR_KEYS)
            good = (r_off >= 0) & (r_off <= 6) & (c_off >= -3) & (c_off <= 3)
            good = good & (k_row >= 0) & (k_row < n_rows * ROWS) & (k_col >= 0) & (k_col < width)
            bias_near[rp * TILES + t] = jnp.where(good, 0.0, -jnp.inf)

    zero = lambda shape: jnp.zeros(shape, jnp.bfloat16)
    for a in range(SLOTS):
        relayed = (a == 0) & (place == 0) | (a == 6) & (place == 7)
        lost = ((place + a - OWN < 0) | (place + a - OWN > 7)) & ~relayed

        @pl.when(lost)
        def _():
            for kv in range(2):
                for r in range(ROWS):
                    far[kv, a, r] = zero((WIDE, CH))

        @pl.when(~lost & (col == 0))
        def _():
            for kv in range(2):
                for r in range(ROWS):
                    far[kv, a, r, 0:STRIP] = zero((STRIP, CH))

        @pl.when(~lost & (col == 3))
        def _():
            for kv in range(2):
                for r in range(ROWS):
                    far[kv, a, r, STRIP + COLS : WIDE] = zero((STRIP, CH))

        if a in (0, 6):
            @pl.when(relayed & inner)
            def _():
                for kv in range(2):
                    for r in range(ROWS):
                        far[kv, a, r, pl.ds(side_in, STRIP)] = zero((STRIP, CH))

    for kv in range(2):
        @pl.when(row == 0)
        def _():
            near[kv, 0:3] = zero((3, NEAR_WIDE, CH))

        @pl.when(row == n_rows - 1)
        def _():
            near[kv, 7:10] = zero((3, NEAR_WIDE, CH))

        @pl.when(col == 0)
        def _():
            near[kv, :, 0:EDGE] = zero((NEAR_ROWS, EDGE, CH))

        @pl.when(col == n_cols - 1)
        def _():
            near[kv, :, EDGE + COLS : NEAR_WIDE] = zero((NEAR_ROWS, EDGE, CH))

    lane_head = lax.broadcasted_iota(jnp.int32, (1, CH), 1) // HEAD
    head_mask = [(lane_head == h).astype(jnp.float32) for h in range(HEADS)]
    head_mask_narrow = [m.astype(jnp.bfloat16) for m in head_mask]
    dims_t = (((1,), (1,)), ((), ()))
    dims = (((1,), (0,)), ((), ()))

    loads[4].wait()
    loads[5].wait()

    def block_queries(q):
        return jnp.concatenate([q * head_mask_narrow[h] for h in range(HEADS)], axis=0)

    @pl.loop(0, ROWS, unroll=2)
    def _(r):
        for t in range(TILES):
            qb[r * TILES + t] = block_queries(qf[r, TILE * t : TILE * (t + 1), :])

    half_tiles = (jnp.where(col < 2, 0, 2), jnp.where(col < 2, 2, 0))

    def score_blocks(slots, part, first=False):
        row_bias = []
        for slot in slots:
            ok = (place + slot - OWN >= 0) & (place + slot - OWN <= 7)
            row_bias.append(jnp.where(ok, 0.0, -jnp.inf).astype(jnp.float32))

        @pl.loop(0, ROWS, unroll=2)
        def _(r):
            for tt in range(2):
                t = half_tiles[part] + tt
                idx = r * TILES + t
                where = pl.ds(pl.multiple_of(TILE * t, TILE), KEYS)
                top = None if first else peak[idx]
                for n in range(0, len(slots), 2):
                    pair = slots[n : n + 2]
                    k = jnp.concatenate([far[0, slot, r, where, :] for slot in pair], axis=0)
                    both = lax.dot_general(qb[idx], k, dims_t, preferred_element_type=jnp.float32) * SCALE
                    for m, slot in enumerate(pair):
                        b = bias_far[t] + row_bias[n + m]
                        s = both[:, m * KEYS : (m + 1) * KEYS].reshape(HEADS, TILE, KEYS) + b[None]
                        s = s.reshape(HEADS * TILE, KEYS)
                        scores[slot, idx] = s
                        top = s if top is None else jnp.maximum(top, s)
                peak[idx] = top

    def value_sum(idx, r, t, slots, o):
        where = pl.ds(pl.multiple_of(TILE * t, TILE), KEYS)
        for n in range(0, len(slots), 2):
            pair = slots[n : n + 2]
            p = jnp.concatenate([probs[slot, idx] for slot in pair], axis=1)
            v = jnp.concatenate([far[1, slot, r, where, :] for slot in pair], axis=0)
            d = lax.dot_general(p, v, dims, preferred_element_type=jnp.float32)
            o = d if o is None else o + d
        return o

    from_stream = [pick(FROM_STREAM[s], place) for s in range(3)]
    after_first = [pick(FROM_SECOND[s], place) == 0 for s in range(3)]
    needs_second = [jnp.bool_(False)] * 3
    for s in range(3):
        for d in range(3):
            needs_second[d] = needs_second[d] | (second_send[s] & ~after_first[s] & (from_stream[s] == d))

    first_slots = (jnp.int32(1), jnp.int32(5), OWN + hop)
    second_slots = (jnp.int32(0), jnp.int32(6), OWN - hop)
    own = jnp.int32(OWN)

    def later_sides(kv):
        for o in range(2):
            for s in range(3):
                if (s, o) != (2, 0):
                    wait_side(event(s, o), kv, mate_ok[o][s], mate_rel[o][s])
        wait_extra(kv)

    def first_arrivals(kv, hf):
        late = kv == 1 and hf == 1
        for s in range(3):
            wait_far(s, 0, kv, hf, ok=~late_in[s] if late else true)
        for s in range(3):
            send_far(s, 1, kv, hf, ok=after_first[s])
        if late:
            for s in range(3):
                send_far(s, 0, kv, hf, ok=values_last[s])
        for s in range(3):
            send_strips(s, 0, kv, hf, ok=~late_in[s] if late else true)

    def second_that_go_on(kv, hf):
        for s in range(3):
            wait_far(s, 1, kv, hf, ok=needs_second[s])
        for s in range(3):
            send_far(s, 1, kv, hf, ok=~after_first[s])

    def second_arrivals(kv, hf):
        for s in range(3):
            wait_far(s, 1, kv, hf, ok=~needs_second[s])
        for s in range(3):
            send_strips(s, 1, kv, hf)

    first_arrivals(0, 0)
    first_arrivals(1, 0)
    first_arrivals(0, 1)
    wait_strip_at(0, 0, OWN)
    for s in range(3):
        wait_strip(s, 0, 0)
    score_blocks((own,) + first_slots, 0, first=True)
    wait_side(0, 0, true, own_rel)
    wait_side(event(2, 0), 0, mate_ok[0][2], mate_rel[0][2])
    score_blocks((own, first_slots[2]), 1, first=True)
    second_that_go_on(0, 0)
    first_arrivals(1, 1)
    second_that_go_on(1, 0)
    second_arrivals(0, 0)
    pass_near()
    second_that_go_on(0, 1)
    second_arrivals(1, 0)

    def near_layer(rp):
        @pl.loop(0, TILES, unroll=True)
        def _(t):
            cols = pl.ds(pl.multiple_of(TILE * t, TILE), TILE)
            keys = pl.ds(pl.multiple_of(TILE * t, TILE), NEAR_KEYS)
            q = qn[pl.ds(2 * rp, 2), cols, :].reshape(2 * TILE, CH)
            k = near[0, pl.ds(2 * rp, 8), keys, :].reshape(8 * NEAR_KEYS, CH)
            v = near[1, pl.ds(2 * rp, 8), keys, :].reshape(8 * NEAR_KEYS, CH)
            s = lax.dot_general(block_queries(q), k, dims_t, preferred_element_type=jnp.float32) * SCALE
            s = s.reshape(HEADS, 2 * TILE, 8 * NEAR_KEYS) + bias_near[rp * TILES + t][None]
            s = s.reshape(HEADS * 2 * TILE, 8 * NEAR_KEYS)
            p = jnp.exp2(s - jnp.max(s, axis=1, keepdims=True))
            inverse = 1.0 / jnp.sum(p, axis=1, keepdims=True)
            o = lax.dot_general(p.astype(jnp.bfloat16), v, dims, preferred_element_type=jnp.float32) * inverse
            out = None
            for h in range(HEADS):
                part = o[h * 2 * TILE : (h + 1) * 2 * TILE] * head_mask[h]
                out = part if out is None else out + part
            out_near[pl.ds(2 * rp, 2), cols, :] = out.astype(jnp.bfloat16).reshape(2, TILE, CH)

    second_arrivals(0, 1)
    second_that_go_on(1, 1)
    for s in range(3):
        wait_strip(s, 1, 0)
    score_blocks(second_slots, 0)
    later_sides(0)
    score_blocks(first_slots[:2] + second_slots, 1)

    @pl.loop(0, ROWS, unroll=2)
    def _(r):
        for t in range(TILES):
            idx = r * TILES + t
            m = jnp.max(peak[idx], axis=1, keepdims=True)
            summed = None
            for a in range(SLOTS):
                p = jnp.exp2(scores[a, idx] - m)
                probs[a, idx] = p.astype(jnp.bfloat16)
                summed = p if summed is None else summed + p
            total[idx] = jnp.broadcast_to(1.0 / jnp.sum(summed, axis=1, keepdims=True), (HEADS * TILE, 128))

    wait_strip_at(0, 1, OWN)
    wait_strip(2, 0, 1)
    wait_side(0, 1, true, own_rel)
    wait_side(event(2, 0), 1, mate_ok[0][2], mate_rel[0][2])

    @pl.loop(0, ROWS, unroll=2)
    def _(r):
        for t in range(TILES):
            idx = r * TILES + t
            acc[idx] = value_sum(idx, r, t, (own, first_slots[2]), None)

    for s in range(2):
        wait_far(s, 0, 1, 1, ok=late_in[s])
    for s in range(2):
        send_strips(s, 0, 1, 1, ok=late_in[s])
    second_arrivals(1, 1)
    wait_near()
    near_layer(0)
    near_layer(1)
    near_out = pltpu.make_async_copy(out_near, on_ref, out_sem.at[0])
    near_out.start()
    for s in range(2):
        wait_strip(s, 0, 1)
    for s in range(3):
        wait_strip(s, 1, 1)
    later_sides(1)

    @pl.loop(0, ROWS, unroll=2)
    def _(r):
        for t in range(TILES):
            idx = r * TILES + t
            o = value_sum(idx, r, t, first_slots[:2] + second_slots, acc[idx])
            out = None
            for h in range(HEADS):
                part = slice(h * TILE, (h + 1) * TILE)
                inverse = total[idx, part, :]
                one = o[part, :] * jnp.concatenate([inverse, inverse], axis=1) * head_mask[h]
                out = one if out is None else out + one
            out_far[r, TILE * t : TILE * (t + 1), :] = out.astype(jnp.bfloat16)

    far_out = pltpu.make_async_copy(out_far, of_ref, out_sem.at[1])
    far_out.start()

    for kv in range(2):
        strip_copy(0, kv, OWN).wait_send()

        @pl.when(inner)
        def _():
            side_copy(0, kv, own_rel).wait_send()

        for s in range(2):
            @pl.when(extra_ok[s])
            def _():
                extra_copy(s, kv).wait_send()

        for o in range(2):
            for s in range(3):
                @pl.when(send_ok[o][s])
                def _():
                    far_copy(s, o, kv, 0).wait_send()
                    far_copy(s, o, kv, 1).wait_send()

                @pl.when(recv_ok[o][s])
                def _():
                    strip_copy(event(s, o), kv, in_slot[o][s]).wait_send()

                @pl.when(side_ok(recv_ok[o][s], recv_rel[o][s] - hop))
                def _():
                    side_copy(event(s, o), kv, recv_rel[o][s]).wait_send()

    for n, (dr, dc) in enumerate(sides):
        for kv in range(1 if dc else 2):
            @pl.when(there(dr, dc) if dc else there(dr, dc) & ~crossing(dr))
            def _():
                near_copy(n, kv).wait_send()

    for kv in range(2):
        for dr in (-1, 1):
            @pl.when(sends_pass(dr))
            def _():
                pass_in(kv, dr).wait_send()

            @pl.when(passes(kv, dr))
            def _():
                pass_on(kv, dr).wait_send()

    near_out.wait()
    far_out.wait()


def finish_kernel(near_ref, far_ref, near_out_ref, far_out_ref, near_held, far_held, sem):
    first = [
        pltpu.make_async_copy(near_ref, near_held, sem.at[0]),
        pltpu.make_async_copy(far_ref, far_held, sem.at[1]),
    ]
    second = [
        pltpu.make_async_copy(near_held, near_out_ref, sem.at[0]),
        pltpu.make_async_copy(far_held, far_out_ref, sem.at[1]),
    ]
    for copy in first:
        copy.start()
    for n in range(2):
        first[n].wait()
        second[n].start()
    for copy in second:
        copy.wait()


def per_device(query_near, key_near, value_near, dilated_queries, dilated_keys, dilated_values):
    block = jax.ShapeDtypeStruct((ROWS, COLS, CH), jnp.bfloat16)
    tiles = ROWS * TILES
    dma = pltpu.SemaphoreType.DMA
    anywhere = pl.BlockSpec(memory_space=pl.ANY)
    results = pl.pallas_call(
        kernel,
        out_shape=(block, block),
        in_specs=[pl.BlockSpec(memory_space=pltpu.HBM)] * 6,
        out_specs=(anywhere, anywhere),
        scratch_shapes=[
            pltpu.VMEM((2, SLOTS, ROWS, WIDE, CH), jnp.bfloat16),
            pltpu.VMEM((2, NEAR_ROWS, NEAR_WIDE, CH), jnp.bfloat16),
            pltpu.VMEM((ROWS, COLS, CH), jnp.bfloat16),
            pltpu.VMEM((ROWS, COLS, CH), jnp.bfloat16),
            pltpu.VMEM((tiles, HEADS * TILE, CH), jnp.bfloat16),
            pltpu.VMEM((SLOTS, tiles, HEADS * TILE, KEYS), jnp.float32),
            pltpu.VMEM((tiles, HEADS * TILE, KEYS), jnp.float32),
            pltpu.VMEM((SLOTS, tiles, HEADS * TILE, KEYS), jnp.bfloat16),
            pltpu.VMEM((tiles, HEADS * TILE, 128), jnp.float32),
            pltpu.VMEM((tiles, HEADS * TILE, CH), jnp.float32),
            pltpu.VMEM((TILES, TILE, KEYS), jnp.float32),
            pltpu.VMEM((2 * TILES, 2 * TILE, 8 * NEAR_KEYS), jnp.float32),
            pltpu.VMEM((2, 2, 4 * ROWS, CH), jnp.bfloat16),
            pltpu.VMEM((9, 2, 4 * ROWS, CH), jnp.bfloat16),
            pltpu.VMEM((2, 3, COLS, CH), jnp.bfloat16),
            pltpu.VMEM((ROWS, COLS, CH), jnp.bfloat16),
            pltpu.VMEM((ROWS, COLS, CH), jnp.bfloat16),
            dma((6,)),
            dma((3, 2, 2, 2)),
            dma((3, 2, 2, 2)),
            dma((7, 2)),
            dma((7, 2)),
            dma((7, 2)),
            dma((7, 2)),
            dma((2,)),
            dma((2,)),
            dma((8, 2)),
            dma((8, 2)),
            dma((2,)),
            dma((2,)),
            dma((2,)),
        ],
        compiler_params=pltpu.CompilerParams(
            collective_id=0, has_side_effects=True, vmem_limit_bytes=56 << 20
        ),
        name="two_layers",
    )(query_near, key_near, value_near, dilated_queries, dilated_keys, dilated_values)
    return pl.pallas_call(
        finish_kernel,
        out_shape=(block, block),
        in_specs=[anywhere] * 2,
        out_specs=(anywhere, anywhere),
        scratch_shapes=[
            pltpu.VMEM((ROWS, COLS, CH), jnp.bfloat16),
            pltpu.VMEM((ROWS, COLS, CH), jnp.bfloat16),
            dma((2,)),
        ],
        compiler_params=pltpu.CompilerParams(vmem_limit_bytes=56 << 20),
        name="results_out",
    )(*results)


def solution(mesh):
    placed = (P("row", "col", None),) * 6
    return jax.shard_map(
        per_device,
        mesh=mesh,
        in_specs=placed,
        out_specs=(P("row", "col", None), P("row", "col", None)),
        check_vma=False,
    )
```

```python
import functools
import math

import jax
import jax.numpy as jnp
from jax import lax
from jax.experimental import pallas as pl
from jax.experimental.pallas import tpu as pltpu
from jax.sharding import PartitionSpec as P

MESH = pl.DeviceIdType.MESH
HEADS = 4
HEAD = 64
CH = 256
ROWS = 4
COLS = 128
STRIP = 48
WIDE = COLS + 2 * STRIP
STEP = 16
SLOTS = 7
OWN = 3
EDGE = 16
NEAR_WIDE = COLS + 2 * EDGE
NEAR_ROWS = ROWS + 6
TILE = 32
TILES = COLS // TILE
KEYS = TILE + 2 * STRIP
NEAR_KEYS = TILE + 2 * EDGE
SCALE = math.log2(math.e) / math.sqrt(HEAD)
NONE = 99

SECOND = (
    (1, -1, -1, NONE, 1, NONE, -2, NONE),
    (NONE, 2, NONE, -1, NONE, 1, 1, -1),
    (4, 2, 2, 2, -2, -2, -2, -4),
)
FROM_STREAM = ((2, 2, 0, 0, 2, 0, 0, 0), (0, 1, 0, 2, 0, 1, 2, 2), (0, 1, 1, 1, 0, 0, 0, 1))
FROM_SECOND = ((0, 0, 1, 0, 0, 0, 0, 0), (0, 0, 0, 0, 0, 1, 0, 0), (1, 0, 0, 0, 0, 0, 0, 1))
VALUES_LAST = ((0,), (7,), ())


def pick(table, place):
    out = jnp.int32(table[0])
    for k in range(1, len(table)):
        out = jnp.where(place == k, jnp.int32(table[k]), out)
    return out


def one_of(place, places):
    out = jnp.bool_(False)
    for k in places:
        out = out | (place == k)
    return out


def kernel(
    qn_ref, kn_ref, vn_ref, qf_ref, kf_ref, vf_ref, on_ref, of_ref,
    far, near, qn, qf, qb, scores, peak, top, probs, total, acc, bias_far, bias_near, edge_out, edge_in, passing, out_near, out_far,
    load_sem, far_send, far_recv, strip_send, strip_recv, side_send, side_recv, extra_send, extra_recv, near_send, near_recv, pass_send, pass_recv, out_sem,
):
    row = lax.axis_index("row")
    col = lax.axis_index("col")
    n_rows = lax.axis_size("row")
    n_cols = lax.axis_size("col")
    x = row // 8
    z = (row // 4) % 2
    y = row % 4
    core = col % 2
    place = 2 * x + z
    inner = (col == 1) | (col == 2)
    true = jnp.bool_(True)

    loads = [
        pltpu.make_async_copy(kf_ref, far.at[0, OWN, :, pl.ds(STRIP, COLS)], load_sem.at[0]),
        pltpu.make_async_copy(vf_ref, far.at[1, OWN, :, pl.ds(STRIP, COLS)], load_sem.at[1]),
        pltpu.make_async_copy(kn_ref, near.at[0, pl.ds(3, ROWS), pl.ds(EDGE, COLS)], load_sem.at[2]),
        pltpu.make_async_copy(vn_ref, near.at[1, pl.ds(3, ROWS), pl.ds(EDGE, COLS)], load_sem.at[3]),
        pltpu.make_async_copy(qf_ref, qf, load_sem.at[4]),
        pltpu.make_async_copy(qn_ref, qn, load_sem.at[5]),
    ]
    for load in loads:
        load.start()

    to_row = ((row + 8) % n_rows, (row + n_rows - 8) % n_rows, row + 4 - 8 * z)
    hop = 1 - 2 * z

    def arrivals(at, hop):
        first_ok = (at >= 2, at < 6, true)
        back = (-2, 2, hop)
        sent = [pick(SECOND[s], (at + back[s] + 8) % 8) for s in range(3)]
        second_ok = [sent[s] != NONE for s in range(3)]
        ring = (jnp.where(at < 2, 8, 0), jnp.where(at >= 6, -8, 0), 0)
        return (first_ok, second_ok), (back, [sent[s] + back[s] + ring[s] for s in range(3)])

    def slot_of(rel):
        return (rel + 10) % 7

    recv_ok, recv_rel = arrivals(place, hop)
    mate_ok, mate_rel = arrivals(place + hop, -hop)
    in_slot = [[slot_of(jnp.int32(rel)) for rel in rels] for rels in recv_rel]
    second_rel = [pick(SECOND[s], place) for s in range(3)]
    second_send = [second_rel[s] != NONE for s in range(3)]
    send_ok = ((x < 3, x > 0, true), second_send)
    shift = (-2, 2, -hop)
    ring = (jnp.where(place >= 6, 8, 0), jnp.where(place < 2, -8, 0), 0)
    src_slot = ([jnp.int32(OWN)] * 3, [slot_of(second_rel[s]) for s in range(3)])
    dst_slot = ([slot_of(jnp.int32(shift[s])) for s in range(3)], [slot_of(second_rel[s] + shift[s] + ring[s]) for s in range(3)])
    values_last = [one_of(place, VALUES_LAST[s]) for s in range(3)]
    late_in = [recv_ok[0][s] & one_of(place + (-2, 2, hop)[s], VALUES_LAST[s]) for s in range(3)]

    def piece(hf):
        offset = jnp.where(col < 2, (COLS, STRIP)[hf], (STRIP, 2 * STRIP)[hf])
        return pl.ds(0, ROWS), pl.ds(pl.multiple_of(offset, 16), (STRIP, COLS - STRIP)[hf])

    def far_copy(s, o, kv, hf):
        return pltpu.make_async_remote_copy(
            far.at[kv, src_slot[o][s], *piece(hf)],
            far.at[kv, dst_slot[o][s], *piece(hf)],
            far_send.at[s, o, kv, hf],
            far_recv.at[s, o, kv, hf],
            device_id=(to_row[s], col),
            device_id_type=MESH,
        )

    def send_far(s, o, kv, hf, ok=true):
        @pl.when(send_ok[o][s] & ok)
        def _():
            far_copy(s, o, kv, hf).start()

    def wait_far(s, o, kv, hf, ok=true):
        @pl.when(recv_ok[o][s] & ok)
        def _():
            block = far.at[kv, in_slot[o][s], *piece(hf)]
            pltpu.make_async_remote_copy(
                block, block, far_send.at[s, o, kv, hf], far_recv.at[s, o, kv, hf],
                device_id=(to_row[s], col), device_id_type=MESH,
            ).wait_recv()

    mate = col + 1 - 2 * core
    strip_src = pl.multiple_of(jnp.where(core == 0, COLS, STRIP), 16)
    strip_dst = pl.multiple_of(jnp.where(core == 0, 0, STRIP + COLS), 16)
    strip_in = pl.multiple_of(jnp.where(core == 0, STRIP + COLS, 0), 16)

    def strip_copy(e, kv, slot):
        return pltpu.make_async_remote_copy(
            far.at[kv, slot, :, pl.ds(strip_src, STRIP)],
            far.at[kv, slot, :, pl.ds(strip_dst, STRIP)],
            strip_send.at[e, kv],
            strip_recv.at[e, kv],
            device_id=(row, mate),
            device_id_type=MESH,
        )

    def wait_strip_at(e, kv, slot):
        block = far.at[kv, slot, :, pl.ds(strip_in, STRIP)]
        pltpu.make_async_remote_copy(
            block, block, strip_send.at[e, kv], strip_recv.at[e, kv],
            device_id=(row, mate), device_id_type=MESH,
        ).wait_recv()

    def event(s, o):
        return 1 + 3 * o + s

    side_src = pl.multiple_of(jnp.where(col == 1, COLS, STRIP), 16)
    side_dst = pl.multiple_of(jnp.where(col == 1, 0, STRIP + COLS), 16)
    side_in = pl.multiple_of(jnp.where(col == 1, STRIP + COLS, 0), 16)

    def side_ok(ok, rel):
        return inner & ok & (rel >= -3) & (rel <= 3)

    def side_copy(e, kv, rel):
        return pltpu.make_async_remote_copy(
            far.at[kv, slot_of(rel), :, pl.ds(side_src, STRIP)],
            far.at[kv, OWN + rel - hop, :, pl.ds(side_dst, STRIP)],
            side_send.at[e, kv],
            side_recv.at[e, kv],
            device_id=(to_row[2], 3 - col),
            device_id_type=MESH,
        )

    def wait_side(e, kv, ok, rel):
        @pl.when(side_ok(ok, rel + hop))
        def _():
            block = far.at[kv, OWN + rel + hop, :, pl.ds(side_in, STRIP)]
            pltpu.make_async_remote_copy(
                block, block, side_send.at[e, kv], side_recv.at[e, kv],
                device_id=(to_row[2], 3 - col), device_id_type=MESH,
            ).wait_recv()

    own_rel = jnp.int32(0)
    extra_ok = (inner & (place == 3), inner & (place == 4))
    extra_from = (1, 5)
    extra_to = (0, 6)
    extra_row = (row + 4, row - 4)

    def extra_copy(s, kv):
        return pltpu.make_async_remote_copy(
            far.at[kv, extra_from[s], :, pl.ds(side_src, STRIP)],
            far.at[kv, extra_to[s], :, pl.ds(side_dst, STRIP)],
            extra_send.at[kv],
            extra_recv.at[kv],
            device_id=(extra_row[s], 3 - col),
            device_id_type=MESH,
        )

    def wait_extra(kv):
        for s in range(2):
            @pl.when(extra_ok[s])
            def _():
                block = far.at[kv, extra_to[1 - s], :, pl.ds(side_in, STRIP)]
                pltpu.make_async_remote_copy(
                    block, block, extra_send.at[kv], extra_recv.at[kv],
                    device_id=(extra_row[s], 3 - col), device_id_type=MESH,
                ).wait_recv()

    def send_strips(s, o, kv, hf, ok=true):
        ok = recv_ok[o][s] & ok
        rel = recv_rel[o][s]
        e = event(s, o)

        @pl.when(ok & (inner if hf else ~inner))
        def _():
            strip_copy(e, kv, in_slot[o][s]).start()

        if hf == 0:
            @pl.when(side_ok(ok, rel - hop))
            def _():
                side_copy(e, kv, rel).start()

            if o == 0 and s < 2:
                @pl.when(extra_ok[s] & ok)
                def _():
                    extra_copy(s, kv).start()

    def wait_strip(s, o, kv):
        @pl.when(recv_ok[o][s])
        def _():
            wait_strip_at(event(s, o), kv, in_slot[o][s])

    sides = [(dr, dc) for dr in (-1, 0, 1) for dc in (-1, 0, 1) if (dr, dc) != (0, 0)]

    def there(dr, dc):
        good = true
        if dr:
            good = good & ((row + dr >= 0) & (row + dr < n_rows))
        if dc:
            good = good & ((col + dc >= 0) & (col + dc < n_cols))
        return good

    row_src = {1: (4, 3), -1: (3, 3)}
    row_dst = {1: (0, 3), -1: (7, 3)}
    row_from = {1: 1, 0: 0, -1: 0}
    row_to = {1: 0, 0: 3, -1: 7}
    main = pl.ds(EDGE, COLS)

    def crossing(dr):
        return {0: jnp.bool_(False), 1: y == 3, -1: y == 0}[dr]

    FIRST_LEG = (2, -1)
    LAST_LEG = (-1, 2)

    def sends_pass(dr):
        return crossing(dr) & there(dr, 0)

    def passes(kv, dr):
        at = {(0, 1): 1, (0, -1): 2, (1, 1): 2, (1, -1): 1}[kv, dr]
        back, on = row - FIRST_LEG[kv] * dr, row + LAST_LEG[kv] * dr
        return (y == at) & (back >= 0) & (back < n_rows) & (on >= 0) & (on < n_rows)

    def pass_in(kv, dr):
        return pltpu.make_async_remote_copy(
            near.at[kv, pl.ds(*row_src[dr]), main],
            passing.at[kv],
            pass_send.at[kv],
            pass_recv.at[kv],
            device_id=(row + FIRST_LEG[kv] * dr, col),
            device_id_type=MESH,
        )

    def pass_on(kv, dr):
        n = sides.index((dr, 0))
        return pltpu.make_async_remote_copy(
            passing.at[kv],
            near.at[kv, pl.ds(*row_dst[dr]), main],
            pass_send.at[kv],
            near_recv.at[n, kv],
            device_id=(row + LAST_LEG[kv] * dr, col),
            device_id_type=MESH,
        )

    def near_copy(n, kv):
        dr, dc = sides[n]
        if dc:
            src, dst = edge_out.at[(dc + 1) // 2], edge_in.at[n]
        else:
            src, dst = near.at[kv, pl.ds(*row_src[dr]), main], near.at[kv, pl.ds(*row_dst[dr]), main]
        return pltpu.make_async_remote_copy(
            src, dst, near_send.at[n, kv], near_recv.at[n, kv], device_id=(row + dr, col + dc), device_id_type=MESH
        )

    def near_arrival(n, kv):
        dr, dc = sides[n]
        block = edge_in.at[n] if dc else near.at[kv, pl.ds(*row_dst[dr]), main]
        return pltpu.make_async_remote_copy(
            block, block, near_send.at[n, kv], near_recv.at[n, kv],
            device_id=(row - dr, col - dc), device_id_type=MESH,
        )

    barrier = pltpu.get_barrier_semaphore()
    expected = jnp.int32(0)
    for s in range(3):
        @pl.when(send_ok[0][s])
        def _():
            pl.semaphore_signal(barrier, inc=1, device_id=(to_row[s], col), device_id_type=MESH)

        expected = expected + recv_ok[0][s].astype(jnp.int32)

    for s, places in ((0, (6, 7)), (1, (0, 1))):
        @pl.when(one_of(place, places))
        def _():
            pl.semaphore_signal(barrier, inc=1, device_id=(to_row[s], col), device_id_type=MESH)

        expected = expected + one_of(place, places).astype(jnp.int32)

    @pl.when(inner)
    def _():
        pl.semaphore_signal(barrier, inc=1, device_id=(to_row[2], 3 - col), device_id_type=MESH)

    expected = expected + inner.astype(jnp.int32)
    for s in range(2):
        @pl.when(extra_ok[s])
        def _():
            pl.semaphore_signal(barrier, inc=1, device_id=(extra_row[s], 3 - col), device_id_type=MESH)

        expected = expected + extra_ok[s].astype(jnp.int32)
    for dr, dc in sides:
        @pl.when(there(dr, dc))
        def _():
            pl.semaphore_signal(barrier, inc=1, device_id=(row + dr, col + dc), device_id_type=MESH)

        expected = expected + there(-dr, -dc).astype(jnp.int32)
    for dr in (-1, 1):
        @pl.when(sends_pass(dr))
        def _():
            pl.semaphore_signal(barrier, inc=1, device_id=(row + 2 * dr, col), device_id_type=MESH)

        @pl.when(passes(0, dr))
        def _():
            pl.semaphore_signal(barrier, inc=1, device_id=(row - 2 * dr, col), device_id_type=MESH)

        @pl.when(passes(1, dr))
        def _():
            pl.semaphore_signal(barrier, inc=1, device_id=(row + 2 * dr, col), device_id_type=MESH)

        @pl.when(sends_pass(-dr))
        def _():
            pl.semaphore_signal(barrier, inc=1, device_id=(row - 2 * dr, col), device_id_type=MESH)

        for good in (sends_pass(dr), passes(0, dr), passes(1, dr), sends_pass(-dr)):
            expected = expected + good.astype(jnp.int32)
    pl.semaphore_wait(barrier, expected)

    for hf in range(2):
        for kv in range(2):
            if hf == 0:
                loads[kv].wait()
            for s in range(3):
                send_far(s, 0, kv, hf, ok=~values_last[s] if (kv and hf) else true)
            if hf == 0:
                strip_copy(0, kv, OWN).start()

                @pl.when(inner)
                def _():
                    side_copy(0, kv, own_rel).start()

    loads[2].wait()
    loads[3].wait()
    for dc in (-1, 1):
        at = EDGE + (COLS - EDGE if dc == 1 else 0)
        inside = EDGE - 4 if dc == 1 else 0
        for kv in range(2):
            parts = [near[kv, 3 + r, at : at + EDGE, :].astype(jnp.float32)[inside : inside + 4] for r in range(ROWS)]
            edge_out[(dc + 1) // 2, kv] = jnp.concatenate(parts, axis=0).astype(jnp.bfloat16)

    def send_near():
        for n, (dr, dc) in enumerate(sides):
            for kv in range(1 if dc else 2):
                @pl.when(there(dr, dc) if dc else there(dr, dc) & ~crossing(dr))
                def _():
                    near_copy(n, kv).start()

        for dr in (-1, 1):
            @pl.when(sends_pass(dr))
            def _():
                pass_in(0, dr).start()
                pass_in(1, dr).start()

    def pass_near():
        for kv in range(2):
            for dr in (-1, 1):
                @pl.when(passes(kv, dr))
                def _():
                    pltpu.make_async_remote_copy(
                        passing.at[kv], passing.at[kv], pass_send.at[kv], pass_recv.at[kv],
                        device_id=(row - FIRST_LEG[kv] * dr, col), device_id_type=MESH,
                    ).wait_recv()
                    pass_on(kv, dr).start()

    def wait_near():
        for n, (dr, dc) in enumerate(sides):
            @pl.when(there(-dr, -dc))
            def _():
                near_arrival(n, 0).wait_recv()
                if dc == 0:
                    near_arrival(n, 1).wait_recv()
                else:
                    at = 0 if dc == 1 else EDGE + COLS
                    blank = jnp.zeros((EDGE - 4, CH), jnp.float32)
                    for kv in range(2):
                        packed = edge_in[n, kv].astype(jnp.float32)
                        for r in range(ROWS if dr == 0 else 3):
                            four = packed[4 * (row_from[dr] + r) : 4 * (row_from[dr] + r) + 4]
                            full = [blank, four] if dc == 1 else [four, blank]
                            near[kv, row_to[dr] + r, at : at + EDGE, :] = jnp.concatenate(full, axis=0).astype(
                                jnp.bfloat16
                            )

    send_near()

    c0 = col * COLS
    width = n_cols * COLS
    for t in range(TILES):
        q_at = lax.broadcasted_iota(jnp.int32, (TILE, KEYS), 0)
        k_at = lax.broadcasted_iota(jnp.int32, (TILE, KEYS), 1)
        apart = k_at - q_at
        k_col = c0 + TILE * t - STRIP + k_at
        good = ((apart & (STEP - 1)) == 0) & (apart >= 0) & (apart <= 2 * STRIP) & (k_col >= 0) & (k_col < width)
        bias_far[t] = jnp.where(good, 0.0, -jnp.inf)
    for rp in range(2):
        for t in range(TILES):
            shape = (2 * TILE, 8 * NEAR_KEYS)
            q_id = lax.broadcasted_iota(jnp.int32, shape, 0)
            k_id = lax.broadcasted_iota(jnp.int32, shape, 1)
            r_off = (k_id // NEAR_KEYS) - (q_id // TILE)
            c_off = (k_id % NEAR_KEYS) - (q_id % TILE) - EDGE
            k_row = row * ROWS + 2 * rp - 3 + (k_id // NEAR_KEYS)
            k_col = c0 + TILE * t - EDGE + (k_id % NEAR_KEYS)
            good = (r_off >= 0) & (r_off <= 6) & (c_off >= -3) & (c_off <= 3)
            good = good & (k_row >= 0) & (k_row < n_rows * ROWS) & (k_col >= 0) & (k_col < width)
            bias_near[rp * TILES + t] = jnp.where(good, 0.0, -jnp.inf)

    zero = lambda shape: jnp.zeros(shape, jnp.bfloat16)
    for a in range(SLOTS):
        relayed = (a == 0) & (place == 0) | (a == 6) & (place == 7)
        lost = ((place + a - OWN < 0) | (place + a - OWN > 7)) & ~relayed

        @pl.when(lost)
        def _():
            for kv in range(2):
                for r in range(ROWS):
                    far[kv, a, r] = zero((WIDE, CH))

        @pl.when(~lost & (col == 0))
        def _():
            for kv in range(2):
                for r in range(ROWS):
                    far[kv, a, r, 0:STRIP] = zero((STRIP, CH))

        @pl.when(~lost & (col == 3))
        def _():
            for kv in range(2):
                for r in range(ROWS):
                    far[kv, a, r, STRIP + COLS : WIDE] = zero((STRIP, CH))

        if a in (0, 6):
            @pl.when(relayed & inner)
            def _():
                for kv in range(2):
                    for r in range(ROWS):
                        far[kv, a, r, pl.ds(side_in, STRIP)] = zero((STRIP, CH))

    for kv in range(2):
        @pl.when(row == 0)
        def _():
            near[kv, 0:3] = zero((3, NEAR_WIDE, CH))

        @pl.when(row == n_rows - 1)
        def _():
            near[kv, 7:10] = zero((3, NEAR_WIDE, CH))

        @pl.when(col == 0)
        def _():
            near[kv, :, 0:EDGE] = zero((NEAR_ROWS, EDGE, CH))

        @pl.when(col == n_cols - 1)
        def _():
            near[kv, :, EDGE + COLS : NEAR_WIDE] = zero((NEAR_ROWS, EDGE, CH))

    lane_head = lax.broadcasted_iota(jnp.int32, (1, CH), 1) // HEAD
    head_mask = [(lane_head == h).astype(jnp.float32) for h in range(HEADS)]
    head_mask_narrow = [m.astype(jnp.bfloat16) for m in head_mask]
    dims_t = (((1,), (1,)), ((), ()))
    dims = (((1,), (0,)), ((), ()))

    loads[4].wait()
    loads[5].wait()

    def block_queries(q):
        return jnp.concatenate([q * head_mask_narrow[h] for h in range(HEADS)], axis=0)

    @pl.loop(0, ROWS, unroll=2)
    def _(r):
        for t in range(TILES):
            qb[r * TILES + t] = block_queries(qf[r, TILE * t : TILE * (t + 1), :])

    half_tiles = (jnp.where(col < 2, 0, 2), jnp.where(col < 2, 2, 0))

    def score_blocks(slots, part, first=False):
        row_bias = []
        for slot in slots:
            ok = (place + slot - OWN >= 0) & (place + slot - OWN <= 7)
            row_bias.append(jnp.where(ok, 0.0, -jnp.inf).astype(jnp.float32))

        @pl.loop(0, ROWS, unroll=2)
        def _(r):
            for tt in range(2):
                t = half_tiles[part] + tt
                idx = r * TILES + t
                where = pl.ds(pl.multiple_of(TILE * t, TILE), KEYS)
                top = None if first else peak[idx]
                for n in range(0, len(slots), 2):
                    pair = slots[n : n + 2]
                    k = jnp.concatenate([far[0, slot, r, where, :] for slot in pair], axis=0)
                    both = lax.dot_general(qb[idx], k, dims_t, preferred_element_type=jnp.float32) * SCALE
                    for m, slot in enumerate(pair):
                        b = bias_far[t] + row_bias[n + m]
                        s = both[:, m * KEYS : (m + 1) * KEYS].reshape(HEADS, TILE, KEYS) + b[None]
                        s = s.reshape(HEADS * TILE, KEYS)
                        scores[slot, idx] = s
                        top = s if top is None else jnp.maximum(top, s)
                peak[idx] = top

    def value_sum(idx, r, t, slots, o):
        where = pl.ds(pl.multiple_of(TILE * t, TILE), KEYS)
        for n in range(0, len(slots), 2):
            pair = slots[n : n + 2]
            p = jnp.concatenate([probs[slot, idx] for slot in pair], axis=1)
            v = jnp.concatenate([far[1, slot, r, where, :] for slot in pair], axis=0)
            d = lax.dot_general(p, v, dims, preferred_element_type=jnp.float32)
            o = d if o is None else o + d
        return o

    from_stream = [pick(FROM_STREAM[s], place) for s in range(3)]
    after_first = [pick(FROM_SECOND[s], place) == 0 for s in range(3)]
    needs_second = [jnp.bool_(False)] * 3
    for s in range(3):
        for d in range(3):
            needs_second[d] = needs_second[d] | (second_send[s] & ~after_first[s] & (from_stream[s] == d))

    first_slots = (jnp.int32(1), jnp.int32(5), OWN + hop)
    second_slots = (jnp.int32(0), jnp.int32(6), OWN - hop)
    own = jnp.int32(OWN)

    def later_sides(kv):
        for o in range(2):
            for s in range(3):
                if (s, o) != (2, 0):
                    wait_side(event(s, o), kv, mate_ok[o][s], mate_rel[o][s])
        wait_extra(kv)

    def first_arrivals(kv, hf):
        late = kv == 1 and hf == 1
        for s in range(3):
            wait_far(s, 0, kv, hf, ok=~late_in[s] if late else true)
        for s in range(3):
            send_far(s, 1, kv, hf, ok=after_first[s])
        if late:
            for s in range(3):
                send_far(s, 0, kv, hf, ok=values_last[s])
        for s in range(3):
            send_strips(s, 0, kv, hf, ok=~late_in[s] if late else true)

    def second_that_go_on(kv, hf):
        for s in range(3):
            wait_far(s, 1, kv, hf, ok=needs_second[s])
        for s in range(3):
            send_far(s, 1, kv, hf, ok=~after_first[s])

    def second_arrivals(kv, hf):
        for s in range(3):
            wait_far(s, 1, kv, hf, ok=~needs_second[s])
        for s in range(3):
            send_strips(s, 1, kv, hf)

    first_arrivals(0, 0)
    first_arrivals(1, 0)
    first_arrivals(0, 1)
    wait_strip_at(0, 0, OWN)
    for s in range(3):
        wait_strip(s, 0, 0)
    score_blocks((own,) + first_slots, 0, first=True)
    wait_side(0, 0, true, own_rel)
    wait_side(event(2, 0), 0, mate_ok[0][2], mate_rel[0][2])
    score_blocks((own, first_slots[2]), 1, first=True)
    second_that_go_on(0, 0)
    first_arrivals(1, 1)
    second_that_go_on(1, 0)
    second_arrivals(0, 0)
    pass_near()
    second_that_go_on(0, 1)
    second_arrivals(1, 0)

    def near_layer(rp):
        @pl.loop(0, TILES, unroll=True)
        def _(t):
            cols = pl.ds(pl.multiple_of(TILE * t, TILE), TILE)
            keys = pl.ds(pl.multiple_of(TILE * t, TILE), NEAR_KEYS)
            q = qn[pl.ds(2 * rp, 2), cols, :].reshape(2 * TILE, CH)
            k = near[0, pl.ds(2 * rp, 8), keys, :].reshape(8 * NEAR_KEYS, CH)
            v = near[1, pl.ds(2 * rp, 8), keys, :].reshape(8 * NEAR_KEYS, CH)
            s = lax.dot_general(block_queries(q), k, dims_t, preferred_element_type=jnp.float32) * SCALE
            s = s.reshape(HEADS, 2 * TILE, 8 * NEAR_KEYS) + bias_near[rp * TILES + t][None]
            s = s.reshape(HEADS * 2 * TILE, 8 * NEAR_KEYS)
            p = jnp.exp2(s - jnp.max(s, axis=1, keepdims=True))
            inverse = 1.0 / jnp.sum(p, axis=1, keepdims=True)
            o = lax.dot_general(p.astype(jnp.bfloat16), v, dims, preferred_element_type=jnp.float32) * inverse
            out = None
            for h in range(HEADS):
                part = o[h * 2 * TILE : (h + 1) * 2 * TILE] * head_mask[h]
                out = part if out is None else out + part
            out_near[pl.ds(2 * rp, 2), cols, :] = out.astype(jnp.bfloat16).reshape(2, TILE, CH)

    later_sides(0)
    score_blocks(first_slots[:2], 1)

    def spread(column):
        return jnp.broadcast_to(column, (HEADS * TILE, KEYS))

    @pl.loop(0, ROWS, unroll=2)
    def _(r):
        for t in range(TILES):
            idx = r * TILES + t
            m = jnp.max(peak[idx], axis=1, keepdims=True)
            summed = None
            for slot in (own,) + first_slots:
                p = jnp.exp2(scores[slot, idx] - m)
                probs[slot, idx] = p.astype(jnp.bfloat16)
                summed = p if summed is None else summed + p
            top[idx] = spread(m)
            total[idx] = spread(jnp.sum(summed, axis=1, keepdims=True))

    wait_strip_at(0, 1, OWN)
    wait_strip(2, 0, 1)
    wait_side(0, 1, true, own_rel)
    wait_side(event(2, 0), 1, mate_ok[0][2], mate_rel[0][2])

    @pl.loop(0, ROWS, unroll=2)
    def _(r):
        for t in range(TILES):
            idx = r * TILES + t
            acc[idx] = value_sum(idx, r, t, (own, first_slots[2]), None)

    second_arrivals(0, 1)
    second_that_go_on(1, 1)
    for s in range(3):
        wait_strip(s, 1, 0)
    score_blocks(second_slots, 0, first=True)
    score_blocks(second_slots, 1, first=True)

    @pl.loop(0, ROWS, unroll=2)
    def _(r):
        for t in range(TILES):
            idx = r * TILES + t
            m = jnp.maximum(top[idx], spread(jnp.max(peak[idx], axis=1, keepdims=True)))
            summed = None
            for slot in second_slots:
                p = jnp.exp2(scores[slot, idx] - m)
                probs[slot, idx] = p.astype(jnp.bfloat16)
                summed = p if summed is None else summed + p
            scale = jnp.exp2(top[idx] - m)
            top[idx] = scale
            total[idx] = 1.0 / (total[idx] * scale + spread(jnp.sum(summed, axis=1, keepdims=True)))

    for s in range(2):
        wait_far(s, 0, 1, 1, ok=late_in[s])
    for s in range(2):
        send_strips(s, 0, 1, 1, ok=late_in[s])
    second_arrivals(1, 1)
    wait_near()
    near_layer(0)
    near_layer(1)
    near_out = pltpu.make_async_copy(out_near, on_ref, out_sem.at[0])
    near_out.start()
    for s in range(2):
        wait_strip(s, 0, 1)
    for s in range(3):
        wait_strip(s, 1, 1)
    later_sides(1)

    @pl.loop(0, ROWS, unroll=2)
    def _(r):
        for t in range(TILES):
            idx = r * TILES + t
            scale = top[idx]
            o = value_sum(idx, r, t, first_slots[:2], acc[idx]) * jnp.concatenate([scale, scale], axis=1)
            o = value_sum(idx, r, t, second_slots, o)
            out = None
            for h in range(HEADS):
                part = slice(h * TILE, (h + 1) * TILE)
                inverse = total[idx, part, :]
                one = o[part, :] * jnp.concatenate([inverse, inverse], axis=1) * head_mask[h]
                out = one if out is None else out + one
            out_far[r, TILE * t : TILE * (t + 1), :] = out.astype(jnp.bfloat16)

    far_out = pltpu.make_async_copy(out_far, of_ref, out_sem.at[1])
    far_out.start()

    for kv in range(2):
        strip_copy(0, kv, OWN).wait_send()

        @pl.when(inner)
        def _():
            side_copy(0, kv, own_rel).wait_send()

        for s in range(2):
            @pl.when(extra_ok[s])
            def _():
                extra_copy(s, kv).wait_send()

        for o in range(2):
            for s in range(3):
                @pl.when(send_ok[o][s])
                def _():
                    far_copy(s, o, kv, 0).wait_send()
                    far_copy(s, o, kv, 1).wait_send()

                @pl.when(recv_ok[o][s])
                def _():
                    strip_copy(event(s, o), kv, in_slot[o][s]).wait_send()

                @pl.when(side_ok(recv_ok[o][s], recv_rel[o][s] - hop))
                def _():
                    side_copy(event(s, o), kv, recv_rel[o][s]).wait_send()

    for n, (dr, dc) in enumerate(sides):
        for kv in range(1 if dc else 2):
            @pl.when(there(dr, dc) if dc else there(dr, dc) & ~crossing(dr))
            def _():
                near_copy(n, kv).wait_send()

    for kv in range(2):
        for dr in (-1, 1):
            @pl.when(sends_pass(dr))
            def _():
                pass_in(kv, dr).wait_send()

            @pl.when(passes(kv, dr))
            def _():
                pass_on(kv, dr).wait_send()

    near_out.wait()
    far_out.wait()


def finish_kernel(near_ref, far_ref, near_out_ref, far_out_ref, near_held, far_held, sem):
    first = [
        pltpu.make_async_copy(near_ref, near_held, sem.at[0]),
        pltpu.make_async_copy(far_ref, far_held, sem.at[1]),
    ]
    second = [
        pltpu.make_async_copy(near_held, near_out_ref, sem.at[0]),
        pltpu.make_async_copy(far_held, far_out_ref, sem.at[1]),
    ]
    for copy in first:
        copy.start()
    for n in range(2):
        first[n].wait()
        second[n].start()
    for copy in second:
        copy.wait()


def per_device(query_near, key_near, value_near, dilated_queries, dilated_keys, dilated_values):
    block = jax.ShapeDtypeStruct((ROWS, COLS, CH), jnp.bfloat16)
    tiles = ROWS * TILES
    dma = pltpu.SemaphoreType.DMA
    anywhere = pl.BlockSpec(memory_space=pl.ANY)
    results = pl.pallas_call(
        kernel,
        out_shape=(block, block),
        in_specs=[pl.BlockSpec(memory_space=pltpu.HBM)] * 6,
        out_specs=(anywhere, anywhere),
        scratch_shapes=[
            pltpu.VMEM((2, SLOTS, ROWS, WIDE, CH), jnp.bfloat16),
            pltpu.VMEM((2, NEAR_ROWS, NEAR_WIDE, CH), jnp.bfloat16),
            pltpu.VMEM((ROWS, COLS, CH), jnp.bfloat16),
            pltpu.VMEM((ROWS, COLS, CH), jnp.bfloat16),
            pltpu.VMEM((tiles, HEADS * TILE, CH), jnp.bfloat16),
            pltpu.VMEM((SLOTS, tiles, HEADS * TILE, KEYS), jnp.float32),
            pltpu.VMEM((tiles, HEADS * TILE, KEYS), jnp.float32),
            pltpu.VMEM((tiles, HEADS * TILE, KEYS), jnp.float32),
            pltpu.VMEM((SLOTS, tiles, HEADS * TILE, KEYS), jnp.bfloat16),
            pltpu.VMEM((tiles, HEADS * TILE, 128), jnp.float32),
            pltpu.VMEM((tiles, HEADS * TILE, CH), jnp.float32),
            pltpu.VMEM((TILES, TILE, KEYS), jnp.float32),
            pltpu.VMEM((2 * TILES, 2 * TILE, 8 * NEAR_KEYS), jnp.float32),
            pltpu.VMEM((2, 2, 4 * ROWS, CH), jnp.bfloat16),
            pltpu.VMEM((9, 2, 4 * ROWS, CH), jnp.bfloat16),
            pltpu.VMEM((2, 3, COLS, CH), jnp.bfloat16),
            pltpu.VMEM((ROWS, COLS, CH), jnp.bfloat16),
            pltpu.VMEM((ROWS, COLS, CH), jnp.bfloat16),
            dma((6,)),
            dma((3, 2, 2, 2)),
            dma((3, 2, 2, 2)),
            dma((7, 2)),
            dma((7, 2)),
            dma((7, 2)),
            dma((7, 2)),
            dma((2,)),
            dma((2,)),
            dma((8, 2)),
            dma((8, 2)),
            dma((2,)),
            dma((2,)),
            dma((2,)),
        ],
        compiler_params=pltpu.CompilerParams(
            collective_id=0, has_side_effects=True, vmem_limit_bytes=56 << 20
        ),
        name="two_layers",
    )(query_near, key_near, value_near, dilated_queries, dilated_keys, dilated_values)
    return pl.pallas_call(
        finish_kernel,
        out_shape=(block, block),
        in_specs=[anywhere] * 2,
        out_specs=(anywhere, anywhere),
        scratch_shapes=[
            pltpu.VMEM((ROWS, COLS, CH), jnp.bfloat16),
            pltpu.VMEM((ROWS, COLS, CH), jnp.bfloat16),
            dma((2,)),
        ],
        compiler_params=pltpu.CompilerParams(vmem_limit_bytes=56 << 20),
        name="results_out",
    )(*results)


def solution(mesh):
    placed = (P("row", "col", None),) * 6
    return jax.shard_map(
        per_device,
        mesh=mesh,
        in_specs=placed,
        out_specs=(P("row", "col", None), P("row", "col", None)),
        check_vma=False,
    )
```

```python
import functools
import math

import jax
import jax.numpy as jnp
from jax import lax
from jax.experimental import pallas as pl
from jax.experimental.pallas import tpu as pltpu
from jax.sharding import PartitionSpec as P

MESH = pl.DeviceIdType.MESH
HEADS = 4
HEAD = 64
CH = 256
ROWS = 4
COLS = 128
STRIP = 48
WIDE = COLS + 2 * STRIP
STEP = 16
SLOTS = 7
OWN = 3
EDGE = 16
NEAR_WIDE = COLS + 2 * EDGE
NEAR_ROWS = ROWS + 6
TILE = 32
TILES = COLS // TILE
KEYS = TILE + 2 * STRIP
NEAR_KEYS = TILE + 2 * EDGE
SCALE = math.log2(math.e) / math.sqrt(HEAD)
NONE = 99

SECOND = (
    (1, -1, -1, NONE, 1, NONE, -2, NONE),
    (NONE, 2, NONE, -1, NONE, 1, 1, -1),
    (4, 2, 2, 2, -2, -2, -2, -4),
)
FROM_STREAM = ((2, 2, 0, 0, 2, 0, 0, 0), (0, 1, 0, 2, 0, 1, 2, 2), (0, 1, 1, 1, 0, 0, 0, 1))
FROM_SECOND = ((0, 0, 1, 0, 0, 0, 0, 0), (0, 0, 0, 0, 0, 1, 0, 0), (1, 0, 0, 0, 0, 0, 0, 1))
VALUES_LAST = ((0,), (7,), ())


def pick(table, place):
    out = jnp.int32(table[0])
    for k in range(1, len(table)):
        out = jnp.where(place == k, jnp.int32(table[k]), out)
    return out


def one_of(place, places):
    out = jnp.bool_(False)
    for k in places:
        out = out | (place == k)
    return out


def kernel(
    qn_ref, kn_ref, vn_ref, qf_ref, kf_ref, vf_ref, on_ref, of_ref,
    far, near, qn, qf, qb, scores, peak, top, probs, total, acc, bias_far, bias_near, edge_out, edge_in, passing, out_near, out_far,
    load_sem, far_send, far_recv, strip_send, strip_recv, side_send, side_recv, extra_send, extra_recv, near_send, near_recv, pass_send, pass_recv, out_sem,
):
    row = lax.axis_index("row")
    col = lax.axis_index("col")
    n_rows = lax.axis_size("row")
    n_cols = lax.axis_size("col")
    x = row // 8
    z = (row // 4) % 2
    y = row % 4
    core = col % 2
    place = 2 * x + z
    inner = (col == 1) | (col == 2)
    true = jnp.bool_(True)

    loads = [
        pltpu.make_async_copy(kf_ref, far.at[0, OWN, :, pl.ds(STRIP, COLS)], load_sem.at[0]),
        pltpu.make_async_copy(vf_ref, far.at[1, OWN, :, pl.ds(STRIP, COLS)], load_sem.at[1]),
        pltpu.make_async_copy(kn_ref, near.at[0, pl.ds(3, ROWS), pl.ds(EDGE, COLS)], load_sem.at[2]),
        pltpu.make_async_copy(vn_ref, near.at[1, pl.ds(3, ROWS), pl.ds(EDGE, COLS)], load_sem.at[3]),
        pltpu.make_async_copy(qf_ref, qf, load_sem.at[4]),
        pltpu.make_async_copy(qn_ref, qn, load_sem.at[5]),
    ]
    for load in loads:
        load.start()

    to_row = ((row + 8) % n_rows, (row + n_rows - 8) % n_rows, row + 4 - 8 * z)
    hop = 1 - 2 * z

    def arrivals(at, hop):
        first_ok = (at >= 2, at < 6, true)
        back = (-2, 2, hop)
        sent = [pick(SECOND[s], (at + back[s] + 8) % 8) for s in range(3)]
        second_ok = [sent[s] != NONE for s in range(3)]
        ring = (jnp.where(at < 2, 8, 0), jnp.where(at >= 6, -8, 0), 0)
        return (first_ok, second_ok), (back, [sent[s] + back[s] + ring[s] for s in range(3)])

    def slot_of(rel):
        return (rel + 10) % 7

    recv_ok, recv_rel = arrivals(place, hop)
    mate_ok, mate_rel = arrivals(place + hop, -hop)
    in_slot = [[slot_of(jnp.int32(rel)) for rel in rels] for rels in recv_rel]
    second_rel = [pick(SECOND[s], place) for s in range(3)]
    second_send = [second_rel[s] != NONE for s in range(3)]
    send_ok = ((x < 3, x > 0, true), second_send)
    shift = (-2, 2, -hop)
    ring = (jnp.where(place >= 6, 8, 0), jnp.where(place < 2, -8, 0), 0)
    src_slot = ([jnp.int32(OWN)] * 3, [slot_of(second_rel[s]) for s in range(3)])
    dst_slot = ([slot_of(jnp.int32(shift[s])) for s in range(3)], [slot_of(second_rel[s] + shift[s] + ring[s]) for s in range(3)])
    values_last = [one_of(place, VALUES_LAST[s]) for s in range(3)]
    late_in = [recv_ok[0][s] & one_of(place + (-2, 2, hop)[s], VALUES_LAST[s]) for s in range(3)]

    def piece(hf):
        offset = jnp.where(col < 2, (COLS, STRIP)[hf], (STRIP, 2 * STRIP)[hf])
        return pl.ds(0, ROWS), pl.ds(pl.multiple_of(offset, 16), (STRIP, COLS - STRIP)[hf])

    def far_copy(s, o, kv, hf):
        return pltpu.make_async_remote_copy(
            far.at[kv, src_slot[o][s], *piece(hf)],
            far.at[kv, dst_slot[o][s], *piece(hf)],
            far_send.at[s, o, kv, hf],
            far_recv.at[s, o, kv, hf],
            device_id=(to_row[s], col),
            device_id_type=MESH,
        )

    def send_far(s, o, kv, hf, ok=true):
        @pl.when(send_ok[o][s] & ok)
        def _():
            far_copy(s, o, kv, hf).start()

    def wait_far(s, o, kv, hf, ok=true):
        @pl.when(recv_ok[o][s] & ok)
        def _():
            block = far.at[kv, in_slot[o][s], *piece(hf)]
            pltpu.make_async_remote_copy(
                block, block, far_send.at[s, o, kv, hf], far_recv.at[s, o, kv, hf],
                device_id=(to_row[s], col), device_id_type=MESH,
            ).wait_recv()

    mate = col + 1 - 2 * core
    strip_src = pl.multiple_of(jnp.where(core == 0, COLS, STRIP), 16)
    strip_dst = pl.multiple_of(jnp.where(core == 0, 0, STRIP + COLS), 16)
    strip_in = pl.multiple_of(jnp.where(core == 0, STRIP + COLS, 0), 16)

    def strip_copy(e, kv, slot):
        return pltpu.make_async_remote_copy(
            far.at[kv, slot, :, pl.ds(strip_src, STRIP)],
            far.at[kv, slot, :, pl.ds(strip_dst, STRIP)],
            strip_send.at[e, kv],
            strip_recv.at[e, kv],
            device_id=(row, mate),
            device_id_type=MESH,
        )

    def wait_strip_at(e, kv, slot):
        block = far.at[kv, slot, :, pl.ds(strip_in, STRIP)]
        pltpu.make_async_remote_copy(
            block, block, strip_send.at[e, kv], strip_recv.at[e, kv],
            device_id=(row, mate), device_id_type=MESH,
        ).wait_recv()

    def event(s, o):
        return 1 + 3 * o + s

    side_src = pl.multiple_of(jnp.where(col == 1, COLS, STRIP), 16)
    side_dst = pl.multiple_of(jnp.where(col == 1, 0, STRIP + COLS), 16)
    side_in = pl.multiple_of(jnp.where(col == 1, STRIP + COLS, 0), 16)

    def side_ok(ok, rel):
        return inner & ok & (rel >= -3) & (rel <= 3)

    def side_copy(e, kv, rel):
        return pltpu.make_async_remote_copy(
            far.at[kv, slot_of(rel), :, pl.ds(side_src, STRIP)],
            far.at[kv, OWN + rel - hop, :, pl.ds(side_dst, STRIP)],
            side_send.at[e, kv],
            side_recv.at[e, kv],
            device_id=(to_row[2], 3 - col),
            device_id_type=MESH,
        )

    def wait_side(e, kv, ok, rel):
        @pl.when(side_ok(ok, rel + hop))
        def _():
            block = far.at[kv, OWN + rel + hop, :, pl.ds(side_in, STRIP)]
            pltpu.make_async_remote_copy(
                block, block, side_send.at[e, kv], side_recv.at[e, kv],
                device_id=(to_row[2], 3 - col), device_id_type=MESH,
            ).wait_recv()

    own_rel = jnp.int32(0)
    extra_ok = (inner & (place == 3), inner & (place == 4))
    extra_from = (1, 5)
    extra_to = (0, 6)
    extra_row = (row + 4, row - 4)

    def extra_copy(s, kv):
        return pltpu.make_async_remote_copy(
            far.at[kv, extra_from[s], :, pl.ds(side_src, STRIP)],
            far.at[kv, extra_to[s], :, pl.ds(side_dst, STRIP)],
            extra_send.at[kv],
            extra_recv.at[kv],
            device_id=(extra_row[s], 3 - col),
            device_id_type=MESH,
        )

    def wait_extra(kv):
        for s in range(2):
            @pl.when(extra_ok[s])
            def _():
                block = far.at[kv, extra_to[1 - s], :, pl.ds(side_in, STRIP)]
                pltpu.make_async_remote_copy(
                    block, block, extra_send.at[kv], extra_recv.at[kv],
                    device_id=(extra_row[s], 3 - col), device_id_type=MESH,
                ).wait_recv()

    def send_strips(s, o, kv, hf, ok=true):
        ok = recv_ok[o][s] & ok
        rel = recv_rel[o][s]
        e = event(s, o)

        @pl.when(ok & (inner if hf else ~inner))
        def _():
            strip_copy(e, kv, in_slot[o][s]).start()

        if hf == 0:
            @pl.when(side_ok(ok, rel - hop))
            def _():
                side_copy(e, kv, rel).start()

            if o == 0 and s < 2:
                @pl.when(extra_ok[s] & ok)
                def _():
                    extra_copy(s, kv).start()

    def wait_strip(s, o, kv):
        @pl.when(recv_ok[o][s])
        def _():
            wait_strip_at(event(s, o), kv, in_slot[o][s])

    sides = [(dr, dc) for dr in (-1, 0, 1) for dc in (-1, 0, 1) if (dr, dc) != (0, 0)]

    def there(dr, dc):
        good = true
        if dr:
            good = good & ((row + dr >= 0) & (row + dr < n_rows))
        if dc:
            good = good & ((col + dc >= 0) & (col + dc < n_cols))
        return good

    row_src = {1: (4, 3), -1: (3, 3)}
    row_dst = {1: (0, 3), -1: (7, 3)}
    row_from = {1: 1, 0: 0, -1: 0}
    row_to = {1: 0, 0: 3, -1: 7}
    main = pl.ds(EDGE, COLS)

    def crossing(dr):
        return {0: jnp.bool_(False), 1: y == 3, -1: y == 0}[dr]

    FIRST_LEG = (2, -1)
    LAST_LEG = (-1, 2)

    def sends_pass(dr):
        return crossing(dr) & there(dr, 0)

    def passes(kv, dr):
        at = {(0, 1): 1, (0, -1): 2, (1, 1): 2, (1, -1): 1}[kv, dr]
        back, on = row - FIRST_LEG[kv] * dr, row + LAST_LEG[kv] * dr
        return (y == at) & (back >= 0) & (back < n_rows) & (on >= 0) & (on < n_rows)

    def pass_in(kv, dr):
        return pltpu.make_async_remote_copy(
            near.at[kv, pl.ds(*row_src[dr]), main],
            passing.at[kv],
            pass_send.at[kv],
            pass_recv.at[kv],
            device_id=(row + FIRST_LEG[kv] * dr, col),
            device_id_type=MESH,
        )

    def pass_on(kv, dr):
        n = sides.index((dr, 0))
        return pltpu.make_async_remote_copy(
            passing.at[kv],
            near.at[kv, pl.ds(*row_dst[dr]), main],
            pass_send.at[kv],
            near_recv.at[n, kv],
            device_id=(row + LAST_LEG[kv] * dr, col),
            device_id_type=MESH,
        )

    def near_copy(n, kv):
        dr, dc = sides[n]
        if dc:
            src, dst = edge_out.at[(dc + 1) // 2], edge_in.at[n]
        else:
            src, dst = near.at[kv, pl.ds(*row_src[dr]), main], near.at[kv, pl.ds(*row_dst[dr]), main]
        return pltpu.make_async_remote_copy(
            src, dst, near_send.at[n, kv], near_recv.at[n, kv], device_id=(row + dr, col + dc), device_id_type=MESH
        )

    def near_arrival(n, kv):
        dr, dc = sides[n]
        block = edge_in.at[n] if dc else near.at[kv, pl.ds(*row_dst[dr]), main]
        return pltpu.make_async_remote_copy(
            block, block, near_send.at[n, kv], near_recv.at[n, kv],
            device_id=(row - dr, col - dc), device_id_type=MESH,
        )

    barrier = pltpu.get_barrier_semaphore()
    expected = jnp.int32(0)
    for s in range(3):
        @pl.when(send_ok[0][s])
        def _():
            pl.semaphore_signal(barrier, inc=1, device_id=(to_row[s], col), device_id_type=MESH)

        expected = expected + recv_ok[0][s].astype(jnp.int32)

    for s, places in ((0, (6, 7)), (1, (0, 1))):
        @pl.when(one_of(place, places))
        def _():
            pl.semaphore_signal(barrier, inc=1, device_id=(to_row[s], col), device_id_type=MESH)

        expected = expected + one_of(place, places).astype(jnp.int32)

    @pl.when(inner)
    def _():
        pl.semaphore_signal(barrier, inc=1, device_id=(to_row[2], 3 - col), device_id_type=MESH)

    expected = expected + inner.astype(jnp.int32)
    for s in range(2):
        @pl.when(extra_ok[s])
        def _():
            pl.semaphore_signal(barrier, inc=1, device_id=(extra_row[s], 3 - col), device_id_type=MESH)

        expected = expected + extra_ok[s].astype(jnp.int32)
    for dr, dc in sides:
        @pl.when(there(dr, dc))
        def _():
            pl.semaphore_signal(barrier, inc=1, device_id=(row + dr, col + dc), device_id_type=MESH)

        expected = expected + there(-dr, -dc).astype(jnp.int32)
    for dr in (-1, 1):
        @pl.when(sends_pass(dr))
        def _():
            pl.semaphore_signal(barrier, inc=1, device_id=(row + 2 * dr, col), device_id_type=MESH)

        @pl.when(passes(0, dr))
        def _():
            pl.semaphore_signal(barrier, inc=1, device_id=(row - 2 * dr, col), device_id_type=MESH)

        @pl.when(passes(1, dr))
        def _():
            pl.semaphore_signal(barrier, inc=1, device_id=(row + 2 * dr, col), device_id_type=MESH)

        @pl.when(sends_pass(-dr))
        def _():
            pl.semaphore_signal(barrier, inc=1, device_id=(row - 2 * dr, col), device_id_type=MESH)

        for good in (sends_pass(dr), passes(0, dr), passes(1, dr), sends_pass(-dr)):
            expected = expected + good.astype(jnp.int32)
    pl.semaphore_wait(barrier, expected)

    for hf in range(2):
        for kv in range(2):
            if hf == 0:
                loads[kv].wait()
            for s in range(3):
                send_far(s, 0, kv, hf, ok=~values_last[s] if (kv and hf) else true)
            if hf == 0:
                strip_copy(0, kv, OWN).start()

                @pl.when(inner)
                def _():
                    side_copy(0, kv, own_rel).start()

    loads[2].wait()
    loads[3].wait()
    for dc in (-1, 1):
        at = EDGE + (COLS - EDGE if dc == 1 else 0)
        inside = EDGE - 4 if dc == 1 else 0
        for kv in range(2):
            parts = [near[kv, 3 + r, at : at + EDGE, :].astype(jnp.float32)[inside : inside + 4] for r in range(ROWS)]
            edge_out[(dc + 1) // 2, kv] = jnp.concatenate(parts, axis=0).astype(jnp.bfloat16)

    def send_near():
        for n, (dr, dc) in enumerate(sides):
            for kv in range(1 if dc else 2):
                @pl.when(there(dr, dc) if dc else there(dr, dc) & ~crossing(dr))
                def _():
                    near_copy(n, kv).start()

        for dr in (-1, 1):
            @pl.when(sends_pass(dr))
            def _():
                pass_in(0, dr).start()
                pass_in(1, dr).start()

    def pass_near():
        for kv in range(2):
            for dr in (-1, 1):
                @pl.when(passes(kv, dr))
                def _():
                    pltpu.make_async_remote_copy(
                        passing.at[kv], passing.at[kv], pass_send.at[kv], pass_recv.at[kv],
                        device_id=(row - FIRST_LEG[kv] * dr, col), device_id_type=MESH,
                    ).wait_recv()
                    pass_on(kv, dr).start()

    def wait_near():
        for n, (dr, dc) in enumerate(sides):
            @pl.when(there(-dr, -dc))
            def _():
                near_arrival(n, 0).wait_recv()
                if dc == 0:
                    near_arrival(n, 1).wait_recv()
                else:
                    at = 0 if dc == 1 else EDGE + COLS
                    blank = jnp.zeros((EDGE - 4, CH), jnp.float32)
                    for kv in range(2):
                        packed = edge_in[n, kv].astype(jnp.float32)
                        for r in range(ROWS if dr == 0 else 3):
                            four = packed[4 * (row_from[dr] + r) : 4 * (row_from[dr] + r) + 4]
                            full = [blank, four] if dc == 1 else [four, blank]
                            near[kv, row_to[dr] + r, at : at + EDGE, :] = jnp.concatenate(full, axis=0).astype(
                                jnp.bfloat16
                            )

    send_near()

    c0 = col * COLS
    width = n_cols * COLS
    for t in range(TILES):
        q_at = lax.broadcasted_iota(jnp.int32, (TILE, KEYS), 0)
        k_at = lax.broadcasted_iota(jnp.int32, (TILE, KEYS), 1)
        apart = k_at - q_at
        k_col = c0 + TILE * t - STRIP + k_at
        good = ((apart & (STEP - 1)) == 0) & (apart >= 0) & (apart <= 2 * STRIP) & (k_col >= 0) & (k_col < width)
        bias_far[t] = jnp.where(good, 0.0, -jnp.inf)
    for rp in range(2):
        for t in range(TILES):
            shape = (2 * TILE, 8 * NEAR_KEYS)
            q_id = lax.broadcasted_iota(jnp.int32, shape, 0)
            k_id = lax.broadcasted_iota(jnp.int32, shape, 1)
            r_off = (k_id // NEAR_KEYS) - (q_id // TILE)
            c_off = (k_id % NEAR_KEYS) - (q_id % TILE) - EDGE
            k_row = row * ROWS + 2 * rp - 3 + (k_id // NEAR_KEYS)
            k_col = c0 + TILE * t - EDGE + (k_id % NEAR_KEYS)
            good = (r_off >= 0) & (r_off <= 6) & (c_off >= -3) & (c_off <= 3)
            good = good & (k_row >= 0) & (k_row < n_rows * ROWS) & (k_col >= 0) & (k_col < width)
            bias_near[rp * TILES + t] = jnp.where(good, 0.0, -jnp.inf)

    zero = lambda shape: jnp.zeros(shape, jnp.bfloat16)
    for a in range(SLOTS):
        relayed = (a == 0) & (place == 0) | (a == 6) & (place == 7)
        lost = ((place + a - OWN < 0) | (place + a - OWN > 7)) & ~relayed

        @pl.when(lost)
        def _():
            for kv in range(2):
                for r in range(ROWS):
                    far[kv, a, r] = zero((WIDE, CH))

        @pl.when(~lost & (col == 0))
        def _():
            for kv in range(2):
                for r in range(ROWS):
                    far[kv, a, r, 0:STRIP] = zero((STRIP, CH))

        @pl.when(~lost & (col == 3))
        def _():
            for kv in range(2):
                for r in range(ROWS):
                    far[kv, a, r, STRIP + COLS : WIDE] = zero((STRIP, CH))

        if a in (0, 6):
            @pl.when(relayed & inner)
            def _():
                for kv in range(2):
                    for r in range(ROWS):
                        far[kv, a, r, pl.ds(side_in, STRIP)] = zero((STRIP, CH))

    for kv in range(2):
        @pl.when(row == 0)
        def _():
            near[kv, 0:3] = zero((3, NEAR_WIDE, CH))

        @pl.when(row == n_rows - 1)
        def _():
            near[kv, 7:10] = zero((3, NEAR_WIDE, CH))

        @pl.when(col == 0)
        def _():
            near[kv, :, 0:EDGE] = zero((NEAR_ROWS, EDGE, CH))

        @pl.when(col == n_cols - 1)
        def _():
            near[kv, :, EDGE + COLS : NEAR_WIDE] = zero((NEAR_ROWS, EDGE, CH))

    lane_head = lax.broadcasted_iota(jnp.int32, (1, CH), 1) // HEAD
    head_mask = [(lane_head == h).astype(jnp.float32) for h in range(HEADS)]
    head_mask_narrow = [m.astype(jnp.bfloat16) for m in head_mask]
    dims_t = (((1,), (1,)), ((), ()))
    dims = (((1,), (0,)), ((), ()))

    loads[4].wait()
    loads[5].wait()

    def block_queries(q):
        return jnp.concatenate([q * head_mask_narrow[h] for h in range(HEADS)], axis=0)

    @pl.loop(0, ROWS, unroll=True)
    def _(r):
        for t in range(TILES):
            qb[r * TILES + t] = block_queries(qf[r, TILE * t : TILE * (t + 1), :])

    half_tiles = (jnp.where(col < 2, 0, 2), jnp.where(col < 2, 2, 0))

    def score_blocks(slots, part, first=False):
        row_bias = []
        for slot in slots:
            ok = (place + slot - OWN >= 0) & (place + slot - OWN <= 7)
            row_bias.append(jnp.where(ok, 0.0, -jnp.inf).astype(jnp.float32))

        @pl.loop(0, ROWS, unroll=True)
        def _(r):
            for tt in range(2):
                t = half_tiles[part] + tt
                idx = r * TILES + t
                where = pl.ds(pl.multiple_of(TILE * t, TILE), KEYS)
                top = None if first else peak[idx]
                for n in range(0, len(slots), 2):
                    pair = slots[n : n + 2]
                    k = jnp.concatenate([far[0, slot, r, where, :] for slot in pair], axis=0)
                    both = lax.dot_general(qb[idx], k, dims_t, preferred_element_type=jnp.float32) * SCALE
                    for m, slot in enumerate(pair):
                        b = bias_far[t] + row_bias[n + m]
                        s = both[:, m * KEYS : (m + 1) * KEYS].reshape(HEADS, TILE, KEYS) + b[None]
                        s = s.reshape(HEADS * TILE, KEYS)
                        scores[slot, idx] = s
                        top = s if top is None else jnp.maximum(top, s)
                peak[idx] = top

    def value_sum(idx, r, t, slots, o):
        where = pl.ds(pl.multiple_of(TILE * t, TILE), KEYS)
        for n in range(0, len(slots), 2):
            pair = slots[n : n + 2]
            p = jnp.concatenate([probs[slot, idx] for slot in pair], axis=1)
            v = jnp.concatenate([far[1, slot, r, where, :] for slot in pair], axis=0)
            d = lax.dot_general(p, v, dims, preferred_element_type=jnp.float32)
            o = d if o is None else o + d
        return o

    from_stream = [pick(FROM_STREAM[s], place) for s in range(3)]
    after_first = [pick(FROM_SECOND[s], place) == 0 for s in range(3)]
    needs_second = [jnp.bool_(False)] * 3
    for s in range(3):
        for d in range(3):
            needs_second[d] = needs_second[d] | (second_send[s] & ~after_first[s] & (from_stream[s] == d))

    first_slots = (jnp.int32(1), jnp.int32(5), OWN + hop)
    second_slots = (jnp.int32(0), jnp.int32(6), OWN - hop)
    own = jnp.int32(OWN)

    def later_sides(kv):
        for o in range(2):
            for s in range(3):
                if (s, o) != (2, 0):
                    wait_side(event(s, o), kv, mate_ok[o][s], mate_rel[o][s])
        wait_extra(kv)

    def first_arrivals(kv, hf):
        late = kv == 1 and hf == 1
        for s in range(3):
            wait_far(s, 0, kv, hf, ok=~late_in[s] if late else true)
        for s in range(3):
            send_far(s, 1, kv, hf, ok=after_first[s])
        if late:
            for s in range(3):
                send_far(s, 0, kv, hf, ok=values_last[s])
        for s in range(3):
            send_strips(s, 0, kv, hf, ok=~late_in[s] if late else true)

    def second_that_go_on(kv, hf):
        for s in range(3):
            wait_far(s, 1, kv, hf, ok=needs_second[s])
        for s in range(3):
            send_far(s, 1, kv, hf, ok=~after_first[s])

    def second_arrivals(kv, hf):
        for s in range(3):
            wait_far(s, 1, kv, hf, ok=~needs_second[s])
        for s in range(3):
            send_strips(s, 1, kv, hf)

    first_arrivals(0, 0)
    first_arrivals(1, 0)
    first_arrivals(0, 1)
    wait_strip_at(0, 0, OWN)
    for s in range(3):
        wait_strip(s, 0, 0)
    score_blocks((own,) + first_slots, 0, first=True)
    wait_side(0, 0, true, own_rel)
    wait_side(event(2, 0), 0, mate_ok[0][2], mate_rel[0][2])
    score_blocks((own, first_slots[2]), 1, first=True)
    second_that_go_on(0, 0)
    first_arrivals(1, 1)
    second_that_go_on(1, 0)
    second_arrivals(0, 0)
    pass_near()
    second_that_go_on(0, 1)
    second_arrivals(1, 0)

    def near_layer(rp):
        @pl.loop(0, TILES, unroll=True)
        def _(t):
            cols = pl.ds(pl.multiple_of(TILE * t, TILE), TILE)
            keys = pl.ds(pl.multiple_of(TILE * t, TILE), NEAR_KEYS)
            q = qn[pl.ds(2 * rp, 2), cols, :].reshape(2 * TILE, CH)
            k = near[0, pl.ds(2 * rp, 8), keys, :].reshape(8 * NEAR_KEYS, CH)
            v = near[1, pl.ds(2 * rp, 8), keys, :].reshape(8 * NEAR_KEYS, CH)
            s = lax.dot_general(block_queries(q), k, dims_t, preferred_element_type=jnp.float32) * SCALE
            s = s.reshape(HEADS, 2 * TILE, 8 * NEAR_KEYS) + bias_near[rp * TILES + t][None]
            s = s.reshape(HEADS * 2 * TILE, 8 * NEAR_KEYS)
            p = jnp.exp2(s - jnp.max(s, axis=1, keepdims=True))
            inverse = 1.0 / jnp.sum(p, axis=1, keepdims=True)
            o = lax.dot_general(p.astype(jnp.bfloat16), v, dims, preferred_element_type=jnp.float32) * inverse
            out = None
            for h in range(HEADS):
                part = o[h * 2 * TILE : (h + 1) * 2 * TILE] * head_mask[h]
                out = part if out is None else out + part
            out_near[pl.ds(2 * rp, 2), cols, :] = out.astype(jnp.bfloat16).reshape(2, TILE, CH)

    later_sides(0)
    score_blocks(first_slots[:2], 1)

    def spread(column):
        return jnp.broadcast_to(column, (HEADS * TILE, KEYS))

    @pl.loop(0, ROWS, unroll=True)
    def _(r):
        for t in range(TILES):
            idx = r * TILES + t
            m = jnp.max(peak[idx], axis=1, keepdims=True)
            summed = None
            for slot in (own,) + first_slots:
                p = jnp.exp2(scores[slot, idx] - m)
                probs[slot, idx] = p.astype(jnp.bfloat16)
                summed = p if summed is None else summed + p
            top[idx] = spread(m)
            total[idx] = spread(jnp.sum(summed, axis=1, keepdims=True))

    wait_strip_at(0, 1, OWN)
    wait_strip(2, 0, 1)
    wait_side(0, 1, true, own_rel)
    wait_side(event(2, 0), 1, mate_ok[0][2], mate_rel[0][2])

    @pl.loop(0, ROWS, unroll=True)
    def _(r):
        for t in range(TILES):
            idx = r * TILES + t
            acc[idx] = value_sum(idx, r, t, (own, first_slots[2]), None)

    second_arrivals(0, 1)
    second_that_go_on(1, 1)
    for s in range(3):
        wait_strip(s, 1, 0)
    score_blocks(second_slots, 0, first=True)
    score_blocks(second_slots, 1, first=True)

    @pl.loop(0, ROWS, unroll=True)
    def _(r):
        for t in range(TILES):
            idx = r * TILES + t
            m = jnp.maximum(top[idx], spread(jnp.max(peak[idx], axis=1, keepdims=True)))
            summed = None
            for slot in second_slots:
                p = jnp.exp2(scores[slot, idx] - m)
                probs[slot, idx] = p.astype(jnp.bfloat16)
                summed = p if summed is None else summed + p
            scale = jnp.exp2(top[idx] - m)
            top[idx] = scale
            total[idx] = 1.0 / (total[idx] * scale + spread(jnp.sum(summed, axis=1, keepdims=True)))

    for s in range(2):
        wait_far(s, 0, 1, 1, ok=late_in[s])
    for s in range(2):
        send_strips(s, 0, 1, 1, ok=late_in[s])
    second_arrivals(1, 1)
    wait_near()
    near_layer(0)
    near_layer(1)
    near_out = pltpu.make_async_copy(out_near, on_ref, out_sem.at[0])
    near_out.start()
    for s in range(2):
        wait_strip(s, 0, 1)
    for s in range(3):
        wait_strip(s, 1, 1)
    later_sides(1)

    @pl.loop(0, ROWS, unroll=True)
    def _(r):
        for t in range(TILES):
            idx = r * TILES + t
            scale = top[idx]
            o = value_sum(idx, r, t, first_slots[:2], acc[idx]) * jnp.concatenate([scale, scale], axis=1)
            o = value_sum(idx, r, t, second_slots, o)
            out = None
            for h in range(HEADS):
                part = slice(h * TILE, (h + 1) * TILE)
                inverse = total[idx, part, :]
                one = o[part, :] * jnp.concatenate([inverse, inverse], axis=1) * head_mask[h]
                out = one if out is None else out + one
            out_far[r, TILE * t : TILE * (t + 1), :] = out.astype(jnp.bfloat16)

    far_out = pltpu.make_async_copy(out_far, of_ref, out_sem.at[1])
    far_out.start()

    for kv in range(2):
        strip_copy(0, kv, OWN).wait_send()

        @pl.when(inner)
        def _():
            side_copy(0, kv, own_rel).wait_send()

        for s in range(2):
            @pl.when(extra_ok[s])
            def _():
                extra_copy(s, kv).wait_send()

        for o in range(2):
            for s in range(3):
                @pl.when(send_ok[o][s])
                def _():
                    far_copy(s, o, kv, 0).wait_send()
                    far_copy(s, o, kv, 1).wait_send()

                @pl.when(recv_ok[o][s])
                def _():
                    strip_copy(event(s, o), kv, in_slot[o][s]).wait_send()

                @pl.when(side_ok(recv_ok[o][s], recv_rel[o][s] - hop))
                def _():
                    side_copy(event(s, o), kv, recv_rel[o][s]).wait_send()

    for n, (dr, dc) in enumerate(sides):
        for kv in range(1 if dc else 2):
            @pl.when(there(dr, dc) if dc else there(dr, dc) & ~crossing(dr))
            def _():
                near_copy(n, kv).wait_send()

    for kv in range(2):
        for dr in (-1, 1):
            @pl.when(sends_pass(dr))
            def _():
                pass_in(kv, dr).wait_send()

            @pl.when(passes(kv, dr))
            def _():
                pass_on(kv, dr).wait_send()

    near_out.wait()
    far_out.wait()


def finish_kernel(near_ref, far_ref, near_out_ref, far_out_ref, near_held, far_held, sem):
    first = [
        pltpu.make_async_copy(near_ref, near_held, sem.at[0]),
        pltpu.make_async_copy(far_ref, far_held, sem.at[1]),
    ]
    second = [
        pltpu.make_async_copy(near_held, near_out_ref, sem.at[0]),
        pltpu.make_async_copy(far_held, far_out_ref, sem.at[1]),
    ]
    for copy in first:
        copy.start()
    for n in range(2):
        first[n].wait()
        second[n].start()
    for copy in second:
        copy.wait()


def per_device(query_near, key_near, value_near, dilated_queries, dilated_keys, dilated_values):
    block = jax.ShapeDtypeStruct((ROWS, COLS, CH), jnp.bfloat16)
    tiles = ROWS * TILES
    dma = pltpu.SemaphoreType.DMA
    anywhere = pl.BlockSpec(memory_space=pl.ANY)
    results = pl.pallas_call(
        kernel,
        out_shape=(block, block),
        in_specs=[pl.BlockSpec(memory_space=pltpu.HBM)] * 6,
        out_specs=(anywhere, anywhere),
        scratch_shapes=[
            pltpu.VMEM((2, SLOTS, ROWS, WIDE, CH), jnp.bfloat16),
            pltpu.VMEM((2, NEAR_ROWS, NEAR_WIDE, CH), jnp.bfloat16),
            pltpu.VMEM((ROWS, COLS, CH), jnp.bfloat16),
            pltpu.VMEM((ROWS, COLS, CH), jnp.bfloat16),
            pltpu.VMEM((tiles, HEADS * TILE, CH), jnp.bfloat16),
            pltpu.VMEM((SLOTS, tiles, HEADS * TILE, KEYS), jnp.float32),
            pltpu.VMEM((tiles, HEADS * TILE, KEYS), jnp.float32),
            pltpu.VMEM((tiles, HEADS * TILE, KEYS), jnp.float32),
            pltpu.VMEM((SLOTS, tiles, HEADS * TILE, KEYS), jnp.bfloat16),
            pltpu.VMEM((tiles, HEADS * TILE, 128), jnp.float32),
            pltpu.VMEM((tiles, HEADS * TILE, CH), jnp.float32),
            pltpu.VMEM((TILES, TILE, KEYS), jnp.float32),
            pltpu.VMEM((2 * TILES, 2 * TILE, 8 * NEAR_KEYS), jnp.float32),
            pltpu.VMEM((2, 2, 4 * ROWS, CH), jnp.bfloat16),
            pltpu.VMEM((9, 2, 4 * ROWS, CH), jnp.bfloat16),
            pltpu.VMEM((2, 3, COLS, CH), jnp.bfloat16),
            pltpu.VMEM((ROWS, COLS, CH), jnp.bfloat16),
            pltpu.VMEM((ROWS, COLS, CH), jnp.bfloat16),
            dma((6,)),
            dma((3, 2, 2, 2)),
            dma((3, 2, 2, 2)),
            dma((7, 2)),
            dma((7, 2)),
            dma((7, 2)),
            dma((7, 2)),
            dma((2,)),
            dma((2,)),
            dma((8, 2)),
            dma((8, 2)),
            dma((2,)),
            dma((2,)),
            dma((2,)),
        ],
        compiler_params=pltpu.CompilerParams(
            collective_id=0, has_side_effects=True, vmem_limit_bytes=56 << 20
        ),
        name="two_layers",
    )(query_near, key_near, value_near, dilated_queries, dilated_keys, dilated_values)
    return pl.pallas_call(
        finish_kernel,
        out_shape=(block, block),
        in_specs=[anywhere] * 2,
        out_specs=(anywhere, anywhere),
        scratch_shapes=[
            pltpu.VMEM((ROWS, COLS, CH), jnp.bfloat16),
            pltpu.VMEM((ROWS, COLS, CH), jnp.bfloat16),
            dma((2,)),
        ],
        compiler_params=pltpu.CompilerParams(vmem_limit_bytes=56 << 20),
        name="results_out",
    )(*results)


def solution(mesh):
    placed = (P("row", "col", None),) * 6
    return jax.shard_map(
        per_device,
        mesh=mesh,
        in_specs=placed,
        out_specs=(P("row", "col", None), P("row", "col", None)),
        check_vma=False,
    )
```
